128 devices in a mesh: xb: 16 (over x, y_hi, core), yb: 8 (over y_lo, z).
Axes of the slice: x: 4, y: 4 (y_hi: 2, y_lo: 2; y = y_hi * 2 + y_lo), z: 4, core: 2. Of those that a mesh axis runs over, the one named last changes fastest.
Arguments:
- rhs_coarse: float32 [512, 256, 128], P('xb', 'yb'), may hold values from -1.5 to 1.5
- beta_coarse: float32 [512, 256, 128], P('xb', 'yb'), may hold values from 0.25 to 4
- rhs_mid: float32 [16, 8, 32, 1024], P('xb', 'yb'), may hold values from -6 to 6
- beta_mid: float32 [16, 8, 32, 1024], P('xb', 'yb'), may hold values from 0.25 to 4
- rhs_fine: float32 [16, 8, 2, 32, 1024], P('xb', 'yb'), may hold values from -24 to 24
- beta_fine: float32 [16, 8, 2, 32, 1024], P('xb', 'yb'), may hold values from 0.25 to 4
- parent_mid: int32 [16, 8], replicated, may hold values from 0 to 15, as said below
- offset_mid: int32 [16, 8, 3], replicated, may hold values from 1 to 15
- parent_fine: int32 [16, 8, 2], replicated, may hold values from -1 to 15, as said below
- offset_fine: int32 [16, 8, 2, 3], replicated, may hold values from 1 to 15
Outputs:
- corr_coarse: float32 [512, 256, 128], P('xb', 'yb')
- corr_mid: float32 [16, 8, 32, 1024], P('xb', 'yb')
- corr_fine: float32 [16, 8, 2, 32, 1024], P('xb', 'yb')
The draws below stay inside these ranges and needn't reach their ends.
Inputs may be any that keep to these rules, and one draw needn't show every extreme that they name: For every j, parent_mid[:, j] is a permutation of 0 to 16 - 1. For every j, each of 0 to 16 - 1 stands in exactly one slot of parent_fine[:, j, :], the other slots are -1, and some device of each column has both slots live.
All inputs are finite; a program needn't handle non-finite values.
Results may differ from the reference program's by a relative error of at most 0.00002.
Values sent between devices are 32-bit elements; how exact they have to be, the bound alone decides.
A program may use at most 64 MiB of HBM per device.

```python
import math
import jax
import jax.numpy as jnp
from jax import lax

BOX = 32
FINE_SLOTS = 2
HALF = 16
LX = 512
LY = 256
LZ = 128
N_XB = 16
N_YB = 8


def draw_parent_mid(key, part):
    key = jax.random.fold_in(key, 11)
    keys = jax.random.split(key, N_YB)
    orders = jax.vmap(lambda one: jax.random.permutation(one, N_XB))(keys)
    return jnp.transpose(orders).astype(jnp.int32)


def column_slots(key):
    first, second, third = jax.random.split(key, 3)
    owners = jax.random.permutation(first, N_XB).astype(jnp.int32)
    crowded = jax.random.randint(second, (), 0, N_XB)
    others = jax.random.permutation(third, 2 * N_XB - 2).astype(jnp.int32)
    others = jnp.where(others >= 2 * crowded, others + 2, others)
    table = jnp.full((2 * N_XB,), -1, jnp.int32)
    table = table.at[2 * crowded].set(owners[0])
    table = table.at[2 * crowded + 1].set(owners[1])
    table = table.at[others[:N_XB - 2]].set(owners[2:])
    return table.reshape(N_XB, 2)


def draw_parent_fine(key, part):
    key = jax.random.fold_in(key, 23)
    keys = jax.random.split(key, N_YB)
    tables = jax.vmap(column_slots)(keys)
    return jnp.transpose(tables, (1, 0, 2)).astype(jnp.int32)


def set_ends(array, stream_key, low, high):
    extent = array.shape
    spot = [jax.random.randint(jax.random.fold_in(stream_key, axis), (), 0, extent[axis]) for axis in range(len(extent))]
    array = array.at[tuple(spot)].set(low)
    longest = extent.index(max(extent))
    spot[longest] = (spot[longest] + 1) % extent[longest]
    return array.at[tuple(spot)].set(high)


def levels(own_key, dims, pieces, least, high):
    level, own = 1.0, jax.random.fold_in(own_key, 6)
    for position, blocks in pieces:
        steps = jnp.exp(jax.random.uniform(jax.random.fold_in(own, position), (blocks,), jnp.float32, least / len(pieces), high / len(pieces)))
        level = level * jnp.repeat(steps, dims[position] // blocks).reshape([-1 if axis == position else 1 for axis in range(len(dims))])
    return level


def centred(stream_key, dims, scale, reach, cuts=(), kind=jnp.bfloat16):
    loudness = levels(stream_key, dims, cuts, -0.22, 0.18) if cuts else 1.0
    entries = jax.random.normal(stream_key, dims, jnp.float32) * scale * loudness
    return jnp.minimum(jnp.maximum(entries, -reach), reach).astype(kind)


def setup_inputs(seed: int = 0) -> dict:
    streams_of = jax.random.split(jax.random.key(seed), 11)
    rhs_coarse = centred(streams_of[0], (LX, LY, LZ), 0.25, 1.5, ((0, 16), (1, 8)), jnp.float32)
    beta_coarse = jnp.clip(jnp.exp(math.log(4.0) - 2.7725887 * jax.random.uniform(streams_of[1], (LX, LY, LZ), jnp.float32) ** levels(streams_of[1], (LX, LY, LZ), ((0, 16), (1, 8)), -0.2, 0.2)), 0.25, 4.0)
    rhs_mid = centred(streams_of[2], (N_XB, N_YB, BOX, BOX * BOX), 1.0, 6.0, ((0, 16), (1, 8)), jnp.float32)
    beta_mid = jnp.clip(jnp.exp(math.log(4.0) - 2.7725887 * jax.random.uniform(streams_of[3], (N_XB, N_YB, BOX, BOX * BOX), jnp.float32) ** levels(streams_of[3], (N_XB, N_YB, BOX, BOX * BOX), ((0, 16), (1, 8)), -0.2, 0.2)), 0.25, 4.0)
    rhs_fine = centred(streams_of[4], (N_XB, N_YB, FINE_SLOTS, BOX, BOX * BOX), 4.0, 24.0, ((0, 16), (1, 8)), jnp.float32)
    beta_fine = jnp.clip(jnp.exp(math.log(4.0) - 2.7725887 * jax.random.uniform(streams_of[5], (N_XB, N_YB, FINE_SLOTS, BOX, BOX * BOX), jnp.float32) ** levels(streams_of[5], (N_XB, N_YB, FINE_SLOTS, BOX, BOX * BOX), ((0, 16), (1, 8)), -0.2, 0.2)), 0.25, 4.0)
    parent_mid = draw_parent_mid(jax.random.fold_in(streams_of[10], 71), 0)
    offset_mid = set_ends(jax.random.randint(streams_of[7], (N_XB, N_YB, 3), 1, HALF), jax.random.fold_in(streams_of[7], 1), 1, HALF - 1).astype(jnp.int32)
    parent_fine = draw_parent_fine(jax.random.fold_in(streams_of[10], 71), 0)
    offset_fine = set_ends(jax.random.randint(streams_of[9], (N_XB, N_YB, FINE_SLOTS, 3), 1, HALF), jax.random.fold_in(streams_of[9], 1), 1, HALF - 1).astype(jnp.int32)
    return dict(rhs_coarse=rhs_coarse, beta_coarse=beta_coarse, rhs_mid=rhs_mid, beta_mid=beta_mid, rhs_fine=rhs_fine, beta_fine=beta_fine, parent_mid=parent_mid, offset_mid=offset_mid, parent_fine=parent_fine, offset_fine=offset_fine)


def faces_from(padded):
    centre = padded[1:-1, 1:-1, 1:-1]
    weights = (
        0.5 * (centre + padded[2:, 1:-1, 1:-1]),
        0.5 * (centre + padded[:-2, 1:-1, 1:-1]),
        0.5 * (centre + padded[1:-1, 2:, 1:-1]),
        0.5 * (centre + padded[1:-1, :-2, 1:-1]),
        0.5 * (centre + padded[1:-1, 1:-1, 2:]),
        0.5 * (centre + padded[1:-1, 1:-1, :-2]),
    )
    total = weights[0] + weights[1] + weights[2] + weights[3] + weights[4] + weights[5]
    return weights, total


def beside_all(padded, weights):
    return (weights[0] * padded[2:, 1:-1, 1:-1] + weights[1] * padded[:-2, 1:-1, 1:-1]
            + weights[2] * padded[1:-1, 2:, 1:-1] + weights[3] * padded[1:-1, :-2, 1:-1]
            + weights[4] * padded[1:-1, 1:-1, 2:] + weights[5] * padded[1:-1, 1:-1, :-2])


def colours(shape):
    summed = (lax.broadcasted_iota(jnp.int32, shape, 0) + lax.broadcasted_iota(jnp.int32, shape, 1)
              + lax.broadcasted_iota(jnp.int32, shape, 2))
    return summed % 2


def relaxed(field, target, weights, total, scale, shell, colour_map):
    for sweep in range(2):
        for colour in (0, 1):
            padded = shell.at[1:-1, 1:-1, 1:-1].set(field)
            fresh = (target / scale + beside_all(padded, weights)) / total
            field = jnp.where(colour_map == colour, fresh, field)
    return field


def residual(field, target, weights, total, scale, shell):
    padded = shell.at[1:-1, 1:-1, 1:-1].set(field)
    return target - scale * (total * field - beside_all(padded, weights))


def shrink(field):
    half = field.shape[0] // 2
    return field.reshape(half, 2, half, 2, half, 2).mean(axis=(1, 3, 5))


def spread(window):
    grown = jnp.repeat(jnp.repeat(jnp.repeat(window, 2, axis=0), 2, axis=1), 2, axis=2)
    return grown[1:-1, 1:-1, 1:-1]


def reference(rhs_coarse, beta_coarse, rhs_mid, beta_mid, rhs_fine, beta_fine, parent_mid, offset_mid, parent_fine, offset_fine):
    nx = parent_mid.shape[0]
    ny = parent_mid.shape[1]
    slots = parent_fine.shape[2]
    span = BOX // 2 + 2
    cube_shape = (BOX, BOX, BOX)
    colour_box = colours(cube_shape)
    empty_shell = jnp.zeros((BOX + 2, BOX + 2, BOX + 2), jnp.float32)
    fine_rhs = rhs_fine.reshape((nx * ny * slots,) + cube_shape)
    fine_beta = beta_fine.reshape((nx * ny * slots,) + cube_shape)
    mid_rhs = rhs_mid.reshape((nx * ny,) + cube_shape)
    mid_beta = beta_mid.reshape((nx * ny,) + cube_shape)

    def fine_down(pair):
        target, beta = pair
        weights, total = faces_from(jnp.pad(beta, 1))
        field = relaxed(jnp.zeros(cube_shape, jnp.float32), target, weights, total, 1.0, empty_shell, colour_box)
        return field, shrink(residual(field, target, weights, total, 1.0, empty_shell))

    fine_start, fine_rests = lax.map(fine_down, (fine_rhs, fine_beta))

    xb_ids = jnp.arange(nx, dtype=jnp.int32)
    col_ids = jnp.arange(ny, dtype=jnp.int32)
    slot_range = jnp.arange(slots, dtype=jnp.int32)
    match = parent_fine[None] == xb_ids[:, None, None, None]
    slot_ids = (xb_ids[:, None, None] * ny + col_ids[None, :, None]) * slots + slot_range[None, None, :]
    child = jnp.sum(jnp.where(match, slot_ids[None], 0), axis=(1, 3)).astype(jnp.int32).reshape(-1)
    child_corner = jnp.sum(jnp.where(match[..., None], offset_fine[None], 0), axis=(1, 3)).astype(jnp.int32).reshape(-1, 3)

    def mid_down(args):
        target, beta, slot, corner = args
        target = lax.dynamic_update_slice(target, fine_rests[slot], (corner[0], corner[1], corner[2]))
        weights, total = faces_from(jnp.pad(beta, 1))
        field = relaxed(jnp.zeros(cube_shape, jnp.float32), target, weights, total, 0.25, empty_shell, colour_box)
        return field, target, shrink(residual(field, target, weights, total, 0.25, empty_shell))

    mid_start, mid_target, mid_rests = lax.map(mid_down, (mid_rhs, mid_beta, child, child_corner))

    coarse_start = jnp.stack([
        parent_mid * BOX + offset_mid[..., 0],
        jnp.broadcast_to(col_ids[None, :] * BOX, (nx, ny)) + offset_mid[..., 1],
        offset_mid[..., 2]], axis=-1).astype(jnp.int32).reshape(-1, 3)

    def place(index, field):
        start = coarse_start[index]
        return lax.dynamic_update_slice(field, mid_rests[index], (start[0], start[1], start[2]))

    coarse_target = lax.fori_loop(0, nx * ny, place, rhs_coarse)
    coarse_weights, coarse_total = faces_from(jnp.pad(beta_coarse, 1))
    coarse_shell = jnp.zeros(tuple(d + 2 for d in rhs_coarse.shape), jnp.float32)
    corr_coarse = relaxed(jnp.zeros_like(rhs_coarse), coarse_target, coarse_weights, coarse_total, 0.0625,
                          coarse_shell, colours(rhs_coarse.shape))

    def mid_up(args):
        start_field, target, beta, start = args
        window = lax.dynamic_slice(corr_coarse, (start[0] - 1, start[1] - 1, start[2] - 1), (span, span, span))
        shell = spread(window)
        weights, total = faces_from(jnp.pad(beta, 1))
        return relaxed(start_field + shell[1:-1, 1:-1, 1:-1], target, weights, total, 0.25, shell, colour_box)

    mid_field = lax.map(mid_up, (mid_start, mid_target, mid_beta, coarse_start))

    fine_parent = (jnp.maximum(parent_fine, 0) * ny + col_ids[None, :, None]).astype(jnp.int32).reshape(-1)
    alive = (parent_fine >= 0).reshape(-1)

    def fine_up(args):
        start_field, target, beta, parent, corner, live = args
        window = lax.dynamic_slice(mid_field[parent], (corner[0] - 1, corner[1] - 1, corner[2] - 1), (span, span, span))
        shell = spread(window)
        weights, total = faces_from(jnp.pad(beta, 1))
        field = relaxed(start_field + shell[1:-1, 1:-1, 1:-1], target, weights, total, 1.0, shell, colour_box)
        return jnp.where(live, field, 0.0)

    fine_field = lax.map(fine_up, (fine_start, fine_rhs, fine_beta, fine_parent,
                                   offset_fine.reshape(-1, 3).astype(jnp.int32), alive))
    corr_mid = mid_field.reshape(nx, ny, BOX, BOX * BOX)
    corr_fine = fine_field.reshape(nx, ny, slots, BOX, BOX * BOX)
    return corr_coarse, corr_mid, corr_fine
```

```python
import functools

import jax
import jax.numpy as jnp
from jax import lax
from jax.experimental import pallas as pl
from jax.experimental.pallas import tpu as pltpu
from jax.sharding import PartitionSpec as P

MESH = pl.DeviceIdType.MESH
F32 = jnp.float32
BF16 = jnp.bfloat16
CH = 64
PAIRS = 20
ROWS = 48
EDGE = 56
WIDE = 2 * EDGE + PAIRS * ROWS
PEERS = [
    (dx, dh, dc)
    for dx, dh in ((2, 1), (1, 1), (3, 1), (2, 0), (0, 1), (1, 0), (3, 0))
    for dc in (0, 1)
] + [(0, 0, 1)]


def iota(shape, dim):
    return lax.broadcasted_iota(jnp.int32, shape, dim)


def each(count, body, unroll=True):
    def step(i, carry):
        body(i)
        return carry

    lax.fori_loop(0, count, step, 0, unroll=unroll)


def chosen_dot(values, choice):
    rows = values.shape[0]
    high = values.astype(BF16).astype(F32)
    rest = values - high
    middle = rest.astype(BF16).astype(F32)
    terms = jnp.concatenate([high, middle, rest - middle], axis=0).astype(BF16)
    out = lax.dot_general(terms, choice, (((1,), (0,)), ((), ())), preferred_element_type=F32)
    return out[:rows] + out[rows : 2 * rows] + out[2 * rows :]


def onehot(mask, value=1.0):
    return jnp.where(mask, value, 0.0).astype(BF16)


class Level:
    def __init__(self, count, scale, refs):
        self.count, self.scale, self.rows = count, scale, count * 128
        (self.full, self.red, self.black, self.coef, self.g, self.inv, self.hb, self.tot, self.rest) = refs

    def field(self, colour):
        return self.black if colour else self.red

    def near(self, colour, at):
        ref = self.field(1 - colour)
        lane = iota((CH, 128), 1)
        odd = (lane // 32 + lane) % 2 == 1
        own = ref[pl.ds(8 + at, CH)]
        above, below = ref[pl.ds(16 + at, CH)], ref[pl.ds(at, CH)]
        after, before = ref[pl.ds(9 + at, CH)], ref[pl.ds(7 + at, CH)]
        other = jnp.where(odd, below, above) if colour else jnp.where(odd, above, below)
        return (
            own,
            other,
            pltpu.roll(jnp.where(lane >= 32, own, after), 96, 1),
            pltpu.roll(jnp.where(lane < 96, own, before), 32, 1),
            pltpu.roll(own, 127, 1),
            pltpu.roll(own, 1, 1),
        )

    def clear_ends(self):
        for ref in (self.red, self.black):
            ref[pl.ds(0, 8)] = jnp.zeros((8, 128), F32)
            ref[pl.ds(8 + self.rows, 8)] = jnp.zeros((8, 128), F32)

    def unfold(self, load):
        for box in range(self.count):
            for s in range(8):
                self.full[pl.ds(box * 256 + s, 32, stride=8)] = load(box, s)

    def packed(self, full, at):
        lane = iota((CH, 128), 1)
        odd = (lane // 32 + lane) % 2 == 1
        planes = full.reshape(CH // 8, 2, 8, 128)
        low, high = planes[:, 0].reshape(CH, 128), planes[:, 1].reshape(CH, 128)
        return jnp.where(odd, high, low), jnp.where(odd, low, high)

    def set_fields(self):
        def body(i):
            at = i * CH
            red, black = self.packed(self.full[pl.ds(2 * at, 2 * CH)], at)
            self.red[pl.ds(8 + at, CH)] = red
            self.black[pl.ds(8 + at, CH)] = black

        each(self.rows // CH, body)

    def set_weights(self):
        def body(i):
            at = i * CH
            lane, row = iota((CH, 128), 1), iota((CH, 128), 0)
            odd = (lane // 32 + lane) % 2 == 1
            s = row % 8
            pair = ((at + row) // 8) % 16
            z = lane % 32
            inside_y = (jnp.logical_not((s == 7) & (lane >= 96)), jnp.logical_not((s == 0) & (lane < 32)))
            inside_z = (z < 31, z > 0)
            for colour in (0, 1):
                first, last = (odd, jnp.logical_not(odd)) if colour else (jnp.logical_not(odd), odd)
                edge = (first & (pair == 0)) | (last & (pair == 15))
                masks = (None, jnp.logical_not(edge)) + inside_y + inside_z
                own = self.field(colour)[pl.ds(8 + at, CH)]
                near = self.near(colour, at)
                faces = [
                    0.5 * (own + (other if mask is None else jnp.where(mask, other, 0.0)))
                    for other, mask in zip(near, masks)
                ]
                total = faces[0] + faces[1] + faces[2] + faces[3] + faces[4] + faces[5]
                inv = 1.0 / total
                for n in range(6):
                    part = faces[n] * inv
                    self.coef[colour, n, pl.ds(at, CH)] = (
                        part if masks[n] is None else jnp.where(masks[n], part, 0.0)
                    )
                self.inv[colour, pl.ds(at, CH)] = inv * (1.0 / self.scale)
                self.hb[colour, pl.ds(at, CH)] = 0.5 * own * inv
                if colour == 0:
                    self.tot[pl.ds(at, CH)] = self.scale * total

        each(self.rows // CH, body)

    def set_target(self, at, red, black):
        for colour, value in ((0, red), (1, black)):
            self.g[colour, pl.ds(at, CH)] = value * self.inv[colour, pl.ds(at, CH)]

    def fresh(self, colour, at):
        near = self.near(colour, at)
        out = self.g[colour, pl.ds(at, CH)]
        for n in range(6):
            out = out + self.coef[colour, n, pl.ds(at, CH)] * near[n]
        return out

    def half_sweep(self, colour):
        def body(i):
            at = i * CH
            self.field(colour)[pl.ds(8 + at, CH)] = self.fresh(colour, at)

        each(self.rows // CH, body)

    def down(self):
        def first(i):
            at = i * CH
            self.red[pl.ds(8 + at, CH)] = self.g[0, pl.ds(at, CH)]

        each(self.rows // CH, first)
        self.half_sweep(1)
        self.half_sweep(0)
        self.half_sweep(1)

        def left(i):
            at = i * CH
            self.rest[pl.ds(at, CH)] = self.tot[pl.ds(at, CH)] * (
                self.fresh(0, at) - self.red[pl.ds(8 + at, CH)]
            )

        each(self.rows // CH, left)

    def restricted(self, mean):
        parts = []
        for box in range(self.count):
            for h in range(2):
                parts.append(
                    jnp.concatenate(
                        [self.rest[pl.ds(box * 128 + 4 * h + j, 16, stride=8)] for j in range(4)], axis=1
                    )
                )
        return chosen_dot(jnp.concatenate(parts, axis=0), mean)

    def start_up(self, pieces, spread):
        sub, lane = iota((8, 128), 0), iota((8, 128), 1)
        odd = (lane // 32 + lane) % 2 == 1
        even = jnp.logical_not(odd)
        rows_of = lane // 32 == sub % 4
        rows_of_face = (
            ((lane < 16) & (sub == 0))
            | ((lane >= 16) & (lane < 32) & (sub == 7))
            | ((lane >= 32) & (lane < 64) & ((lane % 16) // 2 == sub))
        )

        def tiles(rows):
            return jnp.broadcast_to(rows[:, None, :], (rows.shape[0], 8, 128))

        def halves(first, second):
            return jnp.where((sub < 4)[None], tiles(first), tiles(second))

        for box, piece in enumerate(pieces):
            core = jnp.concatenate(
                [
                    halves(piece[0:16], piece[16:32]),
                    halves(piece[48:49], piece[49:50]),
                    halves(piece[50:51], piece[51:52]),
                ],
                axis=0,
            )
            core = jnp.where(rows_of[None], core, 0.0).reshape(144, 128)
            face = jnp.where(rows_of_face[None], tiles(piece[32:48]), 0.0).reshape(128, 128)
            face = jnp.concatenate([face, jnp.zeros((16, 128), F32)], axis=0)
            grown = chosen_dot(jnp.concatenate([core, face], axis=1), spread)
            inner, border = grown[:128, :128], grown[:128, 128:].reshape(16, 8, 128)
            low, high = grown[128:136, :128], grown[136:144, :128]
            at = box * 128
            self.black[pl.ds(8 + at, 128)] = self.black[pl.ds(8 + at, 128)] + inner
            for colour in (0, 1):
                first, last = (odd, even) if colour else (even, odd)
                ghost = jnp.concatenate(
                    [
                        border[:1] + jnp.where(first, low, 0.0)[None],
                        border[1:15],
                        border[15:] + jnp.where(last, high, 0.0)[None],
                    ],
                    axis=0,
                ).reshape(128, 128)
                self.g[colour, pl.ds(at, 128)] = (
                    self.g[colour, pl.ds(at, 128)] + self.hb[colour, pl.ds(at, 128)] * ghost
                )

    def up(self):
        for colour in (0, 1, 0, 1):
            self.half_sweep(colour)

    def finished(self, at):
        lane = iota((CH, 128), 1)
        odd = (lane // 32 + lane) % 2 == 1
        red, black = self.red[pl.ds(8 + at, CH)], self.black[pl.ds(8 + at, CH)]
        low = jnp.where(odd, black, red).reshape(CH // 8, 1, 8, 128)
        high = jnp.where(odd, red, black).reshape(CH // 8, 1, 8, 128)
        return jnp.concatenate([low, high], axis=1).reshape(2 * CH, 128)


def spread_choice():
    l, n = iota((256, 256), 0), iota((256, 256), 1)
    z, q = n % 32, (n % 128) // 32
    inner = (l < 128) & (n < 128) & ((l // 16) % 2 == q // 2) & (l % 16 == z // 2)
    f = l - 128
    along_y = (f >= 0) & (f < 32) & (q == jnp.where(f < 16, 0, 3)) & (z // 2 == f % 16)
    along_z = (f >= 32) & (f < 64) & (q // 2 == f % 2) & (z == jnp.where(f < 48, 0, 31))
    return onehot(inner | ((n >= 128) & (along_y | along_z)))


def mean_choice():
    k, n = iota((512, 128), 0), iota((512, 128), 1)
    lane = k % 128
    return onehot(n == 32 * (k // 128) + 16 * (lane // 64) + (lane % 32) // 2, 0.125)


def place_choice(corner):
    k, n = iota((256, 1024), 0), iota((256, 1024), 1)
    return onehot(n == (k // 16) * 32 + k % 16 + corner[1] * 32 + corner[2])


def window_choice(corner):
    n = iota((1, 384), 1)
    i = n % 16
    source = jnp.where(n < 256, (n // 16) * 32 + i, -4096)
    source = jnp.where((n >= 256) & (n < 272), i - 32, source)
    source = jnp.where((n >= 272) & (n < 288), i + 512, source)
    source = jnp.where((n >= 288) & (n < 304), i * 32 - 1, source)
    source = jnp.where((n >= 304) & (n < 320), i * 32 + 16, source)
    return onehot(iota((1024, 384), 0) == source + corner[1] * 32 + corner[2])


def placed_lhs(piece):
    return jnp.concatenate([piece[0:16], piece[16:32]], axis=1)


def kernel(
    rhs_c, beta_c, rhs_m, beta_m, rhs_f, beta_f, parent_m, offset_m, parent_f, offset_f,
    out_c, out_m, out_f,
    gather1, gather2, gather3, gather4, rim_out, rim_in,
    mean_ref, spread_ref, place_m, place_c, window_m, window_c,
    put_m, put_c, pad_m, pad_c, wide_m, wide_c, cut_m, cut_c,
    beta_e, g_e, field_e, coef_e, inv_e,
    *rest,
):
    fine_refs, mid_refs = rest[:9], rest[9:18]
    send_sems, recv_sems, rim_send, rim_recv = rest[18:]
    fine = Level(2, 1.0, fine_refs)
    mid = Level(1, 0.25, mid_refs)
    n_x, n_y = lax.axis_size("xb"), lax.axis_size("yb")
    row, col = lax.axis_index("xb"), lax.axis_index("yb")

    def beside(dx, dy):
        return (lax.rem(row + dx + n_x, n_x), lax.rem(col + dy + n_y, n_y))

    def peer(dx, dh, dc):
        x, h, c = row // 4, (row // 2) % 2, row % 2
        return (((x + dx) % 4) * 4 + ((h + dh) % 2) * 2 + (c + dc) % 2, col)

    barrier = pltpu.get_barrier_semaphore()
    greeted = [peer(*hop) for hop in PEERS] + [beside(dx, dy) for dx in (-1, 0, 1) for dy in (-1, 1)]
    for device in greeted:
        pl.semaphore_signal(barrier, inc=1, device_id=device, device_id_type=MESH)

    def send_all(buffer, stage):
        for hop in PEERS:
            pltpu.make_async_remote_copy(
                src_ref=buffer.at[row],
                dst_ref=buffer.at[row],
                send_sem=send_sems.at[stage],
                recv_sem=recv_sems.at[stage],
                device_id=peer(*hop),
                device_id_type=MESH,
            ).start()

    def wait_all(buffer, sem):
        whole = buffer.at[pl.ds(0, len(PEERS))]
        pltpu.make_async_copy(whole, whole, sem).wait()

    def send_rim(turn):
        def copy(source, size, target, device):
            pltpu.make_async_remote_copy(
                src_ref=rim_out.at[turn, pl.ds(source, size)],
                dst_ref=rim_in.at[turn, pl.ds(target, size)],
                send_sem=rim_send.at[turn],
                recv_sem=rim_recv.at[turn],
                device_id=device,
                device_id_type=MESH,
            ).start()

        for side_x in (0, 1):
            for side_y in (0, 1):
                copy(
                    256 + 128 * side_y + 112 * side_x, 16,
                    512 + 16 * (2 * (1 - side_x) + 1 - side_y),
                    beside(2 * side_x - 1, 2 * side_y - 1),
                )
        for side in (0, 1):
            copy(256 + 128 * side, 128, 256 + 128 * (1 - side), beside(0, 2 * side - 1))
        for side in (0, 1):
            copy(128 * side, 128, 128 * (1 - side), beside(2 * side - 1, 0))

    def wait_rim(turn, sem):
        whole = rim_in.at[turn]
        pltpu.make_async_copy(whole, whole, sem.at[turn]).wait()

    def fill_rim(turn, ref):
        tile_row = iota((8, 128), 0)
        for side in (0, 1):
            for colour in (0, 1):
                for d in (0, 1):
                    at = EDGE + ((2, 16)[side] + d) * ROWS + 8
                    rim_out[turn, pl.ds(128 * side + (2 * colour + d) * 32, 32)] = ref[colour, pl.ds(at, 32)]

        def body(k):
            at = EDGE + (k + 2) * ROWS
            red, black = ref[0, pl.ds(at + 8, 8)], ref[1, pl.ds(at + 8, 8)]
            rim_out[turn, pl.ds(256 + k * 8, 8)] = jnp.where(tile_row < 4, red, pltpu.roll(black, 4, 0))
            red, black = ref[0, pl.ds(at + 32, 8)], ref[1, pl.ds(at + 32, 8)]
            rim_out[turn, pl.ds(384 + k * 8, 8)] = jnp.where(tile_row < 4, pltpu.roll(black, 4, 0), red)

        each(16, body)

    def take_rim(turn, ref, inside_x, inside_y):
        def keep(value, *sides):
            for side in sides:
                if side is not None:
                    value = jnp.where(side, value, 0.0)
            return value

        for side in (0, 1):
            for colour in (0, 1):
                for d in (0, 1):
                    at = EDGE + ((0, 18)[side] + d) * ROWS + 8
                    part = rim_in[turn, pl.ds(128 * side + (2 * colour + d) * 32, 32)]
                    ref[colour, pl.ds(at, 32)] = keep(part, inside_x[side])

            def body(k, side=side):
                at = EDGE + (k + 2) * ROWS + 40 * side
                part = keep(rim_in[turn, pl.ds(256 + 128 * side + 8 * k, 8)], inside_y[side])
                ref[0, pl.ds(at, 8)] = part
                ref[1, pl.ds(at, 8)] = pltpu.roll(part, 4, 0)

            each(16, body)
            for other in (0, 1):
                for d in (0, 1):
                    at = EDGE + (18 * side + d) * ROWS + 40 * other
                    part = rim_in[turn, pl.ds(512 + 16 * (2 * side + other) + 8 * d, 8)]
                    part = keep(part, inside_x[side], inside_y[other])
                    ref[0, pl.ds(at, 8)] = part
                    ref[1, pl.ds(at, 8)] = pltpu.roll(part, 4, 0)

    mean_ref[...] = mean_choice()
    fine.clear_ends()
    fine.unfold(lambda box, s: beta_f[0, 0, box, :, 128 * s : 128 * s + 128])
    fine.set_fields()
    fine.set_weights()
    fine.unfold(lambda box, s: rhs_f[0, 0, box, :, 128 * s : 128 * s + 128])

    def fine_target(i):
        at = i * CH
        fine.set_target(at, *fine.packed(fine.full[pl.ds(2 * at, 2 * CH)], at))

    each(fine.rows // CH, fine_target)
    fine.down()
    gather1[row] = fine.restricted(mean_ref[...]).reshape(2, 32, 128)
    pl.semaphore_wait(barrier, len(greeted))
    send_all(gather1, 0)

    def own_beta(k):
        lane, line = iota((32, 128), 1), iota((32, 128), 0)
        odd = (line + lane) % 2 == 1
        low, high = beta_c[2 * k], beta_c[2 * k + 1]
        at = EDGE + (k + 2) * ROWS + 8
        beta_e[0, pl.ds(at, 32)] = jnp.where(odd, high, low)
        beta_e[1, pl.ds(at, 32)] = jnp.where(odd, low, high)

    for colour in (0, 1):
        beta_e[colour, pl.ds(0, EDGE)] = jnp.zeros((EDGE, 128), F32)
        beta_e[colour, pl.ds(WIDE - EDGE, EDGE)] = jnp.zeros((EDGE, 128), F32)
    each(16, own_beta, 4)
    fill_rim(0, beta_e)
    send_rim(0)

    mid.clear_ends()
    mid.unfold(lambda box, s: beta_m[0, 0, :, 128 * s : 128 * s + 128])
    mid.set_fields()
    mid.set_weights()
    mid.unfold(lambda box, s: rhs_m[0, 0, :, 128 * s : 128 * s + 128])

    def find_fine(i, carry):
        index, place, x, y, z = carry
        for slot in range(2):
            hit = parent_f[i, col, slot] == row
            index = jnp.where(hit, i, index)
            place = jnp.where(hit, slot, place)
            x = jnp.where(hit, offset_f[i, col, slot, 0], x)
            y = jnp.where(hit, offset_f[i, col, slot, 1], y)
            z = jnp.where(hit, offset_f[i, col, slot, 2], z)
        return index, place, x, y, z

    def find_mid(i, carry):
        index, x, y, z = carry
        hit = parent_m[i, col] == row
        return (
            jnp.where(hit, i, index),
            jnp.where(hit, offset_m[i, col, 0], x),
            jnp.where(hit, offset_m[i, col, 1], y),
            jnp.where(hit, offset_m[i, col, 2], z),
        )

    zero, one = jnp.int32(0), jnp.int32(1)
    child, child_slot, *corner_m = lax.fori_loop(0, 16, find_fine, (zero, zero, one, one, one))
    guest, *corner_c = lax.fori_loop(0, 16, find_mid, (zero, one, one, one))
    place_m[...] = place_choice(corner_m)
    pad_m[0:16] = jnp.zeros((16, 8, 128), F32)
    pad_m[32:48] = jnp.zeros((16, 8, 128), F32)

    wait_all(gather1, recv_sems.at[0])

    put = chosen_dot(placed_lhs(gather1[child, child_slot]), place_m[...])
    for s in range(8):
        put_m[pl.ds(s, 16, stride=8)] = put[:, 128 * s : 128 * s + 128]
    pad_m[16:32] = put_m[...].reshape(16, 8, 128)

    def shift_m(x):
        cut_m[pl.ds(8 * x, 8)] = pad_m[16 - corner_m[0] + x]

    each(32, shift_m)

    def mid_target(i):
        lane, line = iota((2 * CH, 128), 1), iota((2 * CH, 128), 0)
        x = i * (CH // 4) + line // 8 - corner_m[0]
        y = (line % 8) * 4 + lane // 32 - corner_m[1]
        z = lane % 32 - corner_m[2]
        hit = (x >= 0) & (x < 16) & (y >= 0) & (y < 16) & (z >= 0) & (z < 16)
        full = jnp.where(hit, cut_m[pl.ds(2 * CH * i, 2 * CH)], mid.full[pl.ds(2 * CH * i, 2 * CH)])
        mid.set_target(i * CH, *mid.packed(full, i * CH))

    each(mid.rows // CH, mid_target)
    mid.down()
    gather2[row] = mid.restricted(mean_ref[...])
    send_all(gather2, 1)

    place_c[...] = place_choice(corner_c)
    pad_c[0:16] = jnp.zeros((16, 32, 128), F32)
    pad_c[32:48] = jnp.zeros((16, 32, 128), F32)
    wait_rim(0, rim_recv)
    take_rim(0, beta_e, (row > 0, row < n_x - 1), (col > 0, col < n_y - 1))

    def near_wide(ref, colour, at, rows):
        lane, line = iota((rows, 128), 1), iota((rows, 128), 0)
        odd = (line + lane) % 2 == 1
        own = ref[1 - colour, pl.ds(at, rows)]
        above, below = ref[1 - colour, pl.ds(at + ROWS, rows)], ref[1 - colour, pl.ds(at - ROWS, rows)]
        other = jnp.where(odd, below, above) if colour else jnp.where(odd, above, below)
        after, before = ref[1 - colour, pl.ds(at + 1, rows)], ref[1 - colour, pl.ds(at - 1, rows)]
        return own, other, after, before, pltpu.roll(own, 127, 1), pltpu.roll(own, 1, 1)

    def coarse_weights(k):
        lane = iota((ROWS, 128), 1)
        masks = (None, None, None, None, lane < 127, lane > 0)
        at = EDGE + k * ROWS
        for colour in (0, 1):
            own = beta_e[colour, pl.ds(at, ROWS)]
            near = near_wide(beta_e, colour, at, ROWS)
            faces = [
                0.5 * (own + (other if mask is None else jnp.where(mask, other, 0.0)))
                for other, mask in zip(near, masks)
            ]
            total = faces[0] + faces[1] + faces[2] + faces[3] + faces[4] + faces[5]
            real = own > 0.0
            inv = jnp.where(real, 1.0 / total, 0.0)
            for n in range(6):
                keep = real if masks[n] is None else real & masks[n]
                coef_e[colour, n, pl.ds(k * ROWS, ROWS)] = jnp.where(keep, faces[n] * inv, 0.0)
            inv_e[colour, pl.ds(k * ROWS, ROWS)] = 16.0 * inv

    each(PAIRS, coarse_weights, 1)
    window_c[...] = window_choice(corner_c)
    wait_all(gather2, recv_sems.at[1])

    put = chosen_dot(placed_lhs(gather2[guest]), place_c[...])
    for s in range(8):
        part = put[:, 128 * s : 128 * s + 128]
        for q in range(4):
            put_c[pl.ds(4 * s + q, 16, stride=32)] = part if q == 0 else pltpu.roll(part, 128 - 32 * q, 1)

    pad_c[16:32] = put_c[...].reshape(16, 32, 128)

    def coarse_target(k):
        lane, line = iota((32, 128), 1), iota((32, 128), 0)
        odd = (line + lane) % 2 == 1
        y, z = line - corner_c[1], lane - corner_c[2]
        hit = (y >= 0) & (y < 16) & (z >= 0) & (z < 16)
        planes = []
        for d in (0, 1):
            x = 2 * k + d - corner_c[0]
            planes.append(jnp.where(hit & (x >= 0) & (x < 16), pad_c[16 + x], rhs_c[2 * k + d]))
        at = EDGE + (k + 2) * ROWS + 8
        g_e[0, pl.ds(at, 32)] = jnp.where(odd, planes[1], planes[0])
        g_e[1, pl.ds(at, 32)] = jnp.where(odd, planes[0], planes[1])

    each(16, coarse_target, 4)
    fill_rim(1, g_e)
    send_rim(1)
    wait_rim(1, rim_recv)
    take_rim(1, g_e, (None, None), (None, None))

    def coarse_sweep(colour, first, count, line, rows):
        def body(i):
            k = first + i
            at, here = EDGE + k * ROWS + line, k * ROWS + line
            near = near_wide(field_e, colour, at, rows)
            out = g_e[colour, pl.ds(at, rows)] * inv_e[colour, pl.ds(here, rows)]
            for n in range(6):
                out = out + coef_e[colour, n, pl.ds(here, rows)] * near[n]
            field_e[colour, pl.ds(at, rows)] = out

        each(count, body, 2)

    def coarse_first(k):
        field_e[0, pl.ds(EDGE + k * ROWS, ROWS)] = g_e[0, pl.ds(EDGE + k * ROWS, ROWS)] * inv_e[0, pl.ds(k * ROWS, ROWS)]

    each(PAIRS, coarse_first, 4)
    coarse_sweep(1, 1, 18, 0, ROWS)
    coarse_sweep(0, 1, 18, 0, ROWS)
    coarse_sweep(1, 2, 16, 8, 32)

    def coarse_out(k):
        lane, line = iota((32, 128), 1), iota((32, 128), 0)
        odd = (line + lane) % 2 == 1
        at = EDGE + (k + 2) * ROWS + 8
        red, black = field_e[0, pl.ds(at, 32)], field_e[1, pl.ds(at, 32)]
        low, high = jnp.where(odd, black, red), jnp.where(odd, red, black)
        out_c[2 * k] = low
        out_c[2 * k + 1] = high
        wide_c[1 + 2 * k] = low
        wide_c[2 + 2 * k] = high

    each(16, coarse_out, 4)

    def post_window(buffer, lhs, choice):
        got = chosen_dot(lhs, choice)
        for n in range(3):
            buffer[row, pl.ds(16 * n, 16)] = got[1:17, 128 * n : 128 * n + 128]
        for n, (x, h) in enumerate(((0, 0), (0, 1), (17, 0), (17, 1))):
            buffer[row, pl.ds(48 + n, 1)] = got[x : x + 1, 128 * h : 128 * h + 128]

    def cut_window_c(x):
        cut_c[pl.ds(32 * x, 32)] = wide_c[corner_c[0] + x]

    each(18, cut_window_c)
    lane24 = iota((24, 128), 1)
    blocks = []
    for s in range(8):
        block = None
        for q in range(4):
            part = cut_c[pl.ds(4 * s + q, 24, stride=32)]
            if q == 0:
                block = part
            else:
                block = jnp.where(lane24 // 32 == q, pltpu.roll(part, 32 * q, 1), block)
        blocks.append(block)
    post_window(gather3, jnp.concatenate(blocks, axis=1), window_c[...])
    send_all(gather3, 2)
    spread_ref[...] = spread_choice()
    window_m[...] = window_choice(corner_m)
    wait_all(gather3, recv_sems.at[2])

    mid.start_up([gather3[parent_m[row, col]]], spread_ref[...])
    mid.up()

    def mid_out(i):
        full = mid.finished(CH * i)
        mid.full[pl.ds(2 * CH * i, 2 * CH)] = full
        wide_m[pl.ds(1 + CH // 4 * i, CH // 4)] = full.reshape(CH // 4, 8, 128)

    each(mid.rows // CH, mid_out)

    def cut_window_m(x):
        cut_m[pl.ds(8 * x, 8)] = wide_m[corner_m[0] + x]

    each(18, cut_window_m)
    lhs = jnp.concatenate([cut_m[pl.ds(s, 24, stride=8)] for s in range(8)], axis=1)
    post_window(gather4, lhs, window_m[...])
    send_all(gather4, 3)
    for s in range(8):
        out_m[0, 0, :, 128 * s : 128 * s + 128] = mid.full[pl.ds(s, 32, stride=8)]
    wait_all(gather4, recv_sems.at[3])

    owners = [parent_f[row, col, slot] for slot in range(2)]
    fine.start_up([gather4[jnp.maximum(owner, 0)] for owner in owners], spread_ref[...])
    fine.up()

    def fine_out(i):
        fine.full[pl.ds(2 * CH * i, 2 * CH)] = fine.finished(CH * i)

    each(fine.rows // CH, fine_out)
    for box in range(2):
        for s in range(8):
            part = fine.full[pl.ds(box * 256 + s, 32, stride=8)]
            out_f[0, 0, box, :, 128 * s : 128 * s + 128] = jnp.where(owners[box] >= 0, part, 0.0)

    for stage, buffer in enumerate((gather1, gather2, gather3, gather4)):
        wait_all(buffer, send_sems.at[stage])
    for turn in (0, 1):
        wait_rim(turn, rim_send)


def level_scratch(count):
    rows = count * 128
    return [
        pltpu.VMEM((2 * rows, 128), F32),
        pltpu.VMEM((rows + 16, 128), F32),
        pltpu.VMEM((rows + 16, 128), F32),
        pltpu.VMEM((2, 6, rows, 128), F32),
        pltpu.VMEM((2, rows, 128), F32),
        pltpu.VMEM((2, rows, 128), F32),
        pltpu.VMEM((2, rows, 128), F32),
        pltpu.VMEM((rows, 128), F32),
        pltpu.VMEM((rows, 128), F32),
    ]


def on_device(*args):
    shapes = [args[0].shape, args[2].shape, args[4].shape]
    vmem = pl.BlockSpec(memory_space=pltpu.VMEM)
    smem = pl.BlockSpec(memory_space=pltpu.SMEM)
    call = pl.pallas_call(
        kernel,
        out_shape=[jax.ShapeDtypeStruct(shape, F32) for shape in shapes],
        in_specs=[vmem] * 6 + [smem] * 4,
        out_specs=[vmem] * 3,
        scratch_shapes=[
            pltpu.VMEM((16, 2, 32, 128), F32),
            pltpu.VMEM((16, 32, 128), F32),
            pltpu.VMEM((16, 56, 128), F32),
            pltpu.VMEM((16, 56, 128), F32),
            pltpu.VMEM((2, 512, 128), F32),
            pltpu.VMEM((2, 576, 128), F32),
            pltpu.VMEM((512, 128), BF16),
            pltpu.VMEM((256, 256), BF16),
            pltpu.VMEM((256, 1024), BF16),
            pltpu.VMEM((256, 1024), BF16),
            pltpu.VMEM((1024, 384), BF16),
            pltpu.VMEM((1024, 384), BF16),
            pltpu.VMEM((128, 128), F32),
            pltpu.VMEM((512, 128), F32),
            pltpu.VMEM((48, 8, 128), F32),
            pltpu.VMEM((48, 32, 128), F32),
            pltpu.VMEM((33, 8, 128), F32),
            pltpu.VMEM((33, 32, 128), F32),
            pltpu.VMEM((256, 128), F32),
            pltpu.VMEM((24 * 32, 128), F32),
            pltpu.VMEM((2, WIDE, 128), F32),
            pltpu.VMEM((2, WIDE, 128), F32),
            pltpu.VMEM((2, WIDE, 128), F32),
            pltpu.VMEM((2, 6, PAIRS * ROWS, 128), F32),
            pltpu.VMEM((2, PAIRS * ROWS, 128), F32),
            *level_scratch(2),
            *level_scratch(1),
            pltpu.SemaphoreType.DMA((4,)),
            pltpu.SemaphoreType.DMA((4,)),
            pltpu.SemaphoreType.DMA((2,)),
            pltpu.SemaphoreType.DMA((2,)),
        ],
        compiler_params=pltpu.CompilerParams(
            collective_id=0, has_side_effects=True, vmem_limit_bytes=48 * 2**20
        ),
        name="v_cycle",
    )
    return tuple(call(*args))


def solution(mesh):
    return jax.shard_map(
        on_device,
        mesh=mesh,
        in_specs=(
            P("xb", "yb", None),
            P("xb", "yb", None),
            P("xb", "yb", None, None),
            P("xb", "yb", None, None),
            P("xb", "yb", None, None, None),
            P("xb", "yb", None, None, None),
            P(),
            P(),
            P(),
            P(),
        ),
        out_specs=(P("xb", "yb", None), P("xb", "yb", None, None), P("xb", "yb", None, None, None)),
        check_vma=False,
    )
```

```python
import functools

import jax
import jax.numpy as jnp
from jax import lax
from jax.experimental import pallas as pl
from jax.experimental.pallas import tpu as pltpu
from jax.sharding import PartitionSpec as P

MESH = pl.DeviceIdType.MESH
F32 = jnp.float32
BF16 = jnp.bfloat16
CH = 64
PAIRS = 20
ROWS = 48
EDGE = 56
WIDE = 2 * EDGE + PAIRS * ROWS
CHIPS = ((2, 1), (1, 1), (3, 1), (2, 0), (0, 1), (1, 0), (3, 0))
SAME_CORE = [(dx, dh, 0) for dx, dh in CHIPS]
PEERS = [(dx, dh, dc) for dx, dh in CHIPS for dc in (0, 1)] + [(0, 0, 1)]


def iota(shape, dim):
    return lax.broadcasted_iota(jnp.int32, shape, dim)


def each(count, body, unroll=True):
    def step(i, carry):
        body(i)
        return carry

    lax.fori_loop(0, count, step, 0, unroll=unroll)


def chosen_dot(values, choice):
    rows = values.shape[0]
    high = values.astype(BF16).astype(F32)
    rest = values - high
    middle = rest.astype(BF16).astype(F32)
    terms = jnp.concatenate([high, middle, rest - middle], axis=0).astype(BF16)
    out = lax.dot_general(terms, choice, (((1,), (0,)), ((), ())), preferred_element_type=F32)
    return out[:rows] + out[rows : 2 * rows] + out[2 * rows :]


def onehot(mask, value=1.0):
    return jnp.where(mask, value, 0.0).astype(BF16)


class Level:
    def __init__(self, count, scale, refs):
        self.count, self.scale, self.rows = count, scale, count * 128
        (self.full, self.red, self.black, self.coef, self.g, self.inv, self.hb, self.tot, self.rest) = refs

    def field(self, colour):
        return self.black if colour else self.red

    def near(self, colour, at):
        ref = self.field(1 - colour)
        lane = iota((CH, 128), 1)
        odd = (lane // 32 + lane) % 2 == 1
        own = ref[pl.ds(8 + at, CH)]
        above, below = ref[pl.ds(16 + at, CH)], ref[pl.ds(at, CH)]
        after, before = ref[pl.ds(9 + at, CH)], ref[pl.ds(7 + at, CH)]
        other = jnp.where(odd, below, above) if colour else jnp.where(odd, above, below)
        return (
            own,
            other,
            pltpu.roll(jnp.where(lane >= 32, own, after), 96, 1),
            pltpu.roll(jnp.where(lane < 96, own, before), 32, 1),
            pltpu.roll(own, 127, 1),
            pltpu.roll(own, 1, 1),
        )

    def clear_ends(self):
        for ref in (self.red, self.black):
            ref[pl.ds(0, 8)] = jnp.zeros((8, 128), F32)
            ref[pl.ds(8 + self.rows, 8)] = jnp.zeros((8, 128), F32)

    def unfold(self, load):
        for box in range(self.count):
            for s in range(8):
                self.full[pl.ds(box * 256 + s, 32, stride=8)] = load(box, s)

    def packed(self, full, at):
        lane = iota((CH, 128), 1)
        odd = (lane // 32 + lane) % 2 == 1
        planes = full.reshape(CH // 8, 2, 8, 128)
        low, high = planes[:, 0].reshape(CH, 128), planes[:, 1].reshape(CH, 128)
        return jnp.where(odd, high, low), jnp.where(odd, low, high)

    def set_fields(self):
        def body(i):
            at = i * CH
            red, black = self.packed(self.full[pl.ds(2 * at, 2 * CH)], at)
            self.red[pl.ds(8 + at, CH)] = red
            self.black[pl.ds(8 + at, CH)] = black

        each(self.rows // CH, body)

    def set_weights(self):
        def body(i):
            at = i * CH
            lane, row = iota((CH, 128), 1), iota((CH, 128), 0)
            odd = (lane // 32 + lane) % 2 == 1
            s = row % 8
            pair = ((at + row) // 8) % 16
            z = lane % 32
            inside_y = (jnp.logical_not((s == 7) & (lane >= 96)), jnp.logical_not((s == 0) & (lane < 32)))
            inside_z = (z < 31, z > 0)
            for colour in (0, 1):
                first, last = (odd, jnp.logical_not(odd)) if colour else (jnp.logical_not(odd), odd)
                edge = (first & (pair == 0)) | (last & (pair == 15))
                masks = (None, jnp.logical_not(edge)) + inside_y + inside_z
                own = self.field(colour)[pl.ds(8 + at, CH)]
                near = self.near(colour, at)
                faces = [
                    0.5 * (own + (other if mask is None else jnp.where(mask, other, 0.0)))
                    for other, mask in zip(near, masks)
                ]
                total = faces[0] + faces[1] + faces[2] + faces[3] + faces[4] + faces[5]
                inv = 1.0 / total
                for n in range(6):
                    part = faces[n] * inv
                    self.coef[colour, n, pl.ds(at, CH)] = (
                        part if masks[n] is None else jnp.where(masks[n], part, 0.0)
                    )
                self.inv[colour, pl.ds(at, CH)] = inv * (1.0 / self.scale)
                self.hb[colour, pl.ds(at, CH)] = 0.5 * own * inv
                if colour == 0:
                    self.tot[pl.ds(at, CH)] = self.scale * total

        each(self.rows // CH, body)

    def set_target(self, at, red, black):
        for colour, value in ((0, red), (1, black)):
            self.g[colour, pl.ds(at, CH)] = value * self.inv[colour, pl.ds(at, CH)]

    def fresh(self, colour, at):
        near = self.near(colour, at)
        out = self.g[colour, pl.ds(at, CH)]
        for n in range(6):
            out = out + self.coef[colour, n, pl.ds(at, CH)] * near[n]
        return out

    def half_sweep(self, colour):
        def body(i):
            at = i * CH
            self.field(colour)[pl.ds(8 + at, CH)] = self.fresh(colour, at)

        each(self.rows // CH, body)

    def down(self):
        def first(i):
            at = i * CH
            self.red[pl.ds(8 + at, CH)] = self.g[0, pl.ds(at, CH)]

        each(self.rows // CH, first)
        self.half_sweep(1)
        self.half_sweep(0)
        self.half_sweep(1)

        def left(i):
            at = i * CH
            self.rest[pl.ds(at, CH)] = self.tot[pl.ds(at, CH)] * (
                self.fresh(0, at) - self.red[pl.ds(8 + at, CH)]
            )

        each(self.rows // CH, left)

    def restricted(self, mean):
        parts = []
        for box in range(self.count):
            for h in range(2):
                parts.append(
                    jnp.concatenate(
                        [self.rest[pl.ds(box * 128 + 4 * h + j, 16, stride=8)] for j in range(4)], axis=1
                    )
                )
        return chosen_dot(jnp.concatenate(parts, axis=0), mean)

    def start_up(self, pieces, spread):
        sub, lane = iota((8, 128), 0), iota((8, 128), 1)
        odd = (lane // 32 + lane) % 2 == 1
        even = jnp.logical_not(odd)
        rows_of = lane // 32 == sub % 4
        rows_of_face = (
            ((lane < 16) & (sub == 0))
            | ((lane >= 16) & (lane < 32) & (sub == 7))
            | ((lane >= 32) & (lane < 64) & ((lane % 16) // 2 == sub))
        )

        def tiles(rows):
            return jnp.broadcast_to(rows[:, None, :], (rows.shape[0], 8, 128))

        def halves(first, second):
            return jnp.where((sub < 4)[None], tiles(first), tiles(second))

        for box, piece in enumerate(pieces):
            core = jnp.concatenate(
                [
                    halves(piece[0:16], piece[16:32]),
                    halves(piece[48:49], piece[49:50]),
                    halves(piece[50:51], piece[51:52]),
                ],
                axis=0,
            )
            core = jnp.where(rows_of[None], core, 0.0).reshape(144, 128)
            face = jnp.where(rows_of_face[None], tiles(piece[32:48]), 0.0).reshape(128, 128)
            face = jnp.concatenate([face, jnp.zeros((16, 128), F32)], axis=0)
            grown = chosen_dot(jnp.concatenate([core, face], axis=1), spread)
            inner, border = grown[:128, :128], grown[:128, 128:].reshape(16, 8, 128)
            low, high = grown[128:136, :128], grown[136:144, :128]
            at = box * 128
            self.black[pl.ds(8 + at, 128)] = self.black[pl.ds(8 + at, 128)] + inner
            for colour in (0, 1):
                first, last = (odd, even) if colour else (even, odd)
                ghost = jnp.concatenate(
                    [
                        border[:1] + jnp.where(first, low, 0.0)[None],
                        border[1:15],
                        border[15:] + jnp.where(last, high, 0.0)[None],
                    ],
                    axis=0,
                ).reshape(128, 128)
                self.g[colour, pl.ds(at, 128)] = (
                    self.g[colour, pl.ds(at, 128)] + self.hb[colour, pl.ds(at, 128)] * ghost
                )

    def up(self):
        for colour in (0, 1, 0, 1):
            self.half_sweep(colour)

    def finished(self, at):
        lane = iota((CH, 128), 1)
        odd = (lane // 32 + lane) % 2 == 1
        red, black = self.red[pl.ds(8 + at, CH)], self.black[pl.ds(8 + at, CH)]
        low = jnp.where(odd, black, red).reshape(CH // 8, 1, 8, 128)
        high = jnp.where(odd, red, black).reshape(CH // 8, 1, 8, 128)
        return jnp.concatenate([low, high], axis=1).reshape(2 * CH, 128)


def spread_choice():
    l, n = iota((256, 256), 0), iota((256, 256), 1)
    z, q = n % 32, (n % 128) // 32
    inner = (l < 128) & (n < 128) & ((l // 16) % 2 == q // 2) & (l % 16 == z // 2)
    f = l - 128
    along_y = (f >= 0) & (f < 32) & (q == jnp.where(f < 16, 0, 3)) & (z // 2 == f % 16)
    along_z = (f >= 32) & (f < 64) & (q // 2 == f % 2) & (z == jnp.where(f < 48, 0, 31))
    return onehot(inner | ((n >= 128) & (along_y | along_z)))


def mean_choice():
    k, n = iota((512, 128), 0), iota((512, 128), 1)
    lane = k % 128
    return onehot(n == 32 * (k // 128) + 16 * (lane // 64) + (lane % 32) // 2, 0.125)


def place_choice(corner):
    k, n = iota((256, 1024), 0), iota((256, 1024), 1)
    return onehot(n == (k // 16) * 32 + k % 16 + corner[1] * 32 + corner[2])


def window_choice(corner):
    n = iota((1, 384), 1)
    i = n % 16
    source = jnp.where(n < 256, (n // 16) * 32 + i, -4096)
    source = jnp.where((n >= 256) & (n < 272), i - 32, source)
    source = jnp.where((n >= 272) & (n < 288), i + 512, source)
    source = jnp.where((n >= 288) & (n < 304), i * 32 - 1, source)
    source = jnp.where((n >= 304) & (n < 320), i * 32 + 16, source)
    return onehot(iota((1024, 384), 0) == source + corner[1] * 32 + corner[2])


def placed_lhs(piece):
    return jnp.concatenate([piece[0:16], piece[16:32]], axis=1)


def kernel(
    far_rhs_c, far_beta_c, far_rhs_m, far_beta_m, far_rhs_f, far_beta_f,
    far_parent_m, far_offset_m, far_parent_f, far_offset_f,
    far_out_c, far_out_m, far_out_f,
    rhs_c, beta_c, rhs_m, beta_m, rhs_f, beta_f, parent_m, offset_m, parent_f, offset_f,
    out_m, out_f,
    gather1, gather2, gather3, gather4, relay_out1, relay_in1, relay_out3, relay_in3, relay_out4, relay_in4,
    rim_out, rim_in,
    mean_ref, spread_ref, place_m, place_c, window_m, window_c,
    put_m, put_c, pad_m, pad_c, wide_m, wide_c, cut_m, cut_c,
    beta_e, g_e, field_e, coef_e, inv_e,
    *rest,
):
    fine_refs, mid_refs = rest[:9], rest[9:18]
    send_sems, recv_sems, relay_send, relay_recv, rim_send, rim_recv, load_sems, store_sems = rest[18:]
    fine = Level(2, 1.0, fine_refs)
    mid = Level(1, 0.25, mid_refs)
    n_x, n_y = lax.axis_size("xb"), lax.axis_size("yb")
    row, col = lax.axis_index("xb"), lax.axis_index("yb")

    def load(n, source, target):
        copy = pltpu.make_async_copy(source, target, load_sems.at[n])
        copy.start()
        return copy

    def store(n, source, target):
        copy = pltpu.make_async_copy(source, target, store_sems.at[n])
        copy.start()
        return copy

    load_beta_c = load(3, far_beta_c, beta_c)
    load_beta_f = load(0, far_beta_f.at[0, 0], beta_f)
    load_rhs_f = load(1, far_rhs_f.at[0, 0], rhs_f)
    load_beta_m = load(2, far_beta_m.at[0, 0], beta_m)
    load_rhs_m = load(4, far_rhs_m.at[0, 0], rhs_m)
    load_rhs_c = load(5, far_rhs_c, rhs_c)
    load_tables = (
        load(6, far_parent_m, parent_m),
        load(7, far_offset_m, offset_m),
        load(8, far_parent_f.at[col], parent_f),
        load(9, far_offset_f.at[col], offset_f),
    )

    def beside(dx, dy):
        return (lax.rem(row + dx + n_x, n_x), lax.rem(col + dy + n_y, n_y))

    def peer(dx, dh, dc):
        x, h, c = row // 4, (row // 2) % 2, row % 2
        return (((x + dx) % 4) * 4 + ((h + dh) % 2) * 2 + (c + dc) % 2, col)

    barrier = pltpu.get_barrier_semaphore()
    greeted = [peer(*hop) for hop in PEERS] + [beside(dx, dy) for dx in (-1, 0, 1) for dy in (-1, 1)]
    for device in greeted:
        pl.semaphore_signal(barrier, inc=1, device_id=device, device_id_type=MESH)

    twin = row + 1 - 2 * (row % 2)
    chip = row // 2

    def send_all(buffer, stage, place, hops):
        for hop in hops:
            pltpu.make_async_remote_copy(
                src_ref=buffer.at[place],
                dst_ref=buffer.at[place],
                send_sem=send_sems.at[stage],
                recv_sem=recv_sems.at[stage],
                device_id=peer(*hop),
                device_id_type=MESH,
            ).start()

    def wait_all(buffer, sem, hops):
        whole = buffer.at[pl.ds(0, len(hops))]
        pltpu.make_async_copy(whole, whole, sem).wait()

    def wait_one(buffer, sem):
        pltpu.make_async_copy(buffer, buffer, sem).wait()

    def relay(n, source, target):
        pltpu.make_async_remote_copy(
            src_ref=source,
            dst_ref=target,
            send_sem=relay_send.at[n],
            recv_sem=relay_recv.at[n],
            device_id=(twin, col),
            device_id_type=MESH,
        ).start()

    def own_core(device):
        return lax.rem(device, 2) == row % 2

    def chip_of(device):
        return lax.div(device, 2)

    def send_rim(turn):
        def copy(kind, source, size, target, device):
            pltpu.make_async_remote_copy(
                src_ref=rim_out.at[turn, pl.ds(source, size)],
                dst_ref=rim_in.at[turn, pl.ds(target, size)],
                send_sem=rim_send.at[turn],
                recv_sem=rim_recv.at[3 * turn + kind],
                device_id=device,
                device_id_type=MESH,
            ).start()

        for side_x in (0, 1):
            for side_y in (0, 1):
                copy(
                    2, 256 + 128 * side_y + 112 * side_x, 16,
                    512 + 16 * (2 * (1 - side_x) + 1 - side_y),
                    beside(2 * side_x - 1, 2 * side_y - 1),
                )
        for side in (0, 1):
            copy(1, 256 + 128 * side, 128, 256 + 128 * (1 - side), beside(0, 2 * side - 1))
        for side in (0, 1):
            copy(0, 128 * side, 128, 128 * (1 - side), beside(2 * side - 1, 0))

    def wait_rim(turn, kind):
        wait_one(rim_in.at[turn, pl.ds(256 * kind, (256, 256, 64)[kind])], rim_recv.at[3 * turn + kind])

    def fill_rim(turn, ref):
        tile_row = iota((8, 128), 0)
        for side in (0, 1):
            for colour in (0, 1):
                for d in (0, 1):
                    at = EDGE + ((2, 16)[side] + d) * ROWS + 8
                    rim_out[turn, pl.ds(128 * side + (2 * colour + d) * 32, 32)] = ref[colour, pl.ds(at, 32)]

        def body(k):
            at = EDGE + (k + 2) * ROWS
            red, black = ref[0, pl.ds(at + 8, 8)], ref[1, pl.ds(at + 8, 8)]
            rim_out[turn, pl.ds(256 + k * 8, 8)] = jnp.where(tile_row < 4, red, pltpu.roll(black, 4, 0))
            red, black = ref[0, pl.ds(at + 32, 8)], ref[1, pl.ds(at + 32, 8)]
            rim_out[turn, pl.ds(384 + k * 8, 8)] = jnp.where(tile_row < 4, pltpu.roll(black, 4, 0), red)

        each(16, body)

    def keep(value, *sides):
        for side in sides:
            if side is not None:
                value = jnp.where(side, value, 0.0)
        return value

    def take_y(turn, ref, inside_y):
        def body(k):
            for side in (0, 1):
                at = EDGE + (k + 2) * ROWS + 40 * side
                part = keep(rim_in[turn, pl.ds(256 + 128 * side + 8 * k, 8)], inside_y[side])
                ref[0, pl.ds(at, 8)] = part
                ref[1, pl.ds(at, 8)] = pltpu.roll(part, 4, 0)

        each(16, body)

    def take_x(turn, ref, inside_x, inside_y):
        for side in (0, 1):
            for colour in (0, 1):
                for d in (0, 1):
                    at = EDGE + ((0, 18)[side] + d) * ROWS + 8
                    part = rim_in[turn, pl.ds(128 * side + (2 * colour + d) * 32, 32)]
                    ref[colour, pl.ds(at, 32)] = keep(part, inside_x[side])
            for other in (0, 1):
                for d in (0, 1):
                    at = EDGE + (18 * side + d) * ROWS + 40 * other
                    part = rim_in[turn, pl.ds(512 + 16 * (2 * side + other) + 8 * d, 8)]
                    part = keep(part, inside_x[side], inside_y[other])
                    ref[0, pl.ds(at, 8)] = part
                    ref[1, pl.ds(at, 8)] = pltpu.roll(part, 4, 0)

    mean_ref[...] = mean_choice()
    fine.clear_ends()

    def own_beta(k):
        lane, line = iota((32, 128), 1), iota((32, 128), 0)
        odd = (line + lane) % 2 == 1
        low, high = beta_c[2 * k], beta_c[2 * k + 1]
        at = EDGE + (k + 2) * ROWS + 8
        beta_e[0, pl.ds(at, 32)] = jnp.where(odd, high, low)
        beta_e[1, pl.ds(at, 32)] = jnp.where(odd, low, high)

    for colour in (0, 1):
        beta_e[colour, pl.ds(0, EDGE)] = jnp.zeros((EDGE, 128), F32)
        beta_e[colour, pl.ds(WIDE - EDGE, EDGE)] = jnp.zeros((EDGE, 128), F32)
    load_beta_c.wait()
    each(16, own_beta, 4)
    fill_rim(0, beta_e)
    load_beta_f.wait()
    fine.unfold(lambda box, s: beta_f[box, :, 128 * s : 128 * s + 128])
    fine.set_fields()
    fine.set_weights()
    load_rhs_f.wait()
    fine.unfold(lambda box, s: rhs_f[box, :, 128 * s : 128 * s + 128])

    def fine_target(i):
        at = i * CH
        fine.set_target(at, *fine.packed(fine.full[pl.ds(2 * at, 2 * CH)], at))

    each(fine.rows // CH, fine_target)
    pl.semaphore_wait(barrier, len(greeted))
    send_rim(0)
    fine.down()
    gather1[chip] = fine.restricted(mean_ref[...]).reshape(2, 32, 128)
    send_all(gather1, 0, chip, SAME_CORE)

    mid.clear_ends()
    load_beta_m.wait()
    mid.unfold(lambda box, s: beta_m[:, 128 * s : 128 * s + 128])
    mid.set_fields()
    mid.set_weights()
    load_rhs_m.wait()
    mid.unfold(lambda box, s: rhs_m[:, 128 * s : 128 * s + 128])

    for copy in load_tables:
        copy.wait()

    def find_fine(i, carry):
        index, place, x, y, z, twin_index, twin_place = carry
        for slot in range(2):
            twin_hit = parent_f[slot, i] == twin
            twin_index = jnp.where(twin_hit, i, twin_index)
            twin_place = jnp.where(twin_hit, slot, twin_place)
            hit = parent_f[slot, i] == row
            index = jnp.where(hit, i, index)
            place = jnp.where(hit, slot, place)
            x = jnp.where(hit, offset_f[0, slot, i], x)
            y = jnp.where(hit, offset_f[1, slot, i], y)
            z = jnp.where(hit, offset_f[2, slot, i], z)
        return index, place, x, y, z, twin_index, twin_place

    def find_mid(i, carry):
        index, x, y, z = carry
        hit = parent_m[col, i] == row
        return (
            jnp.where(hit, i, index),
            jnp.where(hit, offset_m[0, col, i], x),
            jnp.where(hit, offset_m[1, col, i], y),
            jnp.where(hit, offset_m[2, col, i], z),
        )

    zero, one = jnp.int32(0), jnp.int32(1)
    child, child_slot, *corner_m, twin_child, twin_slot = lax.fori_loop(
        0, 16, find_fine, (zero, zero, one, one, one, zero, zero)
    )
    guest, *corner_c = lax.fori_loop(0, 16, find_mid, (zero, one, one, one))
    place_m[...] = place_choice(corner_m)
    pad_m[0:16] = jnp.zeros((16, 8, 128), F32)
    pad_m[32:48] = jnp.zeros((16, 8, 128), F32)

    wait_all(gather1, recv_sems.at[0], SAME_CORE)
    relay_out1[...] = gather1[chip_of(twin_child), twin_slot]
    relay(0, relay_out1, relay_in1)
    wait_one(relay_in1, relay_recv.at[0])

    piece = jnp.where(own_core(child), gather1[chip_of(child), child_slot], relay_in1[...])
    put = chosen_dot(placed_lhs(piece), place_m[...])
    for s in range(8):
        put_m[pl.ds(s, 16, stride=8)] = put[:, 128 * s : 128 * s + 128]
    pad_m[16:32] = put_m[...].reshape(16, 8, 128)

    def shift_m(x):
        cut_m[pl.ds(8 * x, 8)] = pad_m[16 - corner_m[0] + x]

    each(32, shift_m)

    def mid_target(i):
        lane, line = iota((2 * CH, 128), 1), iota((2 * CH, 128), 0)
        x = i * (CH // 4) + line // 8 - corner_m[0]
        y = (line % 8) * 4 + lane // 32 - corner_m[1]
        z = lane % 32 - corner_m[2]
        hit = (x >= 0) & (x < 16) & (y >= 0) & (y < 16) & (z >= 0) & (z < 16)
        full = jnp.where(hit, cut_m[pl.ds(2 * CH * i, 2 * CH)], mid.full[pl.ds(2 * CH * i, 2 * CH)])
        mid.set_target(i * CH, *mid.packed(full, i * CH))

    each(mid.rows // CH, mid_target)
    mid.down()
    gather2[row] = mid.restricted(mean_ref[...])
    send_all(gather2, 1, row, PEERS)

    place_c[...] = place_choice(corner_c)
    pad_c[0:16] = jnp.zeros((16, 32, 128), F32)
    pad_c[32:48] = jnp.zeros((16, 32, 128), F32)
    for kind in (0, 1, 2):
        wait_rim(0, kind)
    inside_x, inside_y = (row > 0, row < n_x - 1), (col > 0, col < n_y - 1)
    take_y(0, beta_e, inside_y)
    take_x(0, beta_e, inside_x, inside_y)

    def near_wide(ref, colour, at, rows):
        lane, line = iota((rows, 128), 1), iota((rows, 128), 0)
        odd = (line + lane) % 2 == 1
        own = ref[1 - colour, pl.ds(at, rows)]
        above, below = ref[1 - colour, pl.ds(at + ROWS, rows)], ref[1 - colour, pl.ds(at - ROWS, rows)]
        other = jnp.where(odd, below, above) if colour else jnp.where(odd, above, below)
        after, before = ref[1 - colour, pl.ds(at + 1, rows)], ref[1 - colour, pl.ds(at - 1, rows)]
        return own, other, after, before, pltpu.roll(own, 127, 1), pltpu.roll(own, 1, 1)

    def coarse_weights(k):
        lane = iota((ROWS, 128), 1)
        masks = (None, None, None, None, lane < 127, lane > 0)
        at = EDGE + k * ROWS
        for colour in (0, 1):
            own = beta_e[colour, pl.ds(at, ROWS)]
            near = near_wide(beta_e, colour, at, ROWS)
            faces = [
                0.5 * (own + (other if mask is None else jnp.where(mask, other, 0.0)))
                for other, mask in zip(near, masks)
            ]
            total = faces[0] + faces[1] + faces[2] + faces[3] + faces[4] + faces[5]
            real = own > 0.0
            inv = jnp.where(real, 1.0 / total, 0.0)
            for n in range(6):
                keep = real if masks[n] is None else real & masks[n]
                coef_e[colour, n, pl.ds(k * ROWS, ROWS)] = jnp.where(keep, faces[n] * inv, 0.0)
            inv_e[colour, pl.ds(k * ROWS, ROWS)] = 16.0 * inv

    each(PAIRS, coarse_weights, 1)
    window_c[...] = window_choice(corner_c)
    wait_all(gather2, recv_sems.at[1], PEERS)

    put = chosen_dot(placed_lhs(gather2[guest]), place_c[...])
    for s in range(8):
        part = put[:, 128 * s : 128 * s + 128]
        for q in range(4):
            put_c[pl.ds(4 * s + q, 16, stride=32)] = part if q == 0 else pltpu.roll(part, 128 - 32 * q, 1)

    pad_c[16:32] = put_c[...].reshape(16, 32, 128)

    load_rhs_c.wait()

    def coarse_target(k):
        lane, line = iota((32, 128), 1), iota((32, 128), 0)
        odd = (line + lane) % 2 == 1
        y, z = line - corner_c[1], lane - corner_c[2]
        hit = (y >= 0) & (y < 16) & (z >= 0) & (z < 16)
        planes = []
        for d in (0, 1):
            x = 2 * k + d - corner_c[0]
            planes.append(jnp.where(hit & (x >= 0) & (x < 16), pad_c[16 + x], rhs_c[2 * k + d]))
        at = EDGE + (k + 2) * ROWS + 8
        g_e[0, pl.ds(at, 32)] = jnp.where(odd, planes[1], planes[0])
        g_e[1, pl.ds(at, 32)] = jnp.where(odd, planes[0], planes[1])

    each(16, coarse_target, 4)
    fill_rim(1, g_e)
    send_rim(1)

    def coarse_first(first, count, line, rows):
        def body(i):
            at, here = EDGE + (first + i) * ROWS + line, (first + i) * ROWS + line
            field_e[0, pl.ds(at, rows)] = g_e[0, pl.ds(at, rows)] * inv_e[0, pl.ds(here, rows)]

        each(count, body, 4 if count % 4 == 0 else True)

    def coarse_sweep(colour, first, count, line=0, rows=ROWS):
        def body(i):
            k = first + i
            at, here = EDGE + k * ROWS + line, k * ROWS + line
            near = near_wide(field_e, colour, at, rows)
            out = g_e[colour, pl.ds(at, rows)] * inv_e[colour, pl.ds(here, rows)]
            for n in range(6):
                out = out + coef_e[colour, n, pl.ds(here, rows)] * near[n]
            field_e[colour, pl.ds(at, rows)] = out

        each(count, body, 2 if count % 2 == 0 else True)

    coarse_first(2, 16, 8, 32)
    wait_rim(1, 1)
    take_y(1, g_e, (None, None))
    coarse_first(2, 16, 0, 8)
    coarse_first(2, 16, 40, 8)
    coarse_sweep(1, 3, 14)
    coarse_sweep(0, 4, 12)
    coarse_sweep(1, 5, 10, 8, 32)
    wait_rim(1, 0)
    wait_rim(1, 2)
    take_x(1, g_e, (None, None), (None, None))
    for first in (0, 18):
        coarse_first(first, 2, 0, ROWS)
    for first in (1, 17):
        coarse_sweep(1, first, 2)
    for first in (1, 16):
        coarse_sweep(0, first, 3)
    for first in (2, 15):
        coarse_sweep(1, first, 3, 8, 32)

    def coarse_out(k):
        lane, line = iota((32, 128), 1), iota((32, 128), 0)
        odd = (line + lane) % 2 == 1
        at = EDGE + (k + 2) * ROWS + 8
        red, black = field_e[0, pl.ds(at, 32)], field_e[1, pl.ds(at, 32)]
        low, high = jnp.where(odd, black, red), jnp.where(odd, red, black)
        wide_c[1 + 2 * k] = low
        wide_c[2 + 2 * k] = high

    each(16, coarse_out, 4)

    def post_window(buffer, stage, lhs, choice):
        got = chosen_dot(lhs, choice)
        for n in range(3):
            buffer[chip, pl.ds(16 * n, 16)] = got[1:17, 128 * n : 128 * n + 128]
        for n, (x, h) in enumerate(((0, 0), (0, 1), (17, 0), (17, 1))):
            buffer[chip, pl.ds(48 + n, 1)] = got[x : x + 1, 128 * h : 128 * h + 128]
        send_all(buffer, stage, chip, SAME_CORE)

    def cut_window_c(x):
        cut_c[pl.ds(32 * x, 32)] = wide_c[corner_c[0] + x]

    each(18, cut_window_c)
    lane24 = iota((24, 128), 1)
    blocks = []
    for s in range(8):
        block = None
        for q in range(4):
            part = cut_c[pl.ds(4 * s + q, 24, stride=32)]
            if q == 0:
                block = part
            else:
                block = jnp.where(lane24 // 32 == q, pltpu.roll(part, 32 * q, 1), block)
        blocks.append(block)
    post_window(gather3, 2, jnp.concatenate(blocks, axis=1), window_c[...])
    store_c = store(0, wide_c.at[pl.ds(1, 32)], far_out_c)
    spread_ref[...] = spread_choice()
    window_m[...] = window_choice(corner_m)
    wait_all(gather3, recv_sems.at[2], SAME_CORE)
    relay_out3[...] = gather3[chip_of(parent_m[col, twin])]
    relay(1, relay_out3, relay_in3)
    wait_one(relay_in3, relay_recv.at[1])

    owner_m = parent_m[col, row]
    piece = jnp.where(own_core(owner_m), gather3[chip_of(owner_m)], relay_in3[...])
    mid.start_up([piece], spread_ref[...])
    mid.up()

    def mid_out(i):
        full = mid.finished(CH * i)
        mid.full[pl.ds(2 * CH * i, 2 * CH)] = full
        wide_m[pl.ds(1 + CH // 4 * i, CH // 4)] = full.reshape(CH // 4, 8, 128)

    each(mid.rows // CH, mid_out)

    def cut_window_m(x):
        cut_m[pl.ds(8 * x, 8)] = wide_m[corner_m[0] + x]

    each(18, cut_window_m)
    lhs = jnp.concatenate([cut_m[pl.ds(s, 24, stride=8)] for s in range(8)], axis=1)
    post_window(gather4, 3, lhs, window_m[...])
    for s in range(8):
        out_m[:, 128 * s : 128 * s + 128] = mid.full[pl.ds(s, 32, stride=8)]
    store_m = store(1, out_m, far_out_m.at[0, 0])
    wait_all(gather4, recv_sems.at[3], SAME_CORE)
    for slot in range(2):
        relay_out4[slot] = gather4[chip_of(jnp.maximum(parent_f[slot, twin], 0))]
    relay(2, relay_out4, relay_in4)
    wait_one(relay_in4, relay_recv.at[2])

    owners = [parent_f[slot, row] for slot in range(2)]
    pieces = []
    for slot, owner in enumerate(owners):
        owner = jnp.maximum(owner, 0)
        pieces.append(jnp.where(own_core(owner), gather4[chip_of(owner)], relay_in4[slot]))
    fine.start_up(pieces, spread_ref[...])
    fine.up()

    def fine_out(i):
        fine.full[pl.ds(2 * CH * i, 2 * CH)] = fine.finished(CH * i)

    each(fine.rows // CH, fine_out)
    for box in range(2):
        for s in range(8):
            part = fine.full[pl.ds(box * 256 + s, 32, stride=8)]
            out_f[box, :, 128 * s : 128 * s + 128] = jnp.where(owners[box] >= 0, part, 0.0)
    store_f = store(2, out_f, far_out_f.at[0, 0])

    wait_all(gather1, send_sems.at[0], SAME_CORE)
    wait_all(gather2, send_sems.at[1], PEERS)
    wait_all(gather3, send_sems.at[2], SAME_CORE)
    wait_all(gather4, send_sems.at[3], SAME_CORE)
    for n, buffer in enumerate((relay_out1, relay_out3, relay_out4)):
        wait_one(buffer, relay_send.at[n])
    for turn in (0, 1):
        wait_one(rim_in.at[turn], rim_send.at[turn])
    for copy in (store_c, store_m, store_f):
        copy.wait()


def level_scratch(count):
    rows = count * 128
    return [
        pltpu.VMEM((2 * rows, 128), F32),
        pltpu.VMEM((rows + 16, 128), F32),
        pltpu.VMEM((rows + 16, 128), F32),
        pltpu.VMEM((2, 6, rows, 128), F32),
        pltpu.VMEM((2, rows, 128), F32),
        pltpu.VMEM((2, rows, 128), F32),
        pltpu.VMEM((2, rows, 128), F32),
        pltpu.VMEM((rows, 128), F32),
        pltpu.VMEM((rows, 128), F32),
    ]


def write_out(*refs):
    sources, targets, sems = refs[:3], refs[3:6], refs[6]
    copies = [pltpu.make_async_copy(*pair, sems.at[n]) for n, pair in enumerate(zip(sources, targets))]
    for copy in copies:
        copy.start()
    for copy in copies:
        copy.wait()


def on_device(*args):
    fields, (parent_m, offset_m, parent_f, offset_f) = args[:6], args[6:]
    tables = (
        jnp.transpose(parent_m),
        jnp.transpose(offset_m, (2, 1, 0)),
        jnp.transpose(parent_f, (1, 2, 0)),
        jnp.transpose(offset_f, (1, 3, 2, 0)),
    )
    shapes = [args[0].shape, args[2].shape, args[4].shape]
    out_shape = [jax.ShapeDtypeStruct(shape, F32) for shape in shapes]
    vmem = pl.BlockSpec(memory_space=pltpu.VMEM)
    anywhere = pl.BlockSpec(memory_space=pl.ANY)
    call = pl.pallas_call(
        kernel,
        out_shape=out_shape,
        in_specs=[pl.BlockSpec(memory_space=pltpu.HBM)] * 10,
        out_specs=[anywhere] * 3,
        scratch_shapes=[
            *[pltpu.VMEM(shape, F32) for shape in ((32, 32, 128),) * 2 + ((32, 1024),) * 2 + ((2, 32, 1024),) * 2],
            *[pltpu.SMEM(shape, jnp.int32) for shape in (tables[0].shape, tables[1].shape, (2, 16), (3, 2, 16))],
            pltpu.VMEM((32, 1024), F32),
            pltpu.VMEM((2, 32, 1024), F32),
            pltpu.VMEM((8, 2, 32, 128), F32),
            pltpu.VMEM((16, 32, 128), F32),
            pltpu.VMEM((8, 56, 128), F32),
            pltpu.VMEM((8, 56, 128), F32),
            pltpu.VMEM((32, 128), F32),
            pltpu.VMEM((32, 128), F32),
            pltpu.VMEM((56, 128), F32),
            pltpu.VMEM((56, 128), F32),
            pltpu.VMEM((2, 56, 128), F32),
            pltpu.VMEM((2, 56, 128), F32),
            pltpu.VMEM((2, 512, 128), F32),
            pltpu.VMEM((2, 576, 128), F32),
            pltpu.VMEM((512, 128), BF16),
            pltpu.VMEM((256, 256), BF16),
            pltpu.VMEM((256, 1024), BF16),
            pltpu.VMEM((256, 1024), BF16),
            pltpu.VMEM((1024, 384), BF16),
            pltpu.VMEM((1024, 384), BF16),
            pltpu.VMEM((128, 128), F32),
            pltpu.VMEM((512, 128), F32),
            pltpu.VMEM((48, 8, 128), F32),
            pltpu.VMEM((48, 32, 128), F32),
            pltpu.VMEM((33, 8, 128), F32),
            pltpu.VMEM((33, 32, 128), F32),
            pltpu.VMEM((256, 128), F32),
            pltpu.VMEM((24 * 32, 128), F32),
            pltpu.VMEM((2, WIDE, 128), F32),
            pltpu.VMEM((2, WIDE, 128), F32),
            pltpu.VMEM((2, WIDE, 128), F32),
            pltpu.VMEM((2, 6, PAIRS * ROWS, 128), F32),
            pltpu.VMEM((2, PAIRS * ROWS, 128), F32),
            *level_scratch(2),
            *level_scratch(1),
            pltpu.SemaphoreType.DMA((4,)),
            pltpu.SemaphoreType.DMA((4,)),
            pltpu.SemaphoreType.DMA((3,)),
            pltpu.SemaphoreType.DMA((3,)),
            pltpu.SemaphoreType.DMA((2,)),
            pltpu.SemaphoreType.DMA((6,)),
            pltpu.SemaphoreType.DMA((10,)),
            pltpu.SemaphoreType.DMA((3,)),
        ],
        compiler_params=pltpu.CompilerParams(
            collective_id=0, has_side_effects=True, vmem_limit_bytes=60 * 2**20
        ),
        name="v_cycle",
    )
    write = pl.pallas_call(
        write_out,
        out_shape=out_shape,
        in_specs=[vmem] * 3,
        out_specs=[anywhere] * 3,
        scratch_shapes=[pltpu.SemaphoreType.DMA((3,))],
        name="write_out",
    )
    return tuple(write(*call(*fields, *tables)))


def solution(mesh):
    return jax.shard_map(
        on_device,
        mesh=mesh,
        in_specs=(
            P("xb", "yb", None),
            P("xb", "yb", None),
            P("xb", "yb", None, None),
            P("xb", "yb", None, None),
            P("xb", "yb", None, None, None),
            P("xb", "yb", None, None, None),
            P(),
            P(),
            P(),
            P(),
        ),
        out_specs=(P("xb", "yb", None), P("xb", "yb", None, None), P("xb", "yb", None, None, None)),
        check_vma=False,
    )
```

```python
import functools

import jax
import jax.numpy as jnp
from jax import lax
from jax.experimental import pallas as pl
from jax.experimental.pallas import tpu as pltpu
from jax.sharding import PartitionSpec as P

MESH = pl.DeviceIdType.MESH
F32 = jnp.float32
BF16 = jnp.bfloat16
CH = 64
PAIRS = 20
ROWS = 48
EDGE = 56
WIDE = 2 * EDGE + PAIRS * ROWS
CHIPS = ((2, 1), (1, 1), (3, 1), (2, 0), (0, 1), (1, 0), (3, 0))
SAME_CORE = [(dx, dh, 0) for dx, dh in CHIPS]
PEERS = [(dx, dh, dc) for dx, dh in CHIPS for dc in (0, 1)] + [(0, 0, 1)]


def iota(shape, dim):
    return lax.broadcasted_iota(jnp.int32, shape, dim)


def each(count, body, unroll=True):
    def step(i, carry):
        body(i)
        return carry

    lax.fori_loop(0, count, step, 0, unroll=unroll)


def chosen_dot(values, choice):
    rows = values.shape[0]
    high = values.astype(BF16).astype(F32)
    rest = values - high
    middle = rest.astype(BF16).astype(F32)
    terms = jnp.concatenate([high, middle, rest - middle], axis=0).astype(BF16)
    out = lax.dot_general(terms, choice, (((1,), (0,)), ((), ())), preferred_element_type=F32)
    return out[:rows] + out[rows : 2 * rows] + out[2 * rows :]


def onehot(mask, value=1.0):
    return jnp.where(mask, value, 0.0).astype(BF16)


class Level:
    def __init__(self, count, scale, refs):
        self.count, self.scale, self.rows = count, scale, count * 128
        (self.full, self.red, self.black, self.coef, self.g, self.inv, self.hb, self.tot, self.rest) = refs

    def field(self, colour):
        return self.black if colour else self.red

    def near(self, colour, at):
        ref = self.field(1 - colour)
        lane = iota((CH, 128), 1)
        odd = (lane // 32 + lane) % 2 == 1
        own = ref[pl.ds(8 + at, CH)]
        above, below = ref[pl.ds(16 + at, CH)], ref[pl.ds(at, CH)]
        after, before = ref[pl.ds(9 + at, CH)], ref[pl.ds(7 + at, CH)]
        other = jnp.where(odd, below, above) if colour else jnp.where(odd, above, below)
        return (
            own,
            other,
            pltpu.roll(jnp.where(lane >= 32, own, after), 96, 1),
            pltpu.roll(jnp.where(lane < 96, own, before), 32, 1),
            pltpu.roll(own, 127, 1),
            pltpu.roll(own, 1, 1),
        )

    def clear_ends(self):
        for ref in (self.red, self.black):
            ref[pl.ds(0, 8)] = jnp.zeros((8, 128), F32)
            ref[pl.ds(8 + self.rows, 8)] = jnp.zeros((8, 128), F32)

    def unfold(self, load):
        for box in range(self.count):
            for s in range(8):
                self.full[pl.ds(box * 256 + s, 32, stride=8)] = load(box, s)

    def packed(self, full, at):
        lane = iota((CH, 128), 1)
        odd = (lane // 32 + lane) % 2 == 1
        planes = full.reshape(CH // 8, 2, 8, 128)
        low, high = planes[:, 0].reshape(CH, 128), planes[:, 1].reshape(CH, 128)
        return jnp.where(odd, high, low), jnp.where(odd, low, high)

    def set_fields(self):
        def body(i):
            at = i * CH
            red, black = self.packed(self.full[pl.ds(2 * at, 2 * CH)], at)
            self.red[pl.ds(8 + at, CH)] = red
            self.black[pl.ds(8 + at, CH)] = black

        each(self.rows // CH, body)

    def set_weights(self):
        def body(i):
            at = i * CH
            lane, row = iota((CH, 128), 1), iota((CH, 128), 0)
            odd = (lane // 32 + lane) % 2 == 1
            s = row % 8
            pair = ((at + row) // 8) % 16
            z = lane % 32
            inside_y = (jnp.logical_not((s == 7) & (lane >= 96)), jnp.logical_not((s == 0) & (lane < 32)))
            inside_z = (z < 31, z > 0)
            for colour in (0, 1):
                first, last = (odd, jnp.logical_not(odd)) if colour else (jnp.logical_not(odd), odd)
                edge = (first & (pair == 0)) | (last & (pair == 15))
                masks = (None, jnp.logical_not(edge)) + inside_y + inside_z
                own = self.field(colour)[pl.ds(8 + at, CH)]
                near = self.near(colour, at)
                faces = [
                    0.5 * (own + (other if mask is None else jnp.where(mask, other, 0.0)))
                    for other, mask in zip(near, masks)
                ]
                total = faces[0] + faces[1] + faces[2] + faces[3] + faces[4] + faces[5]
                inv = 1.0 / total
                for n in range(6):
                    part = faces[n] * inv
                    self.coef[colour, n, pl.ds(at, CH)] = (
                        part if masks[n] is None else jnp.where(masks[n], part, 0.0)
                    )
                self.inv[colour, pl.ds(at, CH)] = inv * (1.0 / self.scale)
                self.hb[colour, pl.ds(at, CH)] = 0.5 * own * inv
                if colour == 0:
                    self.tot[pl.ds(at, CH)] = self.scale * total

        each(self.rows // CH, body)

    def set_target(self, at, red, black):
        for colour, value in ((0, red), (1, black)):
            self.g[colour, pl.ds(at, CH)] = value * self.inv[colour, pl.ds(at, CH)]

    def fresh(self, colour, at):
        near = self.near(colour, at)
        out = self.g[colour, pl.ds(at, CH)]
        for n in range(6):
            out = out + self.coef[colour, n, pl.ds(at, CH)] * near[n]
        return out

    def half_sweep(self, colour):
        def body(i):
            at = i * CH
            self.field(colour)[pl.ds(8 + at, CH)] = self.fresh(colour, at)

        each(self.rows // CH, body)

    def down(self):
        def first(i):
            at = i * CH
            self.red[pl.ds(8 + at, CH)] = self.g[0, pl.ds(at, CH)]

        each(self.rows // CH, first)
        self.half_sweep(1)
        self.half_sweep(0)
        self.half_sweep(1)

        def left(i):
            at = i * CH
            self.rest[pl.ds(at, CH)] = self.tot[pl.ds(at, CH)] * (
                self.fresh(0, at) - self.red[pl.ds(8 + at, CH)]
            )

        each(self.rows // CH, left)

    def restricted(self, mean):
        parts = []
        for box in range(self.count):
            for h in range(2):
                parts.append(
                    jnp.concatenate(
                        [self.rest[pl.ds(box * 128 + 4 * h + j, 16, stride=8)] for j in range(4)], axis=1
                    )
                )
        return chosen_dot(jnp.concatenate(parts, axis=0), mean)

    def start_up(self, pieces, spread):
        sub, lane = iota((8, 128), 0), iota((8, 128), 1)
        odd = (lane // 32 + lane) % 2 == 1
        even = jnp.logical_not(odd)
        rows_of = lane // 32 == sub % 4
        rows_of_face = (
            ((lane < 16) & (sub == 0))
            | ((lane >= 16) & (lane < 32) & (sub == 7))
            | ((lane >= 32) & (lane < 64) & ((lane % 16) // 2 == sub))
        )

        def tiles(rows):
            return jnp.broadcast_to(rows[:, None, :], (rows.shape[0], 8, 128))

        def halves(first, second):
            return jnp.where((sub < 4)[None], tiles(first), tiles(second))

        for box, piece in enumerate(pieces):
            core = jnp.concatenate(
                [
                    halves(piece[0:16], piece[16:32]),
                    halves(piece[48:49], piece[49:50]),
                    halves(piece[50:51], piece[51:52]),
                ],
                axis=0,
            )
            core = jnp.where(rows_of[None], core, 0.0).reshape(144, 128)
            face = jnp.where(rows_of_face[None], tiles(piece[32:48]), 0.0).reshape(128, 128)
            face = jnp.concatenate([face, jnp.zeros((16, 128), F32)], axis=0)
            grown = chosen_dot(jnp.concatenate([core, face], axis=1), spread)
            inner, border = grown[:128, :128], grown[:128, 128:].reshape(16, 8, 128)
            low, high = grown[128:136, :128], grown[136:144, :128]
            at = box * 128
            self.black[pl.ds(8 + at, 128)] = self.black[pl.ds(8 + at, 128)] + inner
            for colour in (0, 1):
                first, last = (odd, even) if colour else (even, odd)
                ghost = jnp.concatenate(
                    [
                        border[:1] + jnp.where(first, low, 0.0)[None],
                        border[1:15],
                        border[15:] + jnp.where(last, high, 0.0)[None],
                    ],
                    axis=0,
                ).reshape(128, 128)
                self.g[colour, pl.ds(at, 128)] = (
                    self.g[colour, pl.ds(at, 128)] + self.hb[colour, pl.ds(at, 128)] * ghost
                )

    def up(self):
        for colour in (0, 1, 0, 1):
            self.half_sweep(colour)

    def finished(self, at):
        lane = iota((CH, 128), 1)
        odd = (lane // 32 + lane) % 2 == 1
        red, black = self.red[pl.ds(8 + at, CH)], self.black[pl.ds(8 + at, CH)]
        low = jnp.where(odd, black, red).reshape(CH // 8, 1, 8, 128)
        high = jnp.where(odd, red, black).reshape(CH // 8, 1, 8, 128)
        return jnp.concatenate([low, high], axis=1).reshape(2 * CH, 128)


def spread_choice():
    l, n = iota((256, 256), 0), iota((256, 256), 1)
    z, q = n % 32, (n % 128) // 32
    inner = (l < 128) & (n < 128) & ((l // 16) % 2 == q // 2) & (l % 16 == z // 2)
    f = l - 128
    along_y = (f >= 0) & (f < 32) & (q == jnp.where(f < 16, 0, 3)) & (z // 2 == f % 16)
    along_z = (f >= 32) & (f < 64) & (q // 2 == f % 2) & (z == jnp.where(f < 48, 0, 31))
    return onehot(inner | ((n >= 128) & (along_y | along_z)))


def mean_choice():
    k, n = iota((512, 128), 0), iota((512, 128), 1)
    lane = k % 128
    return onehot(n == 32 * (k // 128) + 16 * (lane // 64) + (lane % 32) // 2, 0.125)


def place_choice(corner):
    k, n = iota((256, 1024), 0), iota((256, 1024), 1)
    return onehot(n == (k // 16) * 32 + k % 16 + corner[1] * 32 + corner[2])


def window_choice(corner):
    n = iota((1, 384), 1)
    i = n % 16
    source = jnp.where(n < 256, (n // 16) * 32 + i, -4096)
    source = jnp.where((n >= 256) & (n < 272), i - 32, source)
    source = jnp.where((n >= 272) & (n < 288), i + 512, source)
    source = jnp.where((n >= 288) & (n < 304), i * 32 - 1, source)
    source = jnp.where((n >= 304) & (n < 320), i * 32 + 16, source)
    return onehot(iota((1024, 384), 0) == source + corner[1] * 32 + corner[2])


def placed_lhs(piece):
    return jnp.concatenate([piece[0:16], piece[16:32]], axis=1)


def kernel(
    far_rhs_c, far_beta_c, far_rhs_m, far_beta_m, far_rhs_f, far_beta_f,
    far_parent_m, far_offset_m, far_parent_f, far_offset_f,
    out_c, out_m, out_f,
    rhs_c, beta_c, rhs_m, beta_m, rhs_f, beta_f, parent_m, offset_m, parent_f, offset_f,
    gather1, gather2, gather3, gather4, relay_out1, relay_in1, relay_out3, relay_in3, relay_out4, relay_in4,
    rim_out, rim_in,
    mean_ref, spread_ref, place_m, place_c, window_m, window_c,
    put_m, put_c, pad_m, pad_c, wide_m, wide_c, cut_m, cut_c,
    beta_e, g_e, field_e, coef_e, inv_e,
    *rest,
):
    fine_refs, mid_refs = rest[:9], rest[9:18]
    send_sems, recv_sems, relay_send, relay_recv, rim_send, rim_recv, load_sems, store_sem = rest[18:]
    fine = Level(2, 1.0, fine_refs)
    mid = Level(1, 0.25, mid_refs)
    n_x, n_y = lax.axis_size("xb"), lax.axis_size("yb")
    row, col = lax.axis_index("xb"), lax.axis_index("yb")

    def load(n, source, target):
        copy = pltpu.make_async_copy(source, target, load_sems.at[n])
        copy.start()
        return copy

    load_beta_c = load(3, far_beta_c, beta_c)
    load_beta_f = load(0, far_beta_f.at[0, 0], beta_f)
    load_rhs_f = load(1, far_rhs_f.at[0, 0], rhs_f)
    load_beta_m = load(2, far_beta_m.at[0, 0], beta_m)
    load_rhs_m = load(4, far_rhs_m.at[0, 0], rhs_m)
    load_rhs_c = load(5, far_rhs_c, rhs_c)
    load_tables = (
        load(6, far_parent_m, parent_m),
        load(7, far_offset_m, offset_m),
        load(8, far_parent_f.at[col], parent_f),
        load(9, far_offset_f.at[col], offset_f),
    )

    def beside(dx, dy):
        return (lax.rem(row + dx + n_x, n_x), lax.rem(col + dy + n_y, n_y))

    def peer(dx, dh, dc):
        x, h, c = row // 4, (row // 2) % 2, row % 2
        return (((x + dx) % 4) * 4 + ((h + dh) % 2) * 2 + (c + dc) % 2, col)

    barrier = pltpu.get_barrier_semaphore()
    greeted = [peer(*hop) for hop in PEERS] + [beside(dx, dy) for dx in (-1, 0, 1) for dy in (-1, 1)]
    for device in greeted:
        pl.semaphore_signal(barrier, inc=1, device_id=device, device_id_type=MESH)

    twin = row + 1 - 2 * (row % 2)
    chip = row // 2

    def send_all(buffer, stage, place, hops):
        for hop in hops:
            pltpu.make_async_remote_copy(
                src_ref=buffer.at[place],
                dst_ref=buffer.at[place],
                send_sem=send_sems.at[stage],
                recv_sem=recv_sems.at[stage],
                device_id=peer(*hop),
                device_id_type=MESH,
            ).start()

    def wait_all(buffer, sem, hops):
        whole = buffer.at[pl.ds(0, len(hops))]
        pltpu.make_async_copy(whole, whole, sem).wait()

    def wait_one(buffer, sem):
        pltpu.make_async_copy(buffer, buffer, sem).wait()

    def relay(n, source, target):
        pltpu.make_async_remote_copy(
            src_ref=source,
            dst_ref=target,
            send_sem=relay_send.at[n],
            recv_sem=relay_recv.at[n],
            device_id=(twin, col),
            device_id_type=MESH,
        ).start()

    def own_core(device):
        return lax.rem(device, 2) == row % 2

    def chip_of(device):
        return lax.div(device, 2)

    def send_rim(turn):
        def copy(kind, source, size, target, device):
            pltpu.make_async_remote_copy(
                src_ref=rim_out.at[turn, pl.ds(source, size)],
                dst_ref=rim_in.at[turn, pl.ds(target, size)],
                send_sem=rim_send.at[turn],
                recv_sem=rim_recv.at[3 * turn + kind],
                device_id=device,
                device_id_type=MESH,
            ).start()

        for side_x in (0, 1):
            for side_y in (0, 1):
                copy(
                    2, 256 + 128 * side_y + 112 * side_x, 16,
                    512 + 16 * (2 * (1 - side_x) + 1 - side_y),
                    beside(2 * side_x - 1, 2 * side_y - 1),
                )
        for side in (0, 1):
            copy(1, 256 + 128 * side, 128, 256 + 128 * (1 - side), beside(0, 2 * side - 1))
        for side in (0, 1):
            copy(0, 128 * side, 128, 128 * (1 - side), beside(2 * side - 1, 0))

    def wait_rim(turn, kind):
        wait_one(rim_in.at[turn, pl.ds(256 * kind, (256, 256, 64)[kind])], rim_recv.at[3 * turn + kind])

    def fill_rim(turn, ref):
        tile_row = iota((8, 128), 0)
        for side in (0, 1):
            for colour in (0, 1):
                for d in (0, 1):
                    at = EDGE + ((2, 16)[side] + d) * ROWS + 8
                    rim_out[turn, pl.ds(128 * side + (2 * colour + d) * 32, 32)] = ref[colour, pl.ds(at, 32)]

        def body(k):
            at = EDGE + (k + 2) * ROWS
            red, black = ref[0, pl.ds(at + 8, 8)], ref[1, pl.ds(at + 8, 8)]
            rim_out[turn, pl.ds(256 + k * 8, 8)] = jnp.where(tile_row < 4, red, pltpu.roll(black, 4, 0))
            red, black = ref[0, pl.ds(at + 32, 8)], ref[1, pl.ds(at + 32, 8)]
            rim_out[turn, pl.ds(384 + k * 8, 8)] = jnp.where(tile_row < 4, pltpu.roll(black, 4, 0), red)

        each(16, body)

    def keep(value, *sides):
        for side in sides:
            if side is not None:
                value = jnp.where(side, value, 0.0)
        return value

    def take_y(turn, ref, inside_y):
        def body(k):
            for side in (0, 1):
                at = EDGE + (k + 2) * ROWS + 40 * side
                part = keep(rim_in[turn, pl.ds(256 + 128 * side + 8 * k, 8)], inside_y[side])
                ref[0, pl.ds(at, 8)] = part
                ref[1, pl.ds(at, 8)] = pltpu.roll(part, 4, 0)

        each(16, body)

    def take_x(turn, ref, inside_x, inside_y):
        for side in (0, 1):
            for colour in (0, 1):
                for d in (0, 1):
                    at = EDGE + ((0, 18)[side] + d) * ROWS + 8
                    part = rim_in[turn, pl.ds(128 * side + (2 * colour + d) * 32, 32)]
                    ref[colour, pl.ds(at, 32)] = keep(part, inside_x[side])
            for other in (0, 1):
                for d in (0, 1):
                    at = EDGE + (18 * side + d) * ROWS + 40 * other
                    part = rim_in[turn, pl.ds(512 + 16 * (2 * side + other) + 8 * d, 8)]
                    part = keep(part, inside_x[side], inside_y[other])
                    ref[0, pl.ds(at, 8)] = part
                    ref[1, pl.ds(at, 8)] = pltpu.roll(part, 4, 0)

    mean_ref[...] = mean_choice()
    fine.clear_ends()

    def own_beta(k):
        lane, line = iota((32, 128), 1), iota((32, 128), 0)
        odd = (line + lane) % 2 == 1
        low, high = beta_c[2 * k], beta_c[2 * k + 1]
        at = EDGE + (k + 2) * ROWS + 8
        beta_e[0, pl.ds(at, 32)] = jnp.where(odd, high, low)
        beta_e[1, pl.ds(at, 32)] = jnp.where(odd, low, high)

    for colour in (0, 1):
        beta_e[colour, pl.ds(0, EDGE)] = jnp.zeros((EDGE, 128), F32)
        beta_e[colour, pl.ds(WIDE - EDGE, EDGE)] = jnp.zeros((EDGE, 128), F32)
    load_beta_c.wait()
    each(16, own_beta)
    fill_rim(0, beta_e)
    load_beta_f.wait()
    fine.unfold(lambda box, s: beta_f[box, :, 128 * s : 128 * s + 128])
    fine.set_fields()
    fine.set_weights()
    load_rhs_f.wait()
    fine.unfold(lambda box, s: rhs_f[box, :, 128 * s : 128 * s + 128])

    def fine_target(i):
        at = i * CH
        fine.set_target(at, *fine.packed(fine.full[pl.ds(2 * at, 2 * CH)], at))

    each(fine.rows // CH, fine_target)
    pl.semaphore_wait(barrier, len(greeted))
    send_rim(0)
    fine.down()
    gather1[chip] = fine.restricted(mean_ref[...]).reshape(2, 32, 128)
    send_all(gather1, 0, chip, SAME_CORE)

    mid.clear_ends()
    load_beta_m.wait()
    mid.unfold(lambda box, s: beta_m[:, 128 * s : 128 * s + 128])
    mid.set_fields()
    mid.set_weights()
    load_rhs_m.wait()
    mid.unfold(lambda box, s: rhs_m[:, 128 * s : 128 * s + 128])

    for copy in load_tables:
        copy.wait()

    def find_fine(i, carry):
        index, place, x, y, z, twin_index, twin_place = carry
        for slot in range(2):
            twin_hit = parent_f[slot, i] == twin
            twin_index = jnp.where(twin_hit, i, twin_index)
            twin_place = jnp.where(twin_hit, slot, twin_place)
            hit = parent_f[slot, i] == row
            index = jnp.where(hit, i, index)
            place = jnp.where(hit, slot, place)
            x = jnp.where(hit, offset_f[0, slot, i], x)
            y = jnp.where(hit, offset_f[1, slot, i], y)
            z = jnp.where(hit, offset_f[2, slot, i], z)
        return index, place, x, y, z, twin_index, twin_place

    def find_mid(i, carry):
        index, x, y, z = carry
        hit = parent_m[col, i] == row
        return (
            jnp.where(hit, i, index),
            jnp.where(hit, offset_m[0, col, i], x),
            jnp.where(hit, offset_m[1, col, i], y),
            jnp.where(hit, offset_m[2, col, i], z),
        )

    zero, one = jnp.int32(0), jnp.int32(1)
    child, child_slot, *corner_m, twin_child, twin_slot = lax.fori_loop(
        0, 16, find_fine, (zero, zero, one, one, one, zero, zero)
    )
    guest, *corner_c = lax.fori_loop(0, 16, find_mid, (zero, one, one, one))
    place_m[...] = place_choice(corner_m)
    pad_m[0:16] = jnp.zeros((16, 8, 128), F32)
    pad_m[32:48] = jnp.zeros((16, 8, 128), F32)

    wait_all(gather1, recv_sems.at[0], SAME_CORE)
    relay_out1[...] = gather1[chip_of(twin_child), twin_slot]
    relay(0, relay_out1, relay_in1)
    wait_one(relay_in1, relay_recv.at[0])

    piece = jnp.where(own_core(child), gather1[chip_of(child), child_slot], relay_in1[...])
    put = chosen_dot(placed_lhs(piece), place_m[...])
    for s in range(8):
        put_m[pl.ds(s, 16, stride=8)] = put[:, 128 * s : 128 * s + 128]
    pad_m[16:32] = put_m[...].reshape(16, 8, 128)

    def shift_m(x):
        cut_m[pl.ds(8 * x, 8)] = pad_m[16 - corner_m[0] + x]

    each(32, shift_m)

    def mid_target(i):
        lane, line = iota((2 * CH, 128), 1), iota((2 * CH, 128), 0)
        x = i * (CH // 4) + line // 8 - corner_m[0]
        y = (line % 8) * 4 + lane // 32 - corner_m[1]
        z = lane % 32 - corner_m[2]
        hit = (x >= 0) & (x < 16) & (y >= 0) & (y < 16) & (z >= 0) & (z < 16)
        full = jnp.where(hit, cut_m[pl.ds(2 * CH * i, 2 * CH)], mid.full[pl.ds(2 * CH * i, 2 * CH)])
        mid.set_target(i * CH, *mid.packed(full, i * CH))

    each(mid.rows // CH, mid_target)
    mid.down()
    gather2[row] = mid.restricted(mean_ref[...])
    send_all(gather2, 1, row, PEERS)

    place_c[...] = place_choice(corner_c)
    pad_c[0:16] = jnp.zeros((16, 32, 128), F32)
    pad_c[32:48] = jnp.zeros((16, 32, 128), F32)
    for kind in (0, 1, 2):
        wait_rim(0, kind)
    inside_x, inside_y = (row > 0, row < n_x - 1), (col > 0, col < n_y - 1)
    take_y(0, beta_e, inside_y)
    take_x(0, beta_e, inside_x, inside_y)

    def near_wide(ref, colour, at, rows):
        lane, line = iota((rows, 128), 1), iota((rows, 128), 0)
        odd = (line + lane) % 2 == 1
        own = ref[1 - colour, pl.ds(at, rows)]
        above, below = ref[1 - colour, pl.ds(at + ROWS, rows)], ref[1 - colour, pl.ds(at - ROWS, rows)]
        other = jnp.where(odd, below, above) if colour else jnp.where(odd, above, below)
        after, before = ref[1 - colour, pl.ds(at + 1, rows)], ref[1 - colour, pl.ds(at - 1, rows)]
        return own, other, after, before, pltpu.roll(own, 127, 1), pltpu.roll(own, 1, 1)

    def coarse_weights(k):
        lane = iota((ROWS, 128), 1)
        masks = (None, None, None, None, lane < 127, lane > 0)
        at = EDGE + k * ROWS
        for colour in (0, 1):
            own = beta_e[colour, pl.ds(at, ROWS)]
            near = near_wide(beta_e, colour, at, ROWS)
            faces = [
                0.5 * (own + (other if mask is None else jnp.where(mask, other, 0.0)))
                for other, mask in zip(near, masks)
            ]
            total = faces[0] + faces[1] + faces[2] + faces[3] + faces[4] + faces[5]
            real = own > 0.0
            inv = jnp.where(real, 1.0 / total, 0.0)
            for n in range(6):
                keep = real if masks[n] is None else real & masks[n]
                coef_e[colour, n, pl.ds(k * ROWS, ROWS)] = jnp.where(keep, faces[n] * inv, 0.0)
            inv_e[colour, pl.ds(k * ROWS, ROWS)] = 16.0 * inv

    each(PAIRS, coarse_weights, 4)
    window_c[...] = window_choice(corner_c)
    wait_all(gather2, recv_sems.at[1], PEERS)

    put = chosen_dot(placed_lhs(gather2[guest]), place_c[...])
    for s in range(8):
        part = put[:, 128 * s : 128 * s + 128]
        for q in range(4):
            put_c[pl.ds(4 * s + q, 16, stride=32)] = part if q == 0 else pltpu.roll(part, 128 - 32 * q, 1)

    pad_c[16:32] = put_c[...].reshape(16, 32, 128)

    load_rhs_c.wait()

    def coarse_target(k):
        lane, line = iota((32, 128), 1), iota((32, 128), 0)
        odd = (line + lane) % 2 == 1
        y, z = line - corner_c[1], lane - corner_c[2]
        hit = (y >= 0) & (y < 16) & (z >= 0) & (z < 16)
        planes = []
        for d in (0, 1):
            x = 2 * k + d - corner_c[0]
            planes.append(jnp.where(hit & (x >= 0) & (x < 16), pad_c[16 + x], rhs_c[2 * k + d]))
        at = EDGE + (k + 2) * ROWS + 8
        g_e[0, pl.ds(at, 32)] = jnp.where(odd, planes[1], planes[0])
        g_e[1, pl.ds(at, 32)] = jnp.where(odd, planes[0], planes[1])

    each(16, coarse_target)
    fill_rim(1, g_e)
    send_rim(1)

    def coarse_first(first, count, line, rows):
        def body(i):
            at, here = EDGE + (first + i) * ROWS + line, (first + i) * ROWS + line
            field_e[0, pl.ds(at, rows)] = g_e[0, pl.ds(at, rows)] * inv_e[0, pl.ds(here, rows)]

        each(count, body)

    def coarse_sweep(colour, first, count, line=0, rows=ROWS):
        def body(i):
            k = first + i
            at, here = EDGE + k * ROWS + line, k * ROWS + line
            near = near_wide(field_e, colour, at, rows)
            out = g_e[colour, pl.ds(at, rows)] * inv_e[colour, pl.ds(here, rows)]
            for n in range(6):
                out = out + coef_e[colour, n, pl.ds(here, rows)] * near[n]
            field_e[colour, pl.ds(at, rows)] = out

        each(count, body)

    coarse_first(2, 16, 8, 32)
    wait_rim(1, 1)
    take_y(1, g_e, (None, None))
    coarse_first(2, 16, 0, 8)
    coarse_first(2, 16, 40, 8)
    coarse_sweep(1, 3, 14)
    coarse_sweep(0, 4, 12)
    coarse_sweep(1, 5, 10, 8, 32)
    wait_rim(1, 0)
    wait_rim(1, 2)
    take_x(1, g_e, (None, None), (None, None))
    for first in (0, 18):
        coarse_first(first, 2, 0, ROWS)
    for first in (1, 17):
        coarse_sweep(1, first, 2)
    for first in (1, 16):
        coarse_sweep(0, first, 3)
    for first in (2, 15):
        coarse_sweep(1, first, 3, 8, 32)

    def coarse_out(k):
        lane, line = iota((32, 128), 1), iota((32, 128), 0)
        odd = (line + lane) % 2 == 1
        at = EDGE + (k + 2) * ROWS + 8
        red, black = field_e[0, pl.ds(at, 32)], field_e[1, pl.ds(at, 32)]
        low, high = jnp.where(odd, black, red), jnp.where(odd, red, black)
        wide_c[1 + 2 * k] = low
        wide_c[2 + 2 * k] = high

    each(16, coarse_out)

    def post_window(buffer, stage, lhs, choice):
        got = chosen_dot(lhs, choice)
        for n in range(3):
            buffer[chip, pl.ds(16 * n, 16)] = got[1:17, 128 * n : 128 * n + 128]
        for n, (x, h) in enumerate(((0, 0), (0, 1), (17, 0), (17, 1))):
            buffer[chip, pl.ds(48 + n, 1)] = got[x : x + 1, 128 * h : 128 * h + 128]
        send_all(buffer, stage, chip, SAME_CORE)

    def cut_window_c(x):
        cut_c[pl.ds(32 * x, 32)] = wide_c[corner_c[0] + x]

    each(18, cut_window_c)
    lane24 = iota((24, 128), 1)
    blocks = []
    for s in range(8):
        block = None
        for q in range(4):
            part = cut_c[pl.ds(4 * s + q, 24, stride=32)]
            if q == 0:
                block = part
            else:
                block = jnp.where(lane24 // 32 == q, pltpu.roll(part, 32 * q, 1), block)
        blocks.append(block)
    post_window(gather3, 2, jnp.concatenate(blocks, axis=1), window_c[...])
    store_c = pltpu.make_async_copy(wide_c.at[pl.ds(1, 32)], out_c, store_sem)
    store_c.start()
    spread_ref[...] = spread_choice()
    window_m[...] = window_choice(corner_m)
    wait_all(gather3, recv_sems.at[2], SAME_CORE)
    relay_out3[...] = gather3[chip_of(parent_m[col, twin])]
    relay(1, relay_out3, relay_in3)
    wait_one(relay_in3, relay_recv.at[1])

    owner_m = parent_m[col, row]
    piece = jnp.where(own_core(owner_m), gather3[chip_of(owner_m)], relay_in3[...])
    mid.start_up([piece], spread_ref[...])
    mid.up()

    def mid_out(i):
        full = mid.finished(CH * i)
        mid.full[pl.ds(2 * CH * i, 2 * CH)] = full
        wide_m[pl.ds(1 + CH // 4 * i, CH // 4)] = full.reshape(CH // 4, 8, 128)

    each(mid.rows // CH, mid_out)

    def cut_window_m(x):
        cut_m[pl.ds(8 * x, 8)] = wide_m[corner_m[0] + x]

    each(18, cut_window_m)
    lhs = jnp.concatenate([cut_m[pl.ds(s, 24, stride=8)] for s in range(8)], axis=1)
    post_window(gather4, 3, lhs, window_m[...])
    for s in range(8):
        out_m[0, 0, :, 128 * s : 128 * s + 128] = mid.full[pl.ds(s, 32, stride=8)]
    wait_all(gather4, recv_sems.at[3], SAME_CORE)
    for slot in range(2):
        relay_out4[slot] = gather4[chip_of(jnp.maximum(parent_f[slot, twin], 0))]
    relay(2, relay_out4, relay_in4)
    wait_one(relay_in4, relay_recv.at[2])

    owners = [parent_f[slot, row] for slot in range(2)]
    pieces = []
    for slot, owner in enumerate(owners):
        owner = jnp.maximum(owner, 0)
        pieces.append(jnp.where(own_core(owner), gather4[chip_of(owner)], relay_in4[slot]))
    fine.start_up(pieces, spread_ref[...])
    fine.up()

    def fine_out(i):
        fine.full[pl.ds(2 * CH * i, 2 * CH)] = fine.finished(CH * i)

    each(fine.rows // CH, fine_out)
    for box in range(2):
        for s in range(8):
            part = fine.full[pl.ds(box * 256 + s, 32, stride=8)]
            out_f[0, 0, box, :, 128 * s : 128 * s + 128] = jnp.where(owners[box] >= 0, part, 0.0)

    wait_all(gather1, send_sems.at[0], SAME_CORE)
    wait_all(gather2, send_sems.at[1], PEERS)
    wait_all(gather3, send_sems.at[2], SAME_CORE)
    wait_all(gather4, send_sems.at[3], SAME_CORE)
    for n, buffer in enumerate((relay_out1, relay_out3, relay_out4)):
        wait_one(buffer, relay_send.at[n])
    for turn in (0, 1):
        wait_one(rim_in.at[turn], rim_send.at[turn])
    store_c.wait()


def level_scratch(count):
    rows = count * 128
    return [
        pltpu.VMEM((2 * rows, 128), F32),
        pltpu.VMEM((rows + 16, 128), F32),
        pltpu.VMEM((rows + 16, 128), F32),
        pltpu.VMEM((2, 6, rows, 128), F32),
        pltpu.VMEM((2, rows, 128), F32),
        pltpu.VMEM((2, rows, 128), F32),
        pltpu.VMEM((2, rows, 128), F32),
        pltpu.VMEM((rows, 128), F32),
        pltpu.VMEM((rows, 128), F32),
    ]


def write_out(*refs):
    sources, targets, sem = refs[:3], refs[3:6], refs[6]
    copies = [pltpu.make_async_copy(x, y, sem.at[n]) for n, (x, y) in enumerate(zip(sources, targets))]
    for copy in copies:
        copy.start()
    for copy in copies:
        copy.wait()


def on_device(*args):
    fields, (parent_m, offset_m, parent_f, offset_f) = args[:6], args[6:]
    tables = (
        jnp.transpose(parent_m),
        jnp.transpose(offset_m, (2, 1, 0)),
        jnp.transpose(parent_f, (1, 2, 0)),
        jnp.transpose(offset_f, (1, 3, 2, 0)),
    )
    shapes = [args[0].shape, args[2].shape, args[4].shape]
    out_shape = [jax.ShapeDtypeStruct(shape, F32) for shape in shapes]
    anywhere = pl.BlockSpec(memory_space=pl.ANY)
    call = pl.pallas_call(
        kernel,
        out_shape=out_shape,
        in_specs=[pl.BlockSpec(memory_space=pltpu.HBM)] * 10,
        out_specs=[pl.BlockSpec(memory_space=pltpu.VMEM)] * 3,
        scratch_shapes=[
            *[pltpu.VMEM(shape, F32) for shape in ((32, 32, 128),) * 2 + ((32, 1024),) * 2 + ((2, 32, 1024),) * 2],
            *[pltpu.SMEM(shape, jnp.int32) for shape in (tables[0].shape, tables[1].shape, (2, 16), (3, 2, 16))],
            pltpu.VMEM((8, 2, 32, 128), F32),
            pltpu.VMEM((16, 32, 128), F32),
            pltpu.VMEM((8, 56, 128), F32),
            pltpu.VMEM((8, 56, 128), F32),
            pltpu.VMEM((32, 128), F32),
            pltpu.VMEM((32, 128), F32),
            pltpu.VMEM((56, 128), F32),
            pltpu.VMEM((56, 128), F32),
            pltpu.VMEM((2, 56, 128), F32),
            pltpu.VMEM((2, 56, 128), F32),
            pltpu.VMEM((2, 512, 128), F32),
            pltpu.VMEM((2, 576, 128), F32),
            pltpu.VMEM((512, 128), BF16),
            pltpu.VMEM((256, 256), BF16),
            pltpu.VMEM((256, 1024), BF16),
            pltpu.VMEM((256, 1024), BF16),
            pltpu.VMEM((1024, 384), BF16),
            pltpu.VMEM((1024, 384), BF16),
            pltpu.VMEM((128, 128), F32),
            pltpu.VMEM((512, 128), F32),
            pltpu.VMEM((48, 8, 128), F32),
            pltpu.VMEM((48, 32, 128), F32),
            pltpu.VMEM((33, 8, 128), F32),
            pltpu.VMEM((33, 32, 128), F32),
            pltpu.VMEM((256, 128), F32),
            pltpu.VMEM((24 * 32, 128), F32),
            pltpu.VMEM((2, WIDE, 128), F32),
            pltpu.VMEM((2, WIDE, 128), F32),
            pltpu.VMEM((2, WIDE, 128), F32),
            pltpu.VMEM((2, 6, PAIRS * ROWS, 128), F32),
            pltpu.VMEM((2, PAIRS * ROWS, 128), F32),
            *level_scratch(2),
            *level_scratch(1),
            pltpu.SemaphoreType.DMA((4,)),
            pltpu.SemaphoreType.DMA((4,)),
            pltpu.SemaphoreType.DMA((3,)),
            pltpu.SemaphoreType.DMA((3,)),
            pltpu.SemaphoreType.DMA((2,)),
            pltpu.SemaphoreType.DMA((6,)),
            pltpu.SemaphoreType.DMA((10,)),
            pltpu.SemaphoreType.DMA,
        ],
        compiler_params=pltpu.CompilerParams(
            collective_id=0, has_side_effects=True, vmem_limit_bytes=40 * 2**20
        ),
        name="v_cycle",
    )
    write = pl.pallas_call(
        write_out,
        out_shape=out_shape,
        in_specs=[pl.BlockSpec(memory_space=pltpu.VMEM)] * 3,
        out_specs=[anywhere] * 3,
        scratch_shapes=[pltpu.SemaphoreType.DMA((3,))],
        compiler_params=pltpu.CompilerParams(vmem_limit_bytes=8 * 2**20),
        name="write_out",
    )
    pinned = [pltpu.with_memory_space_constraint(arg, pltpu.HBM) for arg in fields + tables]
    return tuple(write(*call(*pinned)))


def solution(mesh):
    return jax.shard_map(
        on_device,
        mesh=mesh,
        in_specs=(
            P("xb", "yb", None),
            P("xb", "yb", None),
            P("xb", "yb", None, None),
            P("xb", "yb", None, None),
            P("xb", "yb", None, None, None),
            P("xb", "yb", None, None, None),
            P(),
            P(),
            P(),
            P(),
        ),
        out_specs=(P("xb", "yb", None), P("xb", "yb", None, None), P("xb", "yb", None, None, None)),
        check_vma=False,
    )
```

```python
import functools

import jax
import jax.numpy as jnp
from jax import lax
from jax.experimental import pallas as pl
from jax.experimental.pallas import tpu as pltpu
from jax.sharding import PartitionSpec as P

MESH = pl.DeviceIdType.MESH
F32 = jnp.float32
BF16 = jnp.bfloat16
CH = 64
PAIRS = 20
ROWS = 48
EDGE = 56
WIDE = 2 * EDGE + PAIRS * ROWS
CHIPS = ((2, 1), (1, 1), (3, 1), (2, 0), (0, 1), (1, 0), (3, 0))
SAME_CORE = [(dx, dh, 0) for dx, dh in CHIPS]
PEERS = [(dx, dh, dc) for dx, dh in CHIPS for dc in (0, 1)] + [(0, 0, 1)]


def iota(shape, dim):
    return lax.broadcasted_iota(jnp.int32, shape, dim)


def each(count, body, unroll=True):
    def step(i, carry):
        body(i)
        return carry

    lax.fori_loop(0, count, step, 0, unroll=unroll)


def chosen_dot(values, choice):
    rows = values.shape[0]
    high = values.astype(BF16).astype(F32)
    rest = values - high
    middle = rest.astype(BF16).astype(F32)
    terms = jnp.concatenate([high, middle, rest - middle], axis=0).astype(BF16)
    out = lax.dot_general(terms, choice, (((1,), (0,)), ((), ())), preferred_element_type=F32)
    return out[:rows] + out[rows : 2 * rows] + out[2 * rows :]


def onehot(mask, value=1.0):
    return jnp.where(mask, value, 0.0).astype(BF16)


class Level:
    def __init__(self, count, scale, refs):
        self.count, self.scale, self.rows = count, scale, count * 128
        (self.full, self.red, self.black, self.coef, self.g, self.inv, self.hb, self.tot, self.rest) = refs

    def field(self, colour):
        return self.black if colour else self.red

    def near(self, colour, at):
        ref = self.field(1 - colour)
        lane = iota((CH, 128), 1)
        odd = (lane // 32 + lane) % 2 == 1
        own = ref[pl.ds(8 + at, CH)]
        above, below = ref[pl.ds(16 + at, CH)], ref[pl.ds(at, CH)]
        after, before = ref[pl.ds(9 + at, CH)], ref[pl.ds(7 + at, CH)]
        other = jnp.where(odd, below, above) if colour else jnp.where(odd, above, below)
        return (
            own,
            other,
            pltpu.roll(jnp.where(lane >= 32, own, after), 96, 1),
            pltpu.roll(jnp.where(lane < 96, own, before), 32, 1),
            pltpu.roll(own, 127, 1),
            pltpu.roll(own, 1, 1),
        )

    def clear_ends(self):
        for ref in (self.red, self.black):
            ref[pl.ds(0, 8)] = jnp.zeros((8, 128), F32)
            ref[pl.ds(8 + self.rows, 8)] = jnp.zeros((8, 128), F32)

    def unfold(self, load):
        for box in range(self.count):
            for s in range(8):
                self.full[pl.ds(box * 256 + s, 32, stride=8)] = load(box, s)

    def packed(self, full, at):
        lane = iota((CH, 128), 1)
        odd = (lane // 32 + lane) % 2 == 1
        planes = full.reshape(CH // 8, 2, 8, 128)
        low, high = planes[:, 0].reshape(CH, 128), planes[:, 1].reshape(CH, 128)
        return jnp.where(odd, high, low), jnp.where(odd, low, high)

    def set_fields(self):
        def body(i):
            at = i * CH
            red, black = self.packed(self.full[pl.ds(2 * at, 2 * CH)], at)
            self.red[pl.ds(8 + at, CH)] = red
            self.black[pl.ds(8 + at, CH)] = black

        each(self.rows // CH, body)

    def set_weights(self):
        def body(i):
            at = i * CH
            lane, row = iota((CH, 128), 1), iota((CH, 128), 0)
            odd = (lane // 32 + lane) % 2 == 1
            s = row % 8
            pair = ((at + row) // 8) % 16
            z = lane % 32
            inside_y = (jnp.logical_not((s == 7) & (lane >= 96)), jnp.logical_not((s == 0) & (lane < 32)))
            inside_z = (z < 31, z > 0)
            for colour in (0, 1):
                first, last = (odd, jnp.logical_not(odd)) if colour else (jnp.logical_not(odd), odd)
                edge = (first & (pair == 0)) | (last & (pair == 15))
                masks = (None, jnp.logical_not(edge)) + inside_y + inside_z
                own = self.field(colour)[pl.ds(8 + at, CH)]
                near = self.near(colour, at)
                faces = [
                    0.5 * (own + (other if mask is None else jnp.where(mask, other, 0.0)))
                    for other, mask in zip(near, masks)
                ]
                total = faces[0] + faces[1] + faces[2] + faces[3] + faces[4] + faces[5]
                inv = 1.0 / total
                for n in range(6):
                    part = faces[n] * inv
                    self.coef[colour, n, pl.ds(at, CH)] = (
                        part if masks[n] is None else jnp.where(masks[n], part, 0.0)
                    )
                self.inv[colour, pl.ds(at, CH)] = inv * (1.0 / self.scale)
                self.hb[colour, pl.ds(at, CH)] = 0.5 * own * inv
                if colour == 0:
                    self.tot[pl.ds(at, CH)] = self.scale * total

        each(self.rows // CH, body)

    def set_target(self, at, red, black):
        for colour, value in ((0, red), (1, black)):
            self.g[colour, pl.ds(at, CH)] = value * self.inv[colour, pl.ds(at, CH)]

    def fresh(self, colour, at):
        near = self.near(colour, at)
        out = self.g[colour, pl.ds(at, CH)]
        for n in range(6):
            out = out + self.coef[colour, n, pl.ds(at, CH)] * near[n]
        return out

    def half_sweep(self, colour):
        def body(i):
            at = i * CH
            self.field(colour)[pl.ds(8 + at, CH)] = self.fresh(colour, at)

        each(self.rows // CH, body)

    def down(self):
        def first(i):
            at = i * CH
            self.red[pl.ds(8 + at, CH)] = self.g[0, pl.ds(at, CH)]

        each(self.rows // CH, first)
        self.half_sweep(1)
        self.half_sweep(0)
        self.half_sweep(1)

        def left(i):
            at = i * CH
            self.rest[pl.ds(at, CH)] = self.tot[pl.ds(at, CH)] * (
                self.fresh(0, at) - self.red[pl.ds(8 + at, CH)]
            )

        each(self.rows // CH, left)

    def restricted(self, mean):
        parts = []
        for box in range(self.count):
            for h in range(2):
                parts.append(
                    jnp.concatenate(
                        [self.rest[pl.ds(box * 128 + 4 * h + j, 16, stride=8)] for j in range(4)], axis=1
                    )
                )
        return chosen_dot(jnp.concatenate(parts, axis=0), mean)

    def start_up(self, pieces, spread):
        sub, lane = iota((8, 128), 0), iota((8, 128), 1)
        odd = (lane // 32 + lane) % 2 == 1
        even = jnp.logical_not(odd)
        rows_of = lane // 32 == sub % 4
        rows_of_face = (
            ((lane < 16) & (sub == 0))
            | ((lane >= 16) & (lane < 32) & (sub == 7))
            | ((lane >= 32) & (lane < 64) & ((lane % 16) // 2 == sub))
        )

        def tiles(rows):
            return jnp.broadcast_to(rows[:, None, :], (rows.shape[0], 8, 128))

        def halves(first, second):
            return jnp.where((sub < 4)[None], tiles(first), tiles(second))

        for box, piece in enumerate(pieces):
            core = jnp.concatenate(
                [
                    halves(piece[0:16], piece[16:32]),
                    halves(piece[48:49], piece[49:50]),
                    halves(piece[50:51], piece[51:52]),
                ],
                axis=0,
            )
            core = jnp.where(rows_of[None], core, 0.0).reshape(144, 128)
            face = jnp.where(rows_of_face[None], tiles(piece[32:48]), 0.0).reshape(128, 128)
            face = jnp.concatenate([face, jnp.zeros((16, 128), F32)], axis=0)
            grown = chosen_dot(jnp.concatenate([core, face], axis=1), spread)
            inner, border = grown[:128, :128], grown[:128, 128:].reshape(16, 8, 128)
            low, high = grown[128:136, :128], grown[136:144, :128]
            at = box * 128
            self.black[pl.ds(8 + at, 128)] = self.black[pl.ds(8 + at, 128)] + inner
            for colour in (0, 1):
                first, last = (odd, even) if colour else (even, odd)
                ghost = jnp.concatenate(
                    [
                        border[:1] + jnp.where(first, low, 0.0)[None],
                        border[1:15],
                        border[15:] + jnp.where(last, high, 0.0)[None],
                    ],
                    axis=0,
                ).reshape(128, 128)
                self.g[colour, pl.ds(at, 128)] = (
                    self.g[colour, pl.ds(at, 128)] + self.hb[colour, pl.ds(at, 128)] * ghost
                )

    def up(self):
        for colour in (0, 1, 0, 1):
            self.half_sweep(colour)

    def finished(self, at):
        lane = iota((CH, 128), 1)
        odd = (lane // 32 + lane) % 2 == 1
        red, black = self.red[pl.ds(8 + at, CH)], self.black[pl.ds(8 + at, CH)]
        low = jnp.where(odd, black, red).reshape(CH // 8, 1, 8, 128)
        high = jnp.where(odd, red, black).reshape(CH // 8, 1, 8, 128)
        return jnp.concatenate([low, high], axis=1).reshape(2 * CH, 128)


def spread_choice():
    l, n = iota((256, 256), 0), iota((256, 256), 1)
    z, q = n % 32, (n % 128) // 32
    inner = (l < 128) & (n < 128) & ((l // 16) % 2 == q // 2) & (l % 16 == z // 2)
    f = l - 128
    along_y = (f >= 0) & (f < 32) & (q == jnp.where(f < 16, 0, 3)) & (z // 2 == f % 16)
    along_z = (f >= 32) & (f < 64) & (q // 2 == f % 2) & (z == jnp.where(f < 48, 0, 31))
    return onehot(inner | ((n >= 128) & (along_y | along_z)))


def mean_choice():
    k, n = iota((512, 128), 0), iota((512, 128), 1)
    lane = k % 128
    return onehot(n == 32 * (k // 128) + 16 * (lane // 64) + (lane % 32) // 2, 0.125)


def place_choice(corner):
    k, n = iota((256, 1024), 0), iota((256, 1024), 1)
    return onehot(n == (k // 16) * 32 + k % 16 + corner[1] * 32 + corner[2])


def window_choice(corner):
    n = iota((1, 384), 1)
    i = n % 16
    source = jnp.where(n < 256, (n // 16) * 32 + i, -4096)
    source = jnp.where((n >= 256) & (n < 272), i - 32, source)
    source = jnp.where((n >= 272) & (n < 288), i + 512, source)
    source = jnp.where((n >= 288) & (n < 304), i * 32 - 1, source)
    source = jnp.where((n >= 304) & (n < 320), i * 32 + 16, source)
    return onehot(iota((1024, 384), 0) == source + corner[1] * 32 + corner[2])


def placed_lhs(piece):
    return jnp.concatenate([piece[0:16], piece[16:32]], axis=1)


def kernel(
    far_rhs_c, far_beta_c, far_rhs_m, far_beta_m, far_rhs_f, far_beta_f,
    far_parent_m, far_offset_m, far_parent_f, far_offset_f,
    out_c, out_m, out_f,
    rhs_c, beta_c, rhs_m, beta_m, rhs_f, beta_f, parent_m, offset_m, parent_f, offset_f,
    gather1, gather2, gather3, gather4, relay_out1, relay_in1, relay_out2, relay_in2, relay_out3, relay_in3, relay_out4, relay_in4,
    rim_out, rim_in,
    mean_ref, spread_ref, place_m, place_c, window_m, window_c,
    put_m, put_c, pad_m, pad_c, wide_m, wide_c, cut_m, cut_c,
    beta_e, g_e, field_e, coef_e, inv_e,
    *rest,
):
    fine_refs, mid_refs = rest[:9], rest[9:18]
    send_sems, recv_sems, relay_send, relay_recv, rim_send, rim_recv, load_sems = rest[18:]
    fine = Level(2, 1.0, fine_refs)
    mid = Level(1, 0.25, mid_refs)
    n_x, n_y = lax.axis_size("xb"), lax.axis_size("yb")
    row, col = lax.axis_index("xb"), lax.axis_index("yb")

    def load(n, source, target):
        copy = pltpu.make_async_copy(source, target, load_sems.at[n])
        copy.start()
        return copy

    load_beta_f = load(0, far_beta_f.at[0, 0], beta_f)
    load_rhs_f = load(1, far_rhs_f.at[0, 0], rhs_f)
    load_beta_c = load(3, far_beta_c, beta_c)
    load_beta_m = load(2, far_beta_m.at[0, 0], beta_m)
    load_rhs_m = load(4, far_rhs_m.at[0, 0], rhs_m)
    load_rhs_c = load(5, far_rhs_c, rhs_c)
    load_tables = (
        load(6, far_parent_m, parent_m),
        load(7, far_offset_m, offset_m),
        load(8, far_parent_f.at[col], parent_f),
        load(9, far_offset_f.at[col], offset_f),
    )

    def beside(dx, dy):
        return (lax.rem(row + dx + n_x, n_x), lax.rem(col + dy + n_y, n_y))

    def peer(dx, dh, dc):
        x, h, c = row // 4, (row // 2) % 2, row % 2
        return (((x + dx) % 4) * 4 + ((h + dh) % 2) * 2 + (c + dc) % 2, col)

    barrier = pltpu.get_barrier_semaphore()
    greeted = [peer(*hop) for hop in PEERS] + [beside(dx, dy) for dx in (-1, 0, 1) for dy in (-1, 1)]
    for device in greeted:
        pl.semaphore_signal(barrier, inc=1, device_id=device, device_id_type=MESH)

    twin = row + 1 - 2 * (row % 2)
    chip = row // 2

    def send_all(buffer, stage, place, hops):
        for hop in hops:
            pltpu.make_async_remote_copy(
                src_ref=buffer.at[place],
                dst_ref=buffer.at[place],
                send_sem=send_sems.at[stage],
                recv_sem=recv_sems.at[stage],
                device_id=peer(*hop),
                device_id_type=MESH,
            ).start()

    def wait_all(buffer, sem, hops):
        whole = buffer.at[pl.ds(0, len(hops))]
        pltpu.make_async_copy(whole, whole, sem).wait()

    def wait_one(buffer, sem):
        pltpu.make_async_copy(buffer, buffer, sem).wait()

    def relay(n, source, target):
        pltpu.make_async_remote_copy(
            src_ref=source,
            dst_ref=target,
            send_sem=relay_send.at[n],
            recv_sem=relay_recv.at[n],
            device_id=(twin, col),
            device_id_type=MESH,
        ).start()

    def own_core(device):
        return lax.rem(device, 2) == row % 2

    def chip_of(device):
        return lax.div(device, 2)

    def send_rim(turn):
        def copy(kind, source, size, target, device):
            pltpu.make_async_remote_copy(
                src_ref=rim_out.at[turn, pl.ds(source, size)],
                dst_ref=rim_in.at[turn, pl.ds(target, size)],
                send_sem=rim_send.at[turn],
                recv_sem=rim_recv.at[3 * turn + kind],
                device_id=device,
                device_id_type=MESH,
            ).start()

        for side_x in (0, 1):
            for side_y in (0, 1):
                copy(
                    2, 256 + 128 * side_y + 112 * side_x, 16,
                    512 + 16 * (2 * (1 - side_x) + 1 - side_y),
                    beside(2 * side_x - 1, 2 * side_y - 1),
                )
        for side in (0, 1):
            copy(1, 256 + 128 * side, 128, 256 + 128 * (1 - side), beside(0, 2 * side - 1))
        for side in (0, 1):
            copy(0, 128 * side, 128, 128 * (1 - side), beside(2 * side - 1, 0))

    def wait_rim(turn, kind):
        wait_one(rim_in.at[turn, pl.ds(256 * kind, (256, 256, 64)[kind])], rim_recv.at[3 * turn + kind])

    def fill_rim(turn, ref):
        tile_row = iota((8, 128), 0)
        for side in (0, 1):
            for colour in (0, 1):
                for d in (0, 1):
                    at = EDGE + ((2, 16)[side] + d) * ROWS + 8
                    rim_out[turn, pl.ds(128 * side + (2 * colour + d) * 32, 32)] = ref[colour, pl.ds(at, 32)]

        def body(k):
            at = EDGE + (k + 2) * ROWS
            red, black = ref[0, pl.ds(at + 8, 8)], ref[1, pl.ds(at + 8, 8)]
            rim_out[turn, pl.ds(256 + k * 8, 8)] = jnp.where(tile_row < 4, red, pltpu.roll(black, 4, 0))
            red, black = ref[0, pl.ds(at + 32, 8)], ref[1, pl.ds(at + 32, 8)]
            rim_out[turn, pl.ds(384 + k * 8, 8)] = jnp.where(tile_row < 4, pltpu.roll(black, 4, 0), red)

        each(16, body)

    def keep(value, *sides):
        for side in sides:
            if side is not None:
                value = jnp.where(side, value, 0.0)
        return value

    def take_y(turn, ref, inside_y):
        def body(k):
            for side in (0, 1):
                at = EDGE + (k + 2) * ROWS + 40 * side
                part = keep(rim_in[turn, pl.ds(256 + 128 * side + 8 * k, 8)], inside_y[side])
                ref[0, pl.ds(at, 8)] = part
                ref[1, pl.ds(at, 8)] = pltpu.roll(part, 4, 0)

        each(16, body)

    def take_x(turn, ref, inside_x, inside_y):
        for side in (0, 1):
            for colour in (0, 1):
                for d in (0, 1):
                    at = EDGE + ((0, 18)[side] + d) * ROWS + 8
                    part = rim_in[turn, pl.ds(128 * side + (2 * colour + d) * 32, 32)]
                    ref[colour, pl.ds(at, 32)] = keep(part, inside_x[side])
            for other in (0, 1):
                for d in (0, 1):
                    at = EDGE + (18 * side + d) * ROWS + 40 * other
                    part = rim_in[turn, pl.ds(512 + 16 * (2 * side + other) + 8 * d, 8)]
                    part = keep(part, inside_x[side], inside_y[other])
                    ref[0, pl.ds(at, 8)] = part
                    ref[1, pl.ds(at, 8)] = pltpu.roll(part, 4, 0)

    mean_ref[...] = mean_choice()
    fine.clear_ends()

    load_beta_f.wait()
    fine.unfold(lambda box, s: beta_f[box, :, 128 * s : 128 * s + 128])
    fine.set_fields()
    fine.set_weights()
    load_rhs_f.wait()
    fine.unfold(lambda box, s: rhs_f[box, :, 128 * s : 128 * s + 128])

    def fine_target(i):
        at = i * CH
        fine.set_target(at, *fine.packed(fine.full[pl.ds(2 * at, 2 * CH)], at))

    each(fine.rows // CH, fine_target)
    pl.semaphore_wait(barrier, len(greeted))
    fine.down()
    gather1[chip] = fine.restricted(mean_ref[...]).reshape(2, 32, 128)
    send_all(gather1, 0, chip, SAME_CORE)

    def own_beta(k):
        lane, line = iota((32, 128), 1), iota((32, 128), 0)
        odd = (line + lane) % 2 == 1
        low, high = beta_c[2 * k], beta_c[2 * k + 1]
        at = EDGE + (k + 2) * ROWS + 8
        beta_e[0, pl.ds(at, 32)] = jnp.where(odd, high, low)
        beta_e[1, pl.ds(at, 32)] = jnp.where(odd, low, high)

    for colour in (0, 1):
        beta_e[colour, pl.ds(0, EDGE)] = jnp.zeros((EDGE, 128), F32)
        beta_e[colour, pl.ds(WIDE - EDGE, EDGE)] = jnp.zeros((EDGE, 128), F32)
    load_beta_c.wait()
    each(16, own_beta)
    fill_rim(0, beta_e)
    send_rim(0)
    mid.clear_ends()
    load_beta_m.wait()
    mid.unfold(lambda box, s: beta_m[:, 128 * s : 128 * s + 128])
    mid.set_fields()
    mid.set_weights()
    load_rhs_m.wait()
    mid.unfold(lambda box, s: rhs_m[:, 128 * s : 128 * s + 128])

    for copy in load_tables:
        copy.wait()

    def find_fine(i, carry):
        index, place, x, y, z, twin_index, twin_place = carry
        for slot in range(2):
            twin_hit = parent_f[slot, i] == twin
            twin_index = jnp.where(twin_hit, i, twin_index)
            twin_place = jnp.where(twin_hit, slot, twin_place)
            hit = parent_f[slot, i] == row
            index = jnp.where(hit, i, index)
            place = jnp.where(hit, slot, place)
            x = jnp.where(hit, offset_f[0, slot, i], x)
            y = jnp.where(hit, offset_f[1, slot, i], y)
            z = jnp.where(hit, offset_f[2, slot, i], z)
        return index, place, x, y, z, twin_index, twin_place

    def find_mid(i, carry):
        index, x, y, z, twin_index = carry
        hit = parent_m[col, i] == row
        return (
            jnp.where(hit, i, index),
            jnp.where(hit, offset_m[0, col, i], x),
            jnp.where(hit, offset_m[1, col, i], y),
            jnp.where(hit, offset_m[2, col, i], z),
            jnp.where(parent_m[col, i] == twin, i, twin_index),
        )

    zero, one = jnp.int32(0), jnp.int32(1)
    child, child_slot, *corner_m, twin_child, twin_slot = lax.fori_loop(
        0, 16, find_fine, (zero, zero, one, one, one, zero, zero)
    )
    guest, *corner_c, twin_guest = lax.fori_loop(0, 16, find_mid, (zero, one, one, one, zero))
    place_m[...] = place_choice(corner_m)
    pad_m[0:16] = jnp.zeros((16, 8, 128), F32)
    pad_m[32:48] = jnp.zeros((16, 8, 128), F32)

    wait_all(gather1, recv_sems.at[0], SAME_CORE)
    relay_out1[...] = gather1[chip_of(twin_child), twin_slot]
    relay(0, relay_out1, relay_in1)
    wait_one(relay_in1, relay_recv.at[0])

    piece = jnp.where(own_core(child), gather1[chip_of(child), child_slot], relay_in1[...])
    put = chosen_dot(placed_lhs(piece), place_m[...])
    for s in range(8):
        put_m[pl.ds(s, 16, stride=8)] = put[:, 128 * s : 128 * s + 128]
    pad_m[16:32] = put_m[...].reshape(16, 8, 128)

    def shift_m(x):
        cut_m[pl.ds(8 * x, 8)] = pad_m[16 - corner_m[0] + x]

    each(32, shift_m)

    def mid_target(i):
        lane, line = iota((2 * CH, 128), 1), iota((2 * CH, 128), 0)
        x = i * (CH // 4) + line // 8 - corner_m[0]
        y = (line % 8) * 4 + lane // 32 - corner_m[1]
        z = lane % 32 - corner_m[2]
        hit = (x >= 0) & (x < 16) & (y >= 0) & (y < 16) & (z >= 0) & (z < 16)
        full = jnp.where(hit, cut_m[pl.ds(2 * CH * i, 2 * CH)], mid.full[pl.ds(2 * CH * i, 2 * CH)])
        mid.set_target(i * CH, *mid.packed(full, i * CH))

    each(mid.rows // CH, mid_target)
    mid.down()
    gather2[chip] = mid.restricted(mean_ref[...])
    send_all(gather2, 1, chip, SAME_CORE)

    place_c[...] = place_choice(corner_c)
    pad_c[0:16] = jnp.zeros((16, 32, 128), F32)
    pad_c[32:48] = jnp.zeros((16, 32, 128), F32)
    for kind in (0, 1, 2):
        wait_rim(0, kind)
    inside_x, inside_y = (row > 0, row < n_x - 1), (col > 0, col < n_y - 1)
    take_y(0, beta_e, inside_y)
    take_x(0, beta_e, inside_x, inside_y)

    def near_wide(ref, colour, at, rows):
        lane, line = iota((rows, 128), 1), iota((rows, 128), 0)
        odd = (line + lane) % 2 == 1
        own = ref[1 - colour, pl.ds(at, rows)]
        above, below = ref[1 - colour, pl.ds(at + ROWS, rows)], ref[1 - colour, pl.ds(at - ROWS, rows)]
        other = jnp.where(odd, below, above) if colour else jnp.where(odd, above, below)
        after, before = ref[1 - colour, pl.ds(at + 1, rows)], ref[1 - colour, pl.ds(at - 1, rows)]
        return own, other, after, before, pltpu.roll(own, 127, 1), pltpu.roll(own, 1, 1)

    def coarse_weights(k):
        lane = iota((ROWS, 128), 1)
        masks = (None, None, None, None, lane < 127, lane > 0)
        at = EDGE + k * ROWS
        for colour in (0, 1):
            own = beta_e[colour, pl.ds(at, ROWS)]
            near = near_wide(beta_e, colour, at, ROWS)
            faces = [
                0.5 * (own + (other if mask is None else jnp.where(mask, other, 0.0)))
                for other, mask in zip(near, masks)
            ]
            total = faces[0] + faces[1] + faces[2] + faces[3] + faces[4] + faces[5]
            real = own > 0.0
            inv = jnp.where(real, 1.0 / total, 0.0)
            for n in range(6):
                keep = real if masks[n] is None else real & masks[n]
                coef_e[colour, n, pl.ds(k * ROWS, ROWS)] = jnp.where(keep, faces[n] * inv, 0.0)
            inv_e[colour, pl.ds(k * ROWS, ROWS)] = 16.0 * inv

    each(PAIRS, coarse_weights, 4)
    window_c[...] = window_choice(corner_c)
    wait_all(gather2, recv_sems.at[1], SAME_CORE)
    relay_out2[...] = gather2[chip_of(twin_guest)]
    relay(3, relay_out2, relay_in2)
    wait_one(relay_in2, relay_recv.at[3])

    piece = jnp.where(own_core(guest), gather2[chip_of(guest)], relay_in2[...])
    put = chosen_dot(placed_lhs(piece), place_c[...])
    for s in range(8):
        part = put[:, 128 * s : 128 * s + 128]
        for q in range(4):
            put_c[pl.ds(4 * s + q, 16, stride=32)] = part if q == 0 else pltpu.roll(part, 128 - 32 * q, 1)

    pad_c[16:32] = put_c[...].reshape(16, 32, 128)

    load_rhs_c.wait()

    def coarse_target(k):
        lane, line = iota((32, 128), 1), iota((32, 128), 0)
        odd = (line + lane) % 2 == 1
        y, z = line - corner_c[1], lane - corner_c[2]
        hit = (y >= 0) & (y < 16) & (z >= 0) & (z < 16)
        planes = []
        for d in (0, 1):
            x = 2 * k + d - corner_c[0]
            planes.append(jnp.where(hit & (x >= 0) & (x < 16), pad_c[16 + x], rhs_c[2 * k + d]))
        at = EDGE + (k + 2) * ROWS + 8
        g_e[0, pl.ds(at, 32)] = jnp.where(odd, planes[1], planes[0])
        g_e[1, pl.ds(at, 32)] = jnp.where(odd, planes[0], planes[1])

    each(16, coarse_target)
    fill_rim(1, g_e)
    send_rim(1)

    def coarse_first(first, count, line, rows):
        def body(i):
            at, here = EDGE + (first + i) * ROWS + line, (first + i) * ROWS + line
            field_e[0, pl.ds(at, rows)] = g_e[0, pl.ds(at, rows)] * inv_e[0, pl.ds(here, rows)]

        each(count, body)

    def coarse_sweep(colour, first, count, line=0, rows=ROWS):
        def body(i):
            k = first + i
            at, here = EDGE + k * ROWS + line, k * ROWS + line
            near = near_wide(field_e, colour, at, rows)
            out = g_e[colour, pl.ds(at, rows)] * inv_e[colour, pl.ds(here, rows)]
            for n in range(6):
                out = out + coef_e[colour, n, pl.ds(here, rows)] * near[n]
            field_e[colour, pl.ds(at, rows)] = out

        each(count, body)

    coarse_first(2, 16, 8, 32)
    wait_rim(1, 1)
    take_y(1, g_e, (None, None))
    coarse_first(2, 16, 0, 8)
    coarse_first(2, 16, 40, 8)
    coarse_sweep(1, 3, 14)
    coarse_sweep(0, 4, 12)
    coarse_sweep(1, 5, 10, 8, 32)
    wait_rim(1, 0)
    wait_rim(1, 2)
    take_x(1, g_e, (None, None), (None, None))
    for first in (0, 18):
        coarse_first(first, 2, 0, ROWS)
    for first in (1, 17):
        coarse_sweep(1, first, 2)
    for first in (1, 16):
        coarse_sweep(0, first, 3)
    for first in (2, 15):
        coarse_sweep(1, first, 3, 8, 32)

    def coarse_out(k):
        lane, line = iota((32, 128), 1), iota((32, 128), 0)
        odd = (line + lane) % 2 == 1
        at = EDGE + (k + 2) * ROWS + 8
        red, black = field_e[0, pl.ds(at, 32)], field_e[1, pl.ds(at, 32)]
        low, high = jnp.where(odd, black, red), jnp.where(odd, red, black)
        wide_c[1 + 2 * k] = low
        wide_c[2 + 2 * k] = high

    each(16, coarse_out)

    def post_window(buffer, stage, lhs, choice):
        got = chosen_dot(lhs, choice)
        for n in range(3):
            buffer[chip, pl.ds(16 * n, 16)] = got[1:17, 128 * n : 128 * n + 128]
        for n, (x, h) in enumerate(((0, 0), (0, 1), (17, 0), (17, 1))):
            buffer[chip, pl.ds(48 + n, 1)] = got[x : x + 1, 128 * h : 128 * h + 128]
        send_all(buffer, stage, chip, SAME_CORE)

    def cut_window_c(x):
        cut_c[pl.ds(32 * x, 32)] = wide_c[corner_c[0] + x]

    each(18, cut_window_c)
    lane24 = iota((24, 128), 1)
    blocks = []
    for s in range(8):
        block = None
        for q in range(4):
            part = cut_c[pl.ds(4 * s + q, 24, stride=32)]
            if q == 0:
                block = part
            else:
                block = jnp.where(lane24 // 32 == q, pltpu.roll(part, 32 * q, 1), block)
        blocks.append(block)
    post_window(gather3, 2, jnp.concatenate(blocks, axis=1), window_c[...])
    out_c[...] = wide_c[1:33]
    spread_ref[...] = spread_choice()
    window_m[...] = window_choice(corner_m)
    wait_all(gather3, recv_sems.at[2], SAME_CORE)
    relay_out3[...] = gather3[chip_of(parent_m[col, twin])]
    relay(1, relay_out3, relay_in3)
    wait_one(relay_in3, relay_recv.at[1])

    owner_m = parent_m[col, row]
    piece = jnp.where(own_core(owner_m), gather3[chip_of(owner_m)], relay_in3[...])
    mid.start_up([piece], spread_ref[...])
    mid.up()

    def mid_out(i):
        full = mid.finished(CH * i)
        mid.full[pl.ds(2 * CH * i, 2 * CH)] = full
        wide_m[pl.ds(1 + CH // 4 * i, CH // 4)] = full.reshape(CH // 4, 8, 128)

    each(mid.rows // CH, mid_out)

    def cut_window_m(x):
        cut_m[pl.ds(8 * x, 8)] = wide_m[corner_m[0] + x]

    each(18, cut_window_m)
    lhs = jnp.concatenate([cut_m[pl.ds(s, 24, stride=8)] for s in range(8)], axis=1)
    post_window(gather4, 3, lhs, window_m[...])
    for s in range(8):
        out_m[0, 0, :, 128 * s : 128 * s + 128] = mid.full[pl.ds(s, 32, stride=8)]
    wait_all(gather4, recv_sems.at[3], SAME_CORE)
    for slot in range(2):
        relay_out4[slot] = gather4[chip_of(jnp.maximum(parent_f[slot, twin], 0))]
    relay(2, relay_out4, relay_in4)
    wait_one(relay_in4, relay_recv.at[2])

    owners = [parent_f[slot, row] for slot in range(2)]
    pieces = []
    for slot, owner in enumerate(owners):
        owner = jnp.maximum(owner, 0)
        pieces.append(jnp.where(own_core(owner), gather4[chip_of(owner)], relay_in4[slot]))
    fine.start_up(pieces, spread_ref[...])
    fine.up()

    def fine_out(i):
        fine.full[pl.ds(2 * CH * i, 2 * CH)] = fine.finished(CH * i)

    each(fine.rows // CH, fine_out)
    for box in range(2):
        for s in range(8):
            part = fine.full[pl.ds(box * 256 + s, 32, stride=8)]
            out_f[0, 0, box, :, 128 * s : 128 * s + 128] = jnp.where(owners[box] >= 0, part, 0.0)

    wait_all(gather1, send_sems.at[0], SAME_CORE)
    wait_all(gather2, send_sems.at[1], SAME_CORE)
    wait_all(gather3, send_sems.at[2], SAME_CORE)
    wait_all(gather4, send_sems.at[3], SAME_CORE)
    for n, buffer in enumerate((relay_out1, relay_out3, relay_out4, relay_out2)):
        wait_one(buffer, relay_send.at[n])
    for turn in (0, 1):
        wait_one(rim_in.at[turn], rim_send.at[turn])


def level_scratch(count):
    rows = count * 128
    return [
        pltpu.VMEM((2 * rows, 128), F32),
        pltpu.VMEM((rows + 16, 128), F32),
        pltpu.VMEM((rows + 16, 128), F32),
        pltpu.VMEM((2, 6, rows, 128), F32),
        pltpu.VMEM((2, rows, 128), F32),
        pltpu.VMEM((2, rows, 128), F32),
        pltpu.VMEM((2, rows, 128), F32),
        pltpu.VMEM((rows, 128), F32),
        pltpu.VMEM((rows, 128), F32),
    ]


def write_out(*refs):
    sources, targets, sem = refs[:3], refs[3:6], refs[6]
    copies = [pltpu.make_async_copy(x, y, sem.at[n]) for n, (x, y) in enumerate(zip(sources, targets))]
    for copy in copies:
        copy.start()
    for copy in copies:
        copy.wait()


def on_device(*args):
    fields, (parent_m, offset_m, parent_f, offset_f) = args[:6], args[6:]
    tables = (
        jnp.transpose(parent_m),
        jnp.transpose(offset_m, (2, 1, 0)),
        jnp.transpose(parent_f, (1, 2, 0)),
        jnp.transpose(offset_f, (1, 3, 2, 0)),
    )
    shapes = [args[0].shape, args[2].shape, args[4].shape]
    out_shape = [jax.ShapeDtypeStruct(shape, F32) for shape in shapes]
    anywhere = pl.BlockSpec(memory_space=pl.ANY)
    call = pl.pallas_call(
        kernel,
        out_shape=out_shape,
        in_specs=[pl.BlockSpec(memory_space=pltpu.HBM)] * 10,
        out_specs=[pl.BlockSpec(memory_space=pltpu.VMEM)] * 3,
        scratch_shapes=[
            *[pltpu.VMEM(shape, F32) for shape in ((32, 32, 128),) * 2 + ((32, 1024),) * 2 + ((2, 32, 1024),) * 2],
            *[pltpu.SMEM(shape, jnp.int32) for shape in (tables[0].shape, tables[1].shape, (2, 16), (3, 2, 16))],
            pltpu.VMEM((8, 2, 32, 128), F32),
            pltpu.VMEM((8, 32, 128), F32),
            pltpu.VMEM((8, 56, 128), F32),
            pltpu.VMEM((8, 56, 128), F32),
            pltpu.VMEM((32, 128), F32),
            pltpu.VMEM((32, 128), F32),
            pltpu.VMEM((32, 128), F32),
            pltpu.VMEM((32, 128), F32),
            pltpu.VMEM((56, 128), F32),
            pltpu.VMEM((56, 128), F32),
            pltpu.VMEM((2, 56, 128), F32),
            pltpu.VMEM((2, 56, 128), F32),
            pltpu.VMEM((2, 512, 128), F32),
            pltpu.VMEM((2, 576, 128), F32),
            pltpu.VMEM((512, 128), BF16),
            pltpu.VMEM((256, 256), BF16),
            pltpu.VMEM((256, 1024), BF16),
            pltpu.VMEM((256, 1024), BF16),
            pltpu.VMEM((1024, 384), BF16),
            pltpu.VMEM((1024, 384), BF16),
            pltpu.VMEM((128, 128), F32),
            pltpu.VMEM((512, 128), F32),
            pltpu.VMEM((48, 8, 128), F32),
            pltpu.VMEM((48, 32, 128), F32),
            pltpu.VMEM((33, 8, 128), F32),
            pltpu.VMEM((33, 32, 128), F32),
            pltpu.VMEM((256, 128), F32),
            pltpu.VMEM((24 * 32, 128), F32),
            pltpu.VMEM((2, WIDE, 128), F32),
            pltpu.VMEM((2, WIDE, 128), F32),
            pltpu.VMEM((2, WIDE, 128), F32),
            pltpu.VMEM((2, 6, PAIRS * ROWS, 128), F32),
            pltpu.VMEM((2, PAIRS * ROWS, 128), F32),
            *level_scratch(2),
            *level_scratch(1),
            pltpu.SemaphoreType.DMA((4,)),
            pltpu.SemaphoreType.DMA((4,)),
            pltpu.SemaphoreType.DMA((4,)),
            pltpu.SemaphoreType.DMA((4,)),
            pltpu.SemaphoreType.DMA((2,)),
            pltpu.SemaphoreType.DMA((6,)),
            pltpu.SemaphoreType.DMA((10,)),
        ],
        compiler_params=pltpu.CompilerParams(
            collective_id=0, has_side_effects=True, vmem_limit_bytes=40 * 2**20
        ),
        name="v_cycle",
    )
    write = pl.pallas_call(
        write_out,
        out_shape=out_shape,
        in_specs=[pl.BlockSpec(memory_space=pltpu.VMEM)] * 3,
        out_specs=[anywhere] * 3,
        scratch_shapes=[pltpu.SemaphoreType.DMA((3,))],
        compiler_params=pltpu.CompilerParams(vmem_limit_bytes=8 * 2**20),
        name="write_out",
    )
    pinned = [pltpu.with_memory_space_constraint(arg, pltpu.HBM) for arg in fields + tables]
    return tuple(write(*call(*pinned)))


def solution(mesh):
    return jax.shard_map(
        on_device,
        mesh=mesh,
        in_specs=(
            P("xb", "yb", None),
            P("xb", "yb", None),
            P("xb", "yb", None, None),
            P("xb", "yb", None, None),
            P("xb", "yb", None, None, None),
            P("xb", "yb", None, None, None),
            P(),
            P(),
            P(),
            P(),
        ),
        out_specs=(P("xb", "yb", None), P("xb", "yb", None, None), P("xb", "yb", None, None, None)),
        check_vma=False,
    )
```

```python
import functools

import jax
import jax.numpy as jnp
from jax import lax
from jax.experimental import pallas as pl
from jax.experimental.pallas import tpu as pltpu
from jax.sharding import PartitionSpec as P

MESH = pl.DeviceIdType.MESH
F32 = jnp.float32
BF16 = jnp.bfloat16
CH = 64
PAIRS = 20
ROWS = 48
EDGE = 56
WIDE = 2 * EDGE + PAIRS * ROWS
CHIPS = ((2, 1), (1, 1), (3, 1), (2, 0), (0, 1), (1, 0), (3, 0))
SAME_CORE = [(dx, dh, 0) for dx, dh in CHIPS]


def iota(shape, dim):
    return lax.broadcasted_iota(jnp.int32, shape, dim)


def each(count, body, unroll=True):
    def step(i, carry):
        body(i)
        return carry

    lax.fori_loop(0, count, step, 0, unroll=unroll)


def chosen_dot(values, choice):
    rows = values.shape[0]
    high = values.astype(BF16).astype(F32)
    rest = values - high
    middle = rest.astype(BF16).astype(F32)
    terms = jnp.concatenate([high, middle, rest - middle], axis=0).astype(BF16)
    out = lax.dot_general(terms, choice, (((1,), (0,)), ((), ())), preferred_element_type=F32)
    return out[:rows] + out[rows : 2 * rows] + out[2 * rows :]


def onehot(mask, value=1.0):
    return jnp.where(mask, value, 0.0).astype(BF16)


class Level:
    def __init__(self, count, scale, refs):
        self.count, self.scale, self.rows = count, scale, count * 128
        (self.full, self.red, self.black, self.coef, self.g, self.inv, self.hb, self.tot, self.rest) = refs

    def field(self, colour):
        return self.black if colour else self.red

    def near(self, colour, at):
        ref = self.field(1 - colour)
        lane = iota((CH, 128), 1)
        odd = (lane // 32 + lane) % 2 == 1
        own = ref[pl.ds(8 + at, CH)]
        above, below = ref[pl.ds(16 + at, CH)], ref[pl.ds(at, CH)]
        after, before = ref[pl.ds(9 + at, CH)], ref[pl.ds(7 + at, CH)]
        other = jnp.where(odd, below, above) if colour else jnp.where(odd, above, below)
        return (
            own,
            other,
            pltpu.roll(jnp.where(lane >= 32, own, after), 96, 1),
            pltpu.roll(jnp.where(lane < 96, own, before), 32, 1),
            pltpu.roll(own, 127, 1),
            pltpu.roll(own, 1, 1),
        )

    def clear_ends(self):
        for ref in (self.red, self.black):
            ref[pl.ds(0, 8)] = jnp.zeros((8, 128), F32)
            ref[pl.ds(8 + self.rows, 8)] = jnp.zeros((8, 128), F32)

    def unfold(self, load):
        for box in range(self.count):
            for s in range(8):
                self.full[pl.ds(box * 256 + s, 32, stride=8)] = load(box, s)

    def packed(self, full, at):
        lane = iota((CH, 128), 1)
        odd = (lane // 32 + lane) % 2 == 1
        planes = full.reshape(CH // 8, 2, 8, 128)
        low, high = planes[:, 0].reshape(CH, 128), planes[:, 1].reshape(CH, 128)
        return jnp.where(odd, high, low), jnp.where(odd, low, high)

    def set_fields(self):
        def body(i):
            at = i * CH
            red, black = self.packed(self.full[pl.ds(2 * at, 2 * CH)], at)
            self.red[pl.ds(8 + at, CH)] = red
            self.black[pl.ds(8 + at, CH)] = black

        each(self.rows // CH, body)

    def set_weights(self):
        def body(i):
            at = i * CH
            lane, row = iota((CH, 128), 1), iota((CH, 128), 0)
            odd = (lane // 32 + lane) % 2 == 1
            s = row % 8
            pair = ((at + row) // 8) % 16
            z = lane % 32
            inside_y = (jnp.logical_not((s == 7) & (lane >= 96)), jnp.logical_not((s == 0) & (lane < 32)))
            inside_z = (z < 31, z > 0)
            for colour in (0, 1):
                first, last = (odd, jnp.logical_not(odd)) if colour else (jnp.logical_not(odd), odd)
                edge = (first & (pair == 0)) | (last & (pair == 15))
                masks = (None, jnp.logical_not(edge)) + inside_y + inside_z
                own = self.field(colour)[pl.ds(8 + at, CH)]
                near = self.near(colour, at)
                faces = [
                    0.5 * (own + (other if mask is None else jnp.where(mask, other, 0.0)))
                    for other, mask in zip(near, masks)
                ]
                total = faces[0] + faces[1] + faces[2] + faces[3] + faces[4] + faces[5]
                inv = 1.0 / total
                for n in range(6):
                    part = faces[n] * inv
                    self.coef[colour, n, pl.ds(at, CH)] = (
                        part if masks[n] is None else jnp.where(masks[n], part, 0.0)
                    )
                self.inv[colour, pl.ds(at, CH)] = inv * (1.0 / self.scale)
                self.hb[colour, pl.ds(at, CH)] = 0.5 * own * inv
                if colour == 0:
                    self.tot[pl.ds(at, CH)] = self.scale * total

        each(self.rows // CH, body)

    def set_target(self, at, red, black):
        for colour, value in ((0, red), (1, black)):
            self.g[colour, pl.ds(at, CH)] = value * self.inv[colour, pl.ds(at, CH)]

    def fresh(self, colour, at):
        near = self.near(colour, at)
        out = self.g[colour, pl.ds(at, CH)]
        for n in range(6):
            out = out + self.coef[colour, n, pl.ds(at, CH)] * near[n]
        return out

    def half_sweep(self, colour):
        def body(i):
            at = i * CH
            self.field(colour)[pl.ds(8 + at, CH)] = self.fresh(colour, at)

        each(self.rows // CH, body)

    def down(self):
        def first(i):
            at = i * CH
            self.red[pl.ds(8 + at, CH)] = self.g[0, pl.ds(at, CH)]

        each(self.rows // CH, first)
        self.half_sweep(1)
        self.half_sweep(0)
        self.half_sweep(1)

        def left(i):
            at = i * CH
            self.rest[pl.ds(at, CH)] = self.tot[pl.ds(at, CH)] * (
                self.fresh(0, at) - self.red[pl.ds(8 + at, CH)]
            )

        each(self.rows // CH, left)

    def restricted(self, mean):
        parts = []
        for box in range(self.count):
            for h in range(2):
                parts.append(
                    jnp.concatenate(
                        [self.rest[pl.ds(box * 128 + 4 * h + j, 16, stride=8)] for j in range(4)], axis=1
                    )
                )
        return chosen_dot(jnp.concatenate(parts, axis=0), mean)

    def start_up(self, pieces, spread):
        sub, lane = iota((8, 128), 0), iota((8, 128), 1)
        odd = (lane // 32 + lane) % 2 == 1
        even = jnp.logical_not(odd)
        rows_of = lane // 32 == sub % 4
        rows_of_face = (
            ((lane < 16) & (sub == 0))
            | ((lane >= 16) & (lane < 32) & (sub == 7))
            | ((lane >= 32) & (lane < 64) & ((lane % 16) // 2 == sub))
        )

        def tiles(rows):
            return jnp.broadcast_to(rows[:, None, :], (rows.shape[0], 8, 128))

        def halves(first, second):
            return jnp.where((sub < 4)[None], tiles(first), tiles(second))

        for box, piece in enumerate(pieces):
            core = jnp.concatenate(
                [
                    halves(piece[0:16], piece[16:32]),
                    halves(piece[48:49], piece[49:50]),
                    halves(piece[50:51], piece[51:52]),
                ],
                axis=0,
            )
            core = jnp.where(rows_of[None], core, 0.0).reshape(144, 128)
            face = jnp.where(rows_of_face[None], tiles(piece[32:48]), 0.0).reshape(128, 128)
            face = jnp.concatenate([face, jnp.zeros((16, 128), F32)], axis=0)
            grown = chosen_dot(jnp.concatenate([core, face], axis=1), spread)
            inner, border = grown[:128, :128], grown[:128, 128:].reshape(16, 8, 128)
            low, high = grown[128:136, :128], grown[136:144, :128]
            at = box * 128
            self.black[pl.ds(8 + at, 128)] = self.black[pl.ds(8 + at, 128)] + inner
            for colour in (0, 1):
                first, last = (odd, even) if colour else (even, odd)
                ghost = jnp.concatenate(
                    [
                        border[:1] + jnp.where(first, low, 0.0)[None],
                        border[1:15],
                        border[15:] + jnp.where(last, high, 0.0)[None],
                    ],
                    axis=0,
                ).reshape(128, 128)
                self.g[colour, pl.ds(at, 128)] = (
                    self.g[colour, pl.ds(at, 128)] + self.hb[colour, pl.ds(at, 128)] * ghost
                )

    def up(self):
        for colour in (0, 1, 0, 1):
            self.half_sweep(colour)

    def finished(self, at):
        lane = iota((CH, 128), 1)
        odd = (lane // 32 + lane) % 2 == 1
        red, black = self.red[pl.ds(8 + at, CH)], self.black[pl.ds(8 + at, CH)]
        low = jnp.where(odd, black, red).reshape(CH // 8, 1, 8, 128)
        high = jnp.where(odd, red, black).reshape(CH // 8, 1, 8, 128)
        return jnp.concatenate([low, high], axis=1).reshape(2 * CH, 128)


def spread_choice():
    l, n = iota((256, 256), 0), iota((256, 256), 1)
    z, q = n % 32, (n % 128) // 32
    inner = (l < 128) & (n < 128) & ((l // 16) % 2 == q // 2) & (l % 16 == z // 2)
    f = l - 128
    along_y = (f >= 0) & (f < 32) & (q == jnp.where(f < 16, 0, 3)) & (z // 2 == f % 16)
    along_z = (f >= 32) & (f < 64) & (q // 2 == f % 2) & (z == jnp.where(f < 48, 0, 31))
    return onehot(inner | ((n >= 128) & (along_y | along_z)))


def mean_choice():
    k, n = iota((512, 128), 0), iota((512, 128), 1)
    lane = k % 128
    return onehot(n == 32 * (k // 128) + 16 * (lane // 64) + (lane % 32) // 2, 0.125)


def place_choice(corner):
    k, n = iota((256, 1024), 0), iota((256, 1024), 1)
    return onehot(n == (k // 16) * 32 + k % 16 + corner[1] * 32 + corner[2])


def window_choice(corner):
    n = iota((1, 384), 1)
    i = n % 16
    source = jnp.where(n < 256, (n // 16) * 32 + i, -4096)
    source = jnp.where((n >= 256) & (n < 272), i - 32, source)
    source = jnp.where((n >= 272) & (n < 288), i + 512, source)
    source = jnp.where((n >= 288) & (n < 304), i * 32 - 1, source)
    source = jnp.where((n >= 304) & (n < 320), i * 32 + 16, source)
    return onehot(iota((1024, 384), 0) == source + corner[1] * 32 + corner[2])


def placed_lhs(piece):
    return jnp.concatenate([piece[0:16], piece[16:32]], axis=1)


def kernel(
    far_rhs_c, far_beta_c, far_rhs_m, far_beta_m, far_rhs_f, far_beta_f,
    far_parent_m, far_offset_m, far_parent_f, far_offset_f,
    out_c, out_m, out_f,
    rhs_c, beta_c, rhs_m, beta_m, rhs_f, beta_f, parent_m, offset_m, parent_f, offset_f,
    gather1, gather2, gather3, gather4, relay_out1, relay_in1, relay_out2, relay_in2, relay_out3, relay_in3, relay_out4, relay_in4,
    rim_out, rim_in,
    mean_ref, spread_ref, place_m, place_c, window_m, window_c,
    put_m, put_c, pad_m, pad_c, wide_m, wide_c, cut_m, cut_c,
    beta_e, g_e, field_e, coef_e, inv_e,
    *rest,
):
    fine_refs, mid_refs = rest[:9], rest[9:18]
    send_sems, recv_sems, relay_send, relay_recv, rim_send, rim_recv, load_sems = rest[18:]
    fine = Level(2, 1.0, fine_refs)
    mid = Level(1, 0.25, mid_refs)
    n_x, n_y = lax.axis_size("xb"), lax.axis_size("yb")
    row, col = lax.axis_index("xb"), lax.axis_index("yb")

    def load(n, source, target):
        copy = pltpu.make_async_copy(source, target, load_sems.at[n])
        copy.start()
        return copy

    load_beta_f = load(0, far_beta_f.at[0, 0], beta_f)
    load_rhs_f = load(1, far_rhs_f.at[0, 0], rhs_f)
    load_beta_c = load(3, far_beta_c, beta_c)
    load_beta_m = load(2, far_beta_m.at[0, 0], beta_m)
    load_rhs_m = load(4, far_rhs_m.at[0, 0], rhs_m)
    load_rhs_c = load(5, far_rhs_c, rhs_c)
    load_tables = (
        load(6, far_parent_m, parent_m),
        load(7, far_offset_m, offset_m),
        load(8, far_parent_f.at[col], parent_f),
        load(9, far_offset_f.at[col], offset_f),
    )

    def beside(dx, dy):
        return (lax.rem(row + dx + n_x, n_x), lax.rem(col + dy + n_y, n_y))

    def peer(dx, dh, dc):
        x, h, c = row // 4, (row // 2) % 2, row % 2
        return (((x + dx) % 4) * 4 + ((h + dh) % 2) * 2 + (c + dc) % 2, col)

    barrier = pltpu.get_barrier_semaphore()
    greeted = [peer(*hop) for hop in SAME_CORE] + [peer(0, 0, 1), beside(-1, 0), beside(1, 0)]
    greeted += [beside(dx, dy) for dx in (-1, 0, 1) for dy in (-1, 1)]
    for device in greeted:
        pl.semaphore_signal(barrier, inc=1, device_id=device, device_id_type=MESH)

    twin = row + 1 - 2 * (row % 2)
    chip = row // 2

    def send_all(buffer, stage, place, hops):
        for hop in hops:
            pltpu.make_async_remote_copy(
                src_ref=buffer.at[place],
                dst_ref=buffer.at[place],
                send_sem=send_sems.at[stage],
                recv_sem=recv_sems.at[stage],
                device_id=peer(*hop),
                device_id_type=MESH,
            ).start()

    def wait_all(buffer, sem, hops):
        whole = buffer.at[pl.ds(0, len(hops))]
        pltpu.make_async_copy(whole, whole, sem).wait()

    def wait_one(buffer, sem):
        pltpu.make_async_copy(buffer, buffer, sem).wait()

    def relay(n, source, target):
        pltpu.make_async_remote_copy(
            src_ref=source,
            dst_ref=target,
            send_sem=relay_send.at[n],
            recv_sem=relay_recv.at[n],
            device_id=(twin, col),
            device_id_type=MESH,
        ).start()

    def own_core(device):
        return lax.rem(device, 2) == row % 2

    def chip_of(device):
        return lax.div(device, 2)

    def send_rim(turn):
        def copy(kind, source, size, target, device):
            pltpu.make_async_remote_copy(
                src_ref=rim_out.at[turn, pl.ds(source, size)],
                dst_ref=rim_in.at[turn, pl.ds(target, size)],
                send_sem=rim_send.at[turn],
                recv_sem=rim_recv.at[3 * turn + kind],
                device_id=device,
                device_id_type=MESH,
            ).start()

        for side_x in (0, 1):
            for side_y in (0, 1):
                copy(
                    2, 256 + 128 * side_y + 112 * side_x, 16,
                    512 + 16 * (2 * (1 - side_x) + 1 - side_y),
                    beside(2 * side_x - 1, 2 * side_y - 1),
                )
        for side in (0, 1):
            copy(1, 256 + 128 * side, 128, 256 + 128 * (1 - side), beside(0, 2 * side - 1))
        for side in (0, 1):
            copy(0, 128 * side, 128, 128 * (1 - side), beside(2 * side - 1, 0))

    def wait_rim(turn, kind):
        wait_one(rim_in.at[turn, pl.ds(256 * kind, (256, 256, 64)[kind])], rim_recv.at[3 * turn + kind])

    def fill_rim(turn, ref):
        tile_row = iota((8, 128), 0)
        for side in (0, 1):
            for colour in (0, 1):
                for d in (0, 1):
                    at = EDGE + ((2, 16)[side] + d) * ROWS + 8
                    rim_out[turn, pl.ds(128 * side + (2 * colour + d) * 32, 32)] = ref[colour, pl.ds(at, 32)]

        def body(k):
            at = EDGE + (k + 2) * ROWS
            red, black = ref[0, pl.ds(at + 8, 8)], ref[1, pl.ds(at + 8, 8)]
            rim_out[turn, pl.ds(256 + k * 8, 8)] = jnp.where(tile_row < 4, red, pltpu.roll(black, 4, 0))
            red, black = ref[0, pl.ds(at + 32, 8)], ref[1, pl.ds(at + 32, 8)]
            rim_out[turn, pl.ds(384 + k * 8, 8)] = jnp.where(tile_row < 4, pltpu.roll(black, 4, 0), red)

        each(16, body)

    def keep(value, *sides):
        for side in sides:
            if side is not None:
                value = jnp.where(side, value, 0.0)
        return value

    def take_y(turn, ref, inside_y):
        def body(k):
            for side in (0, 1):
                at = EDGE + (k + 2) * ROWS + 40 * side
                part = keep(rim_in[turn, pl.ds(256 + 128 * side + 8 * k, 8)], inside_y[side])
                ref[0, pl.ds(at, 8)] = part
                ref[1, pl.ds(at, 8)] = pltpu.roll(part, 4, 0)

        each(16, body)

    def take_x(turn, ref, inside_x, inside_y):
        for side in (0, 1):
            for colour in (0, 1):
                for d in (0, 1):
                    at = EDGE + ((0, 18)[side] + d) * ROWS + 8
                    part = rim_in[turn, pl.ds(128 * side + (2 * colour + d) * 32, 32)]
                    ref[colour, pl.ds(at, 32)] = keep(part, inside_x[side])
            for other in (0, 1):
                for d in (0, 1):
                    at = EDGE + (18 * side + d) * ROWS + 40 * other
                    part = rim_in[turn, pl.ds(512 + 16 * (2 * side + other) + 8 * d, 8)]
                    part = keep(part, inside_x[side], inside_y[other])
                    ref[0, pl.ds(at, 8)] = part
                    ref[1, pl.ds(at, 8)] = pltpu.roll(part, 4, 0)

    mean_ref[...] = mean_choice()
    fine.clear_ends()

    load_beta_f.wait()
    fine.unfold(lambda box, s: beta_f[box, :, 128 * s : 128 * s + 128])
    fine.set_fields()
    fine.set_weights()
    load_rhs_f.wait()
    fine.unfold(lambda box, s: rhs_f[box, :, 128 * s : 128 * s + 128])

    def fine_target(i):
        at = i * CH
        fine.set_target(at, *fine.packed(fine.full[pl.ds(2 * at, 2 * CH)], at))

    each(fine.rows // CH, fine_target)
    pl.semaphore_wait(barrier, len(greeted))
    fine.down()
    gather1[chip] = fine.restricted(mean_ref[...]).reshape(2, 32, 128)
    send_all(gather1, 0, chip, SAME_CORE)

    def own_beta(k):
        lane, line = iota((32, 128), 1), iota((32, 128), 0)
        odd = (line + lane) % 2 == 1
        low, high = beta_c[2 * k], beta_c[2 * k + 1]
        at = EDGE + (k + 2) * ROWS + 8
        beta_e[0, pl.ds(at, 32)] = jnp.where(odd, high, low)
        beta_e[1, pl.ds(at, 32)] = jnp.where(odd, low, high)

    for colour in (0, 1):
        beta_e[colour, pl.ds(0, EDGE)] = jnp.zeros((EDGE, 128), F32)
        beta_e[colour, pl.ds(WIDE - EDGE, EDGE)] = jnp.zeros((EDGE, 128), F32)
    load_beta_c.wait()
    each(16, own_beta)
    fill_rim(0, beta_e)
    send_rim(0)
    mid.clear_ends()
    load_beta_m.wait()
    mid.unfold(lambda box, s: beta_m[:, 128 * s : 128 * s + 128])
    mid.set_fields()
    mid.set_weights()
    load_rhs_m.wait()
    mid.unfold(lambda box, s: rhs_m[:, 128 * s : 128 * s + 128])

    for copy in load_tables:
        copy.wait()

    def find_fine(i, carry):
        index, place, x, y, z, twin_index, twin_place = carry
        for slot in range(2):
            twin_hit = parent_f[slot, i] == twin
            twin_index = jnp.where(twin_hit, i, twin_index)
            twin_place = jnp.where(twin_hit, slot, twin_place)
            hit = parent_f[slot, i] == row
            index = jnp.where(hit, i, index)
            place = jnp.where(hit, slot, place)
            x = jnp.where(hit, offset_f[0, slot, i], x)
            y = jnp.where(hit, offset_f[1, slot, i], y)
            z = jnp.where(hit, offset_f[2, slot, i], z)
        return index, place, x, y, z, twin_index, twin_place

    def find_mid(i, carry):
        index, x, y, z, twin_index = carry
        hit = parent_m[col, i] == row
        return (
            jnp.where(hit, i, index),
            jnp.where(hit, offset_m[0, col, i], x),
            jnp.where(hit, offset_m[1, col, i], y),
            jnp.where(hit, offset_m[2, col, i], z),
            jnp.where(parent_m[col, i] == twin, i, twin_index),
        )

    zero, one = jnp.int32(0), jnp.int32(1)
    child, child_slot, *corner_m, twin_child, twin_slot = lax.fori_loop(
        0, 16, find_fine, (zero, zero, one, one, one, zero, zero)
    )
    guest, *corner_c, twin_guest = lax.fori_loop(0, 16, find_mid, (zero, one, one, one, zero))
    place_m[...] = place_choice(corner_m)
    pad_m[0:16] = jnp.zeros((16, 8, 128), F32)
    pad_m[32:48] = jnp.zeros((16, 8, 128), F32)

    wait_all(gather1, recv_sems.at[0], SAME_CORE)
    relay_out1[...] = gather1[chip_of(twin_child), twin_slot]
    relay(0, relay_out1, relay_in1)
    wait_one(relay_in1, relay_recv.at[0])

    piece = jnp.where(own_core(child), gather1[chip_of(child), child_slot], relay_in1[...])
    put = chosen_dot(placed_lhs(piece), place_m[...])
    for s in range(8):
        put_m[pl.ds(s, 16, stride=8)] = put[:, 128 * s : 128 * s + 128]
    pad_m[16:32] = put_m[...].reshape(16, 8, 128)

    def shift_m(x):
        cut_m[pl.ds(8 * x, 8)] = pad_m[16 - corner_m[0] + x]

    each(32, shift_m)

    def mid_target(i):
        lane, line = iota((2 * CH, 128), 1), iota((2 * CH, 128), 0)
        x = i * (CH // 4) + line // 8 - corner_m[0]
        y = (line % 8) * 4 + lane // 32 - corner_m[1]
        z = lane % 32 - corner_m[2]
        hit = (x >= 0) & (x < 16) & (y >= 0) & (y < 16) & (z >= 0) & (z < 16)
        full = jnp.where(hit, cut_m[pl.ds(2 * CH * i, 2 * CH)], mid.full[pl.ds(2 * CH * i, 2 * CH)])
        mid.set_target(i * CH, *mid.packed(full, i * CH))

    each(mid.rows // CH, mid_target)
    mid.down()
    gather2[chip] = mid.restricted(mean_ref[...])
    send_all(gather2, 1, chip, SAME_CORE)

    place_c[...] = place_choice(corner_c)
    pad_c[0:16] = jnp.zeros((16, 32, 128), F32)
    pad_c[32:48] = jnp.zeros((16, 32, 128), F32)
    for kind in (0, 1, 2):
        wait_rim(0, kind)
    inside_x, inside_y = (row > 0, row < n_x - 1), (col > 0, col < n_y - 1)
    take_y(0, beta_e, inside_y)
    take_x(0, beta_e, inside_x, inside_y)

    def near_wide(ref, colour, at, rows):
        lane, line = iota((rows, 128), 1), iota((rows, 128), 0)
        odd = (line + lane) % 2 == 1
        own = ref[1 - colour, pl.ds(at, rows)]
        above, below = ref[1 - colour, pl.ds(at + ROWS, rows)], ref[1 - colour, pl.ds(at - ROWS, rows)]
        other = jnp.where(odd, below, above) if colour else jnp.where(odd, above, below)
        after, before = ref[1 - colour, pl.ds(at + 1, rows)], ref[1 - colour, pl.ds(at - 1, rows)]
        return own, other, after, before, pltpu.roll(own, 127, 1), pltpu.roll(own, 1, 1)

    def coarse_weights(k):
        lane = iota((ROWS, 128), 1)
        masks = (None, None, None, None, lane < 127, lane > 0)
        at = EDGE + k * ROWS
        for colour in (0, 1):
            own = beta_e[colour, pl.ds(at, ROWS)]
            near = near_wide(beta_e, colour, at, ROWS)
            faces = [
                0.5 * (own + (other if mask is None else jnp.where(mask, other, 0.0)))
                for other, mask in zip(near, masks)
            ]
            total = faces[0] + faces[1] + faces[2] + faces[3] + faces[4] + faces[5]
            real = own > 0.0
            inv = jnp.where(real, 1.0 / total, 0.0)
            for n in range(6):
                keep = real if masks[n] is None else real & masks[n]
                coef_e[colour, n, pl.ds(k * ROWS, ROWS)] = jnp.where(keep, faces[n] * inv, 0.0)
            inv_e[colour, pl.ds(k * ROWS, ROWS)] = 16.0 * inv

    each(PAIRS, coarse_weights, 4)
    window_c[...] = window_choice(corner_c)
    wait_all(gather2, recv_sems.at[1], SAME_CORE)
    relay_out2[...] = gather2[chip_of(twin_guest)]
    relay(3, relay_out2, relay_in2)
    wait_one(relay_in2, relay_recv.at[3])

    piece = jnp.where(own_core(guest), gather2[chip_of(guest)], relay_in2[...])
    put = chosen_dot(placed_lhs(piece), place_c[...])
    for s in range(8):
        part = put[:, 128 * s : 128 * s + 128]
        for q in range(4):
            put_c[pl.ds(4 * s + q, 16, stride=32)] = part if q == 0 else pltpu.roll(part, 128 - 32 * q, 1)

    pad_c[16:32] = put_c[...].reshape(16, 32, 128)

    load_rhs_c.wait()

    def coarse_target(k):
        lane, line = iota((32, 128), 1), iota((32, 128), 0)
        odd = (line + lane) % 2 == 1
        y, z = line - corner_c[1], lane - corner_c[2]
        hit = (y >= 0) & (y < 16) & (z >= 0) & (z < 16)
        planes = []
        for d in (0, 1):
            x = 2 * k + d - corner_c[0]
            planes.append(jnp.where(hit & (x >= 0) & (x < 16), pad_c[16 + x], rhs_c[2 * k + d]))
        at = EDGE + (k + 2) * ROWS + 8
        g_e[0, pl.ds(at, 32)] = jnp.where(odd, planes[1], planes[0])
        g_e[1, pl.ds(at, 32)] = jnp.where(odd, planes[0], planes[1])

    each(16, coarse_target)
    fill_rim(1, g_e)
    send_rim(1)

    def coarse_first(first, count, line, rows):
        def body(i):
            at, here = EDGE + (first + i) * ROWS + line, (first + i) * ROWS + line
            field_e[0, pl.ds(at, rows)] = g_e[0, pl.ds(at, rows)] * inv_e[0, pl.ds(here, rows)]

        each(count, body)

    def coarse_sweep(colour, first, count, line=0, rows=ROWS):
        def body(i):
            k = first + i
            at, here = EDGE + k * ROWS + line, k * ROWS + line
            near = near_wide(field_e, colour, at, rows)
            out = g_e[colour, pl.ds(at, rows)] * inv_e[colour, pl.ds(here, rows)]
            for n in range(6):
                out = out + coef_e[colour, n, pl.ds(here, rows)] * near[n]
            field_e[colour, pl.ds(at, rows)] = out

        each(count, body)

    coarse_first(2, 16, 8, 32)
    wait_rim(1, 1)
    take_y(1, g_e, (None, None))
    coarse_first(2, 16, 0, 8)
    coarse_first(2, 16, 40, 8)
    coarse_sweep(1, 3, 14)
    coarse_sweep(0, 4, 12)
    coarse_sweep(1, 5, 10, 8, 32)
    wait_rim(1, 0)
    wait_rim(1, 2)
    take_x(1, g_e, (None, None), (None, None))
    for first in (0, 18):
        coarse_first(first, 2, 0, ROWS)
    for first in (1, 17):
        coarse_sweep(1, first, 2)
    for first in (1, 16):
        coarse_sweep(0, first, 3)
    for first in (2, 15):
        coarse_sweep(1, first, 3, 8, 32)

    def coarse_out(k):
        lane, line = iota((32, 128), 1), iota((32, 128), 0)
        odd = (line + lane) % 2 == 1
        at = EDGE + (k + 2) * ROWS + 8
        red, black = field_e[0, pl.ds(at, 32)], field_e[1, pl.ds(at, 32)]
        low, high = jnp.where(odd, black, red), jnp.where(odd, red, black)
        wide_c[1 + 2 * k] = low
        wide_c[2 + 2 * k] = high

    each(16, coarse_out)

    def post_window(buffer, stage, lhs, choice):
        got = chosen_dot(lhs, choice)
        for n in range(3):
            buffer[chip, pl.ds(16 * n, 16)] = got[1:17, 128 * n : 128 * n + 128]
        for n, (x, h) in enumerate(((0, 0), (0, 1), (17, 0), (17, 1))):
            buffer[chip, pl.ds(48 + n, 1)] = got[x : x + 1, 128 * h : 128 * h + 128]
        send_all(buffer, stage, chip, SAME_CORE)

    def cut_window_c(x):
        cut_c[pl.ds(32 * x, 32)] = wide_c[corner_c[0] + x]

    each(18, cut_window_c)
    lane24 = iota((24, 128), 1)
    blocks = []
    for s in range(8):
        block = None
        for q in range(4):
            part = cut_c[pl.ds(4 * s + q, 24, stride=32)]
            if q == 0:
                block = part
            else:
                block = jnp.where(lane24 // 32 == q, pltpu.roll(part, 32 * q, 1), block)
        blocks.append(block)
    post_window(gather3, 2, jnp.concatenate(blocks, axis=1), window_c[...])
    out_c[...] = wide_c[1:33]
    spread_ref[...] = spread_choice()
    window_m[...] = window_choice(corner_m)
    wait_all(gather3, recv_sems.at[2], SAME_CORE)
    relay_out3[...] = gather3[chip_of(parent_m[col, twin])]
    relay(1, relay_out3, relay_in3)
    wait_one(relay_in3, relay_recv.at[1])

    owner_m = parent_m[col, row]
    piece = jnp.where(own_core(owner_m), gather3[chip_of(owner_m)], relay_in3[...])
    mid.start_up([piece], spread_ref[...])
    mid.up()

    def mid_out(i):
        full = mid.finished(CH * i)
        mid.full[pl.ds(2 * CH * i, 2 * CH)] = full
        wide_m[pl.ds(1 + CH // 4 * i, CH // 4)] = full.reshape(CH // 4, 8, 128)

    each(mid.rows // CH, mid_out)

    def cut_window_m(x):
        cut_m[pl.ds(8 * x, 8)] = wide_m[corner_m[0] + x]

    each(18, cut_window_m)
    lhs = jnp.concatenate([cut_m[pl.ds(s, 24, stride=8)] for s in range(8)], axis=1)
    post_window(gather4, 3, lhs, window_m[...])
    for s in range(8):
        out_m[0, 0, :, 128 * s : 128 * s + 128] = mid.full[pl.ds(s, 32, stride=8)]
    wait_all(gather4, recv_sems.at[3], SAME_CORE)
    for slot in range(2):
        relay_out4[slot] = gather4[chip_of(jnp.maximum(parent_f[slot, twin], 0))]
    relay(2, relay_out4, relay_in4)
    wait_one(relay_in4, relay_recv.at[2])

    owners = [parent_f[slot, row] for slot in range(2)]
    pieces = []
    for slot, owner in enumerate(owners):
        owner = jnp.maximum(owner, 0)
        pieces.append(jnp.where(own_core(owner), gather4[chip_of(owner)], relay_in4[slot]))
    fine.start_up(pieces, spread_ref[...])
    fine.up()

    def fine_out(i):
        fine.full[pl.ds(2 * CH * i, 2 * CH)] = fine.finished(CH * i)

    each(fine.rows // CH, fine_out)
    for box in range(2):
        for s in range(8):
            part = fine.full[pl.ds(box * 256 + s, 32, stride=8)]
            out_f[0, 0, box, :, 128 * s : 128 * s + 128] = jnp.where(owners[box] >= 0, part, 0.0)

    wait_all(gather1, send_sems.at[0], SAME_CORE)
    wait_all(gather2, send_sems.at[1], SAME_CORE)
    wait_all(gather3, send_sems.at[2], SAME_CORE)
    wait_all(gather4, send_sems.at[3], SAME_CORE)
    for n, buffer in enumerate((relay_out1, relay_out3, relay_out4, relay_out2)):
        wait_one(buffer, relay_send.at[n])
    for turn in (0, 1):
        wait_one(rim_in.at[turn], rim_send.at[turn])


def level_scratch(count):
    rows = count * 128
    return [
        pltpu.VMEM((2 * rows, 128), F32),
        pltpu.VMEM((rows + 16, 128), F32),
        pltpu.VMEM((rows + 16, 128), F32),
        pltpu.VMEM((2, 6, rows, 128), F32),
        pltpu.VMEM((2, rows, 128), F32),
        pltpu.VMEM((2, rows, 128), F32),
        pltpu.VMEM((2, rows, 128), F32),
        pltpu.VMEM((rows, 128), F32),
        pltpu.VMEM((rows, 128), F32),
    ]


def write_out(*refs):
    sources, targets, sem = refs[:3], refs[3:6], refs[6]
    copies = [pltpu.make_async_copy(x, y, sem.at[n]) for n, (x, y) in enumerate(zip(sources, targets))]
    for copy in copies:
        copy.start()
    for copy in copies:
        copy.wait()


def on_device(*args):
    fields, (parent_m, offset_m, parent_f, offset_f) = args[:6], args[6:]
    tables = (
        jnp.transpose(parent_m),
        jnp.transpose(offset_m, (2, 1, 0)),
        jnp.transpose(parent_f, (1, 2, 0)),
        jnp.transpose(offset_f, (1, 3, 2, 0)),
    )
    shapes = [args[0].shape, args[2].shape, args[4].shape]
    out_shape = [jax.ShapeDtypeStruct(shape, F32) for shape in shapes]
    anywhere = pl.BlockSpec(memory_space=pl.ANY)
    call = pl.pallas_call(
        kernel,
        out_shape=out_shape,
        in_specs=[pl.BlockSpec(memory_space=pltpu.HBM)] * 10,
        out_specs=[pl.BlockSpec(memory_space=pltpu.VMEM)] * 3,
        scratch_shapes=[
            *[pltpu.VMEM(shape, F32) for shape in ((32, 32, 128),) * 2 + ((32, 1024),) * 2 + ((2, 32, 1024),) * 2],
            *[pltpu.SMEM(shape, jnp.int32) for shape in (tables[0].shape, tables[1].shape, (2, 16), (3, 2, 16))],
            pltpu.VMEM((8, 2, 32, 128), F32),
            pltpu.VMEM((8, 32, 128), F32),
            pltpu.VMEM((8, 56, 128), F32),
            pltpu.VMEM((8, 56, 128), F32),
            pltpu.VMEM((32, 128), F32),
            pltpu.VMEM((32, 128), F32),
            pltpu.VMEM((32, 128), F32),
            pltpu.VMEM((32, 128), F32),
            pltpu.VMEM((56, 128), F32),
            pltpu.VMEM((56, 128), F32),
            pltpu.VMEM((2, 56, 128), F32),
            pltpu.VMEM((2, 56, 128), F32),
            pltpu.VMEM((2, 512, 128), F32),
            pltpu.VMEM((2, 576, 128), F32),
            pltpu.VMEM((512, 128), BF16),
            pltpu.VMEM((256, 256), BF16),
            pltpu.VMEM((256, 1024), BF16),
            pltpu.VMEM((256, 1024), BF16),
            pltpu.VMEM((1024, 384), BF16),
            pltpu.VMEM((1024, 384), BF16),
            pltpu.VMEM((128, 128), F32),
            pltpu.VMEM((512, 128), F32),
            pltpu.VMEM((48, 8, 128), F32),
            pltpu.VMEM((48, 32, 128), F32),
            pltpu.VMEM((33, 8, 128), F32),
            pltpu.VMEM((33, 32, 128), F32),
            pltpu.VMEM((256, 128), F32),
            pltpu.VMEM((24 * 32, 128), F32),
            pltpu.VMEM((2, WIDE, 128), F32),
            pltpu.VMEM((2, WIDE, 128), F32),
            pltpu.VMEM((2, WIDE, 128), F32),
            pltpu.VMEM((2, 6, PAIRS * ROWS, 128), F32),
            pltpu.VMEM((2, PAIRS * ROWS, 128), F32),
            *level_scratch(2),
            *level_scratch(1),
            pltpu.SemaphoreType.DMA((4,)),
            pltpu.SemaphoreType.DMA((4,)),
            pltpu.SemaphoreType.DMA((4,)),
            pltpu.SemaphoreType.DMA((4,)),
            pltpu.SemaphoreType.DMA((2,)),
            pltpu.SemaphoreType.DMA((6,)),
            pltpu.SemaphoreType.DMA((10,)),
        ],
        compiler_params=pltpu.CompilerParams(
            collective_id=0, has_side_effects=True, vmem_limit_bytes=40 * 2**20
        ),
        name="v_cycle",
    )
    write = pl.pallas_call(
        write_out,
        out_shape=out_shape,
        in_specs=[pl.BlockSpec(memory_space=pltpu.VMEM)] * 3,
        out_specs=[anywhere] * 3,
        scratch_shapes=[pltpu.SemaphoreType.DMA((3,))],
        compiler_params=pltpu.CompilerParams(vmem_limit_bytes=8 * 2**20),
        name="write_out",
    )
    pinned = [pltpu.with_memory_space_constraint(arg, pltpu.HBM) for arg in fields + tables]
    return tuple(write(*call(*pinned)))


def solution(mesh):
    return jax.shard_map(
        on_device,
        mesh=mesh,
        in_specs=(
            P("xb", "yb", None),
            P("xb", "yb", None),
            P("xb", "yb", None, None),
            P("xb", "yb", None, None),
            P("xb", "yb", None, None, None),
            P("xb", "yb", None, None, None),
            P(),
            P(),
            P(),
            P(),
        ),
        out_specs=(P("xb", "yb", None), P("xb", "yb", None, None), P("xb", "yb", None, None, None)),
        check_vma=False,
    )
```

```python
import functools

import jax
import jax.numpy as jnp
from jax import lax
from jax.experimental import pallas as pl
from jax.experimental.pallas import tpu as pltpu
from jax.sharding import PartitionSpec as P

MESH = pl.DeviceIdType.MESH
F32 = jnp.float32
BF16 = jnp.bfloat16
CH = 64
PAIRS = 20
ROWS = 48
EDGE = 56
WIDE = 2 * EDGE + PAIRS * ROWS
CHIPS = ((2, 1), (1, 1), (3, 1), (0, 1), (2, 0), (1, 0), (3, 0))
SAME_CORE = [(dx, dh, 0) for dx, dh in CHIPS]


def iota(shape, dim):
    return lax.broadcasted_iota(jnp.int32, shape, dim)


def each(count, body, unroll=True):
    def step(i, carry):
        body(i)
        return carry

    lax.fori_loop(0, count, step, 0, unroll=unroll)


def chosen_dot(values, choice):
    rows = values.shape[0]
    high = values.astype(BF16).astype(F32)
    rest = values - high
    middle = rest.astype(BF16).astype(F32)
    terms = jnp.concatenate([high, middle, rest - middle], axis=0).astype(BF16)
    out = lax.dot_general(terms, choice, (((1,), (0,)), ((), ())), preferred_element_type=F32)
    return out[:rows] + out[rows : 2 * rows] + out[2 * rows :]


def onehot(mask, value=1.0):
    return jnp.where(mask, value, 0.0).astype(BF16)


class Level:
    def __init__(self, count, scale, refs):
        self.count, self.scale, self.rows = count, scale, count * 128
        (self.full, self.red, self.black, self.coef, self.g, self.inv, self.hb, self.tot, self.rest) = refs

    def field(self, colour):
        return self.black if colour else self.red

    def near(self, colour, at):
        ref = self.field(1 - colour)
        lane = iota((CH, 128), 1)
        odd = (lane // 32 + lane) % 2 == 1
        own = ref[pl.ds(8 + at, CH)]
        above, below = ref[pl.ds(16 + at, CH)], ref[pl.ds(at, CH)]
        after, before = ref[pl.ds(9 + at, CH)], ref[pl.ds(7 + at, CH)]
        other = jnp.where(odd, below, above) if colour else jnp.where(odd, above, below)
        return (
            own,
            other,
            pltpu.roll(jnp.where(lane >= 32, own, after), 96, 1),
            pltpu.roll(jnp.where(lane < 96, own, before), 32, 1),
            pltpu.roll(own, 127, 1),
            pltpu.roll(own, 1, 1),
        )

    def clear_ends(self):
        for ref in (self.red, self.black):
            ref[pl.ds(0, 8)] = jnp.zeros((8, 128), F32)
            ref[pl.ds(8 + self.rows, 8)] = jnp.zeros((8, 128), F32)

    def unfold(self, load):
        for box in range(self.count):
            for s in range(8):
                self.full[pl.ds(box * 256 + s, 32, stride=8)] = load(box, s)

    def packed(self, full, at):
        lane = iota((CH, 128), 1)
        odd = (lane // 32 + lane) % 2 == 1
        planes = full.reshape(CH // 8, 2, 8, 128)
        low, high = planes[:, 0].reshape(CH, 128), planes[:, 1].reshape(CH, 128)
        return jnp.where(odd, high, low), jnp.where(odd, low, high)

    def set_fields(self):
        def body(i):
            at = i * CH
            red, black = self.packed(self.full[pl.ds(2 * at, 2 * CH)], at)
            self.red[pl.ds(8 + at, CH)] = red
            self.black[pl.ds(8 + at, CH)] = black

        each(self.rows // CH, body)

    def set_weights(self):
        def body(i):
            at = i * CH
            lane, row = iota((CH, 128), 1), iota((CH, 128), 0)
            odd = (lane // 32 + lane) % 2 == 1
            s = row % 8
            pair = ((at + row) // 8) % 16
            z = lane % 32
            inside_y = (jnp.logical_not((s == 7) & (lane >= 96)), jnp.logical_not((s == 0) & (lane < 32)))
            inside_z = (z < 31, z > 0)
            for colour in (0, 1):
                first, last = (odd, jnp.logical_not(odd)) if colour else (jnp.logical_not(odd), odd)
                edge = (first & (pair == 0)) | (last & (pair == 15))
                masks = (None, jnp.logical_not(edge)) + inside_y + inside_z
                own = self.field(colour)[pl.ds(8 + at, CH)]
                near = self.near(colour, at)
                faces = [
                    0.5 * (own + (other if mask is None else jnp.where(mask, other, 0.0)))
                    for other, mask in zip(near, masks)
                ]
                total = faces[0] + faces[1] + faces[2] + faces[3] + faces[4] + faces[5]
                inv = 1.0 / total
                for n in range(6):
                    part = faces[n] * inv
                    self.coef[colour, n, pl.ds(at, CH)] = (
                        part if masks[n] is None else jnp.where(masks[n], part, 0.0)
                    )
                self.inv[colour, pl.ds(at, CH)] = inv * (1.0 / self.scale)
                self.hb[colour, pl.ds(at, CH)] = 0.5 * own * inv
                if colour == 0:
                    self.tot[pl.ds(at, CH)] = self.scale * total

        each(self.rows // CH, body)

    def set_target(self, at, red, black):
        for colour, value in ((0, red), (1, black)):
            self.g[colour, pl.ds(at, CH)] = value * self.inv[colour, pl.ds(at, CH)]

    def fresh(self, colour, at):
        near = self.near(colour, at)
        out = self.g[colour, pl.ds(at, CH)]
        for n in range(6):
            out = out + self.coef[colour, n, pl.ds(at, CH)] * near[n]
        return out

    def half_sweep(self, colour):
        def body(i):
            at = i * CH
            self.field(colour)[pl.ds(8 + at, CH)] = self.fresh(colour, at)

        each(self.rows // CH, body)

    def down(self):
        def first(i):
            at = i * CH
            self.red[pl.ds(8 + at, CH)] = self.g[0, pl.ds(at, CH)]

        each(self.rows // CH, first)
        self.half_sweep(1)
        self.half_sweep(0)
        self.half_sweep(1)

        def left(i):
            at = i * CH
            self.rest[pl.ds(at, CH)] = self.tot[pl.ds(at, CH)] * (
                self.fresh(0, at) - self.red[pl.ds(8 + at, CH)]
            )

        each(self.rows // CH, left)

    def restricted(self, mean):
        parts = []
        for box in range(self.count):
            for h in range(2):
                parts.append(
                    jnp.concatenate(
                        [self.rest[pl.ds(box * 128 + 4 * h + j, 16, stride=8)] for j in range(4)], axis=1
                    )
                )
        return chosen_dot(jnp.concatenate(parts, axis=0), mean)

    def start_up(self, pieces, spread):
        sub, lane = iota((8, 128), 0), iota((8, 128), 1)
        odd = (lane // 32 + lane) % 2 == 1
        even = jnp.logical_not(odd)
        rows_of = lane // 32 == sub % 4
        rows_of_face = (
            ((lane < 16) & (sub == 0))
            | ((lane >= 16) & (lane < 32) & (sub == 7))
            | ((lane >= 32) & (lane < 64) & ((lane % 16) // 2 == sub))
        )

        def tiles(rows):
            return jnp.broadcast_to(rows[:, None, :], (rows.shape[0], 8, 128))

        def halves(first, second):
            return jnp.where((sub < 4)[None], tiles(first), tiles(second))

        for box, piece in enumerate(pieces):
            core = jnp.concatenate(
                [
                    halves(piece[0:16], piece[16:32]),
                    halves(piece[48:49], piece[49:50]),
                    halves(piece[50:51], piece[51:52]),
                ],
                axis=0,
            )
            core = jnp.where(rows_of[None], core, 0.0).reshape(144, 128)
            face = jnp.where(rows_of_face[None], tiles(piece[32:48]), 0.0).reshape(128, 128)
            face = jnp.concatenate([face, jnp.zeros((16, 128), F32)], axis=0)
            grown = chosen_dot(jnp.concatenate([core, face], axis=1), spread)
            inner, border = grown[:128, :128], grown[:128, 128:].reshape(16, 8, 128)
            low, high = grown[128:136, :128], grown[136:144, :128]
            at = box * 128
            self.black[pl.ds(8 + at, 128)] = self.black[pl.ds(8 + at, 128)] + inner
            for colour in (0, 1):
                first, last = (odd, even) if colour else (even, odd)
                ghost = jnp.concatenate(
                    [
                        border[:1] + jnp.where(first, low, 0.0)[None],
                        border[1:15],
                        border[15:] + jnp.where(last, high, 0.0)[None],
                    ],
                    axis=0,
                ).reshape(128, 128)
                self.g[colour, pl.ds(at, 128)] = (
                    self.g[colour, pl.ds(at, 128)] + self.hb[colour, pl.ds(at, 128)] * ghost
                )

    def up(self):
        for colour in (0, 1, 0, 1):
            self.half_sweep(colour)

    def finished(self, at):
        lane = iota((CH, 128), 1)
        odd = (lane // 32 + lane) % 2 == 1
        red, black = self.red[pl.ds(8 + at, CH)], self.black[pl.ds(8 + at, CH)]
        low = jnp.where(odd, black, red).reshape(CH // 8, 1, 8, 128)
        high = jnp.where(odd, red, black).reshape(CH // 8, 1, 8, 128)
        return jnp.concatenate([low, high], axis=1).reshape(2 * CH, 128)


def spread_choice():
    l, n = iota((256, 256), 0), iota((256, 256), 1)
    z, q = n % 32, (n % 128) // 32
    inner = (l < 128) & (n < 128) & ((l // 16) % 2 == q // 2) & (l % 16 == z // 2)
    f = l - 128
    along_y = (f >= 0) & (f < 32) & (q == jnp.where(f < 16, 0, 3)) & (z // 2 == f % 16)
    along_z = (f >= 32) & (f < 64) & (q // 2 == f % 2) & (z == jnp.where(f < 48, 0, 31))
    return onehot(inner | ((n >= 128) & (along_y | along_z)))


def mean_choice():
    k, n = iota((512, 128), 0), iota((512, 128), 1)
    lane = k % 128
    return onehot(n == 32 * (k // 128) + 16 * (lane // 64) + (lane % 32) // 2, 0.125)


def place_choice(corner):
    k, n = iota((256, 1024), 0), iota((256, 1024), 1)
    return onehot(n == (k // 16) * 32 + k % 16 + corner[1] * 32 + corner[2])


def window_choice(corner):
    n = iota((1, 384), 1)
    i = n % 16
    source = jnp.where(n < 256, (n // 16) * 32 + i, -4096)
    source = jnp.where((n >= 256) & (n < 272), i - 32, source)
    source = jnp.where((n >= 272) & (n < 288), i + 512, source)
    source = jnp.where((n >= 288) & (n < 304), i * 32 - 1, source)
    source = jnp.where((n >= 304) & (n < 320), i * 32 + 16, source)
    return onehot(iota((1024, 384), 0) == source + corner[1] * 32 + corner[2])


def placed_lhs(piece):
    return jnp.concatenate([piece[0:16], piece[16:32]], axis=1)


def kernel(
    far_rhs_c, far_beta_c, far_rhs_m, far_beta_m, far_rhs_f, far_beta_f,
    far_parent_m, far_offset_m, far_parent_f, far_offset_f,
    out_c, out_m, out_f,
    rhs_c, beta_c, rhs_m, beta_m, rhs_f, beta_f, parent_m, offset_m, parent_f, offset_f,
    gather1, gather2, gather3, gather4, relay_out1, relay_in1, relay_out2, relay_in2, relay_out3, relay_in3, relay_out4, relay_in4,
    rim_out, rim_in,
    mean_ref, spread_ref, place_m, place_c, window_m, window_c,
    put_m, put_c, pad_m, pad_c, wide_m, wide_c, cut_m, cut_c,
    beta_e, g_e, field_e, coef_e, inv_e,
    *rest,
):
    fine_refs, mid_refs = rest[:9], rest[9:18]
    send_sems, recv_sems, relay_send, relay_recv, rim_send, rim_recv, load_sems = rest[18:]
    fine = Level(2, 1.0, fine_refs)
    mid = Level(1, 0.25, mid_refs)
    n_x, n_y = lax.axis_size("xb"), lax.axis_size("yb")
    row, col = lax.axis_index("xb"), lax.axis_index("yb")

    def load(n, source, target):
        copy = pltpu.make_async_copy(source, target, load_sems.at[n])
        copy.start()
        return copy

    load_beta_f = load(0, far_beta_f.at[0, 0], beta_f)
    load_rhs_f = load(1, far_rhs_f.at[0, 0], rhs_f)
    load_beta_c = load(3, far_beta_c, beta_c)
    load_beta_m = load(2, far_beta_m.at[0, 0], beta_m)
    load_rhs_m = load(4, far_rhs_m.at[0, 0], rhs_m)
    load_rhs_c = load(5, far_rhs_c, rhs_c)
    load_tables = (
        load(6, far_parent_m, parent_m),
        load(7, far_offset_m, offset_m),
        load(8, far_parent_f.at[col], parent_f),
        load(9, far_offset_f.at[col], offset_f),
    )

    def beside(dx, dy):
        return (lax.rem(row + dx + n_x, n_x), lax.rem(col + dy + n_y, n_y))

    def peer(dx, dh, dc):
        x, h, c = row // 4, (row // 2) % 2, row % 2
        return (((x + dx) % 4) * 4 + ((h + dh) % 2) * 2 + (c + dc) % 2, col)

    barrier = pltpu.get_barrier_semaphore()
    greeted = [peer(*hop) for hop in SAME_CORE] + [peer(0, 0, 1), beside(-1, 0), beside(1, 0)]
    greeted += [beside(dx, dy) for dx in (-1, 0, 1) for dy in (-1, 1)]
    for device in greeted:
        pl.semaphore_signal(barrier, inc=1, device_id=device, device_id_type=MESH)

    twin = row + 1 - 2 * (row % 2)
    chip = row // 2

    def send_all(buffer, stage, place, hops):
        for hop in hops:
            pltpu.make_async_remote_copy(
                src_ref=buffer.at[place],
                dst_ref=buffer.at[place],
                send_sem=send_sems.at[stage],
                recv_sem=recv_sems.at[stage],
                device_id=peer(*hop),
                device_id_type=MESH,
            ).start()

    def wait_all(buffer, sem, hops):
        whole = buffer.at[pl.ds(0, len(hops))]
        pltpu.make_async_copy(whole, whole, sem).wait()

    def wait_one(buffer, sem):
        pltpu.make_async_copy(buffer, buffer, sem).wait()

    def relay(n, source, target):
        pltpu.make_async_remote_copy(
            src_ref=source,
            dst_ref=target,
            send_sem=relay_send.at[n],
            recv_sem=relay_recv.at[n],
            device_id=(twin, col),
            device_id_type=MESH,
        ).start()

    def own_core(device):
        return lax.rem(device, 2) == row % 2

    def chip_of(device):
        return lax.div(device, 2)

    def send_rim(turn):
        def copy(kind, source, size, target, device):
            pltpu.make_async_remote_copy(
                src_ref=rim_out.at[turn, pl.ds(source, size)],
                dst_ref=rim_in.at[turn, pl.ds(target, size)],
                send_sem=rim_send.at[turn],
                recv_sem=rim_recv.at[3 * turn + kind],
                device_id=device,
                device_id_type=MESH,
            ).start()

        for side_x in (0, 1):
            for side_y in (0, 1):
                copy(
                    2, 256 + 128 * side_y + 112 * side_x, 16,
                    512 + 16 * (2 * (1 - side_x) + 1 - side_y),
                    beside(2 * side_x - 1, 2 * side_y - 1),
                )
        for side in (0, 1):
            copy(1, 256 + 128 * side, 128, 256 + 128 * (1 - side), beside(0, 2 * side - 1))
        for side in (0, 1):
            copy(0, 128 * side, 128, 128 * (1 - side), beside(2 * side - 1, 0))

    def wait_rim(turn, kind):
        wait_one(rim_in.at[turn, pl.ds(256 * kind, (256, 256, 64)[kind])], rim_recv.at[3 * turn + kind])

    def fill_rim(turn, ref):
        tile_row = iota((8, 128), 0)
        for side in (0, 1):
            for colour in (0, 1):
                for d in (0, 1):
                    at = EDGE + ((2, 16)[side] + d) * ROWS + 8
                    rim_out[turn, pl.ds(128 * side + (2 * colour + d) * 32, 32)] = ref[colour, pl.ds(at, 32)]

        def body(k):
            at = EDGE + (k + 2) * ROWS
            red, black = ref[0, pl.ds(at + 8, 8)], ref[1, pl.ds(at + 8, 8)]
            rim_out[turn, pl.ds(256 + k * 8, 8)] = jnp.where(tile_row < 4, red, pltpu.roll(black, 4, 0))
            red, black = ref[0, pl.ds(at + 32, 8)], ref[1, pl.ds(at + 32, 8)]
            rim_out[turn, pl.ds(384 + k * 8, 8)] = jnp.where(tile_row < 4, pltpu.roll(black, 4, 0), red)

        each(16, body)

    def keep(value, *sides):
        for side in sides:
            if side is not None:
                value = jnp.where(side, value, 0.0)
        return value

    def take_y(turn, ref, inside_y):
        def body(k):
            for side in (0, 1):
                at = EDGE + (k + 2) * ROWS + 40 * side
                part = keep(rim_in[turn, pl.ds(256 + 128 * side + 8 * k, 8)], inside_y[side])
                ref[0, pl.ds(at, 8)] = part
                ref[1, pl.ds(at, 8)] = pltpu.roll(part, 4, 0)

        each(16, body)

    def take_x(turn, ref, inside_x, inside_y):
        for side in (0, 1):
            for colour in (0, 1):
                for d in (0, 1):
                    at = EDGE + ((0, 18)[side] + d) * ROWS + 8
                    part = rim_in[turn, pl.ds(128 * side + (2 * colour + d) * 32, 32)]
                    ref[colour, pl.ds(at, 32)] = keep(part, inside_x[side])
            for other in (0, 1):
                for d in (0, 1):
                    at = EDGE + (18 * side + d) * ROWS + 40 * other
                    part = rim_in[turn, pl.ds(512 + 16 * (2 * side + other) + 8 * d, 8)]
                    part = keep(part, inside_x[side], inside_y[other])
                    ref[0, pl.ds(at, 8)] = part
                    ref[1, pl.ds(at, 8)] = pltpu.roll(part, 4, 0)

    mean_ref[...] = mean_choice()
    fine.clear_ends()

    load_beta_f.wait()
    fine.unfold(lambda box, s: beta_f[box, :, 128 * s : 128 * s + 128])
    fine.set_fields()
    fine.set_weights()
    load_rhs_f.wait()
    fine.unfold(lambda box, s: rhs_f[box, :, 128 * s : 128 * s + 128])

    def fine_target(i):
        at = i * CH
        fine.set_target(at, *fine.packed(fine.full[pl.ds(2 * at, 2 * CH)], at))

    each(fine.rows // CH, fine_target)
    pl.semaphore_wait(barrier, len(greeted))
    fine.down()
    gather1[chip] = fine.restricted(mean_ref[...]).reshape(2, 32, 128)
    send_all(gather1, 0, chip, SAME_CORE)

    def own_beta(k):
        lane, line = iota((32, 128), 1), iota((32, 128), 0)
        odd = (line + lane) % 2 == 1
        low, high = beta_c[2 * k], beta_c[2 * k + 1]
        at = EDGE + (k + 2) * ROWS + 8
        beta_e[0, pl.ds(at, 32)] = jnp.where(odd, high, low)
        beta_e[1, pl.ds(at, 32)] = jnp.where(odd, low, high)

    for colour in (0, 1):
        beta_e[colour, pl.ds(0, EDGE)] = jnp.zeros((EDGE, 128), F32)
        beta_e[colour, pl.ds(WIDE - EDGE, EDGE)] = jnp.zeros((EDGE, 128), F32)
    load_beta_c.wait()
    each(16, own_beta)
    fill_rim(0, beta_e)
    send_rim(0)
    mid.clear_ends()
    load_beta_m.wait()
    mid.unfold(lambda box, s: beta_m[:, 128 * s : 128 * s + 128])
    mid.set_fields()
    mid.set_weights()
    load_rhs_m.wait()
    mid.unfold(lambda box, s: rhs_m[:, 128 * s : 128 * s + 128])

    for copy in load_tables:
        copy.wait()

    def find_fine(i, carry):
        index, place, x, y, z, twin_index, twin_place = carry
        for slot in range(2):
            twin_hit = parent_f[slot, i] == twin
            twin_index = jnp.where(twin_hit, i, twin_index)
            twin_place = jnp.where(twin_hit, slot, twin_place)
            hit = parent_f[slot, i] == row
            index = jnp.where(hit, i, index)
            place = jnp.where(hit, slot, place)
            x = jnp.where(hit, offset_f[0, slot, i], x)
            y = jnp.where(hit, offset_f[1, slot, i], y)
            z = jnp.where(hit, offset_f[2, slot, i], z)
        return index, place, x, y, z, twin_index, twin_place

    def find_mid(i, carry):
        index, x, y, z, twin_index = carry
        hit = parent_m[col, i] == row
        return (
            jnp.where(hit, i, index),
            jnp.where(hit, offset_m[0, col, i], x),
            jnp.where(hit, offset_m[1, col, i], y),
            jnp.where(hit, offset_m[2, col, i], z),
            jnp.where(parent_m[col, i] == twin, i, twin_index),
        )

    zero, one = jnp.int32(0), jnp.int32(1)
    child, child_slot, *corner_m, twin_child, twin_slot = lax.fori_loop(
        0, 16, find_fine, (zero, zero, one, one, one, zero, zero)
    )
    guest, *corner_c, twin_guest = lax.fori_loop(0, 16, find_mid, (zero, one, one, one, zero))
    place_m[...] = place_choice(corner_m)
    pad_m[0:16] = jnp.zeros((16, 8, 128), F32)
    pad_m[32:48] = jnp.zeros((16, 8, 128), F32)

    wait_all(gather1, recv_sems.at[0], SAME_CORE)
    relay_out1[...] = gather1[chip_of(twin_child), twin_slot]
    relay(0, relay_out1, relay_in1)
    wait_one(relay_in1, relay_recv.at[0])

    piece = jnp.where(own_core(child), gather1[chip_of(child), child_slot], relay_in1[...])
    put = chosen_dot(placed_lhs(piece), place_m[...])
    for s in range(8):
        put_m[pl.ds(s, 16, stride=8)] = put[:, 128 * s : 128 * s + 128]
    pad_m[16:32] = put_m[...].reshape(16, 8, 128)

    def shift_m(x):
        cut_m[pl.ds(8 * x, 8)] = pad_m[16 - corner_m[0] + x]

    each(32, shift_m)

    def mid_target(i):
        lane, line = iota((2 * CH, 128), 1), iota((2 * CH, 128), 0)
        x = i * (CH // 4) + line // 8 - corner_m[0]
        y = (line % 8) * 4 + lane // 32 - corner_m[1]
        z = lane % 32 - corner_m[2]
        hit = (x >= 0) & (x < 16) & (y >= 0) & (y < 16) & (z >= 0) & (z < 16)
        full = jnp.where(hit, cut_m[pl.ds(2 * CH * i, 2 * CH)], mid.full[pl.ds(2 * CH * i, 2 * CH)])
        mid.set_target(i * CH, *mid.packed(full, i * CH))

    each(mid.rows // CH, mid_target)
    mid.down()
    gather2[chip] = mid.restricted(mean_ref[...])
    send_all(gather2, 1, chip, SAME_CORE)

    place_c[...] = place_choice(corner_c)
    pad_c[0:16] = jnp.zeros((16, 32, 128), F32)
    pad_c[32:48] = jnp.zeros((16, 32, 128), F32)
    for kind in (0, 1, 2):
        wait_rim(0, kind)
    inside_x, inside_y = (row > 0, row < n_x - 1), (col > 0, col < n_y - 1)
    take_y(0, beta_e, inside_y)
    take_x(0, beta_e, inside_x, inside_y)

    def near_wide(ref, colour, at, rows):
        lane, line = iota((rows, 128), 1), iota((rows, 128), 0)
        odd = (line + lane) % 2 == 1
        own = ref[1 - colour, pl.ds(at, rows)]
        above, below = ref[1 - colour, pl.ds(at + ROWS, rows)], ref[1 - colour, pl.ds(at - ROWS, rows)]
        other = jnp.where(odd, below, above) if colour else jnp.where(odd, above, below)
        after, before = ref[1 - colour, pl.ds(at + 1, rows)], ref[1 - colour, pl.ds(at - 1, rows)]
        return own, other, after, before, pltpu.roll(own, 127, 1), pltpu.roll(own, 1, 1)

    def coarse_weights(k):
        lane = iota((ROWS, 128), 1)
        masks = (None, None, None, None, lane < 127, lane > 0)
        at = EDGE + k * ROWS
        for colour in (0, 1):
            own = beta_e[colour, pl.ds(at, ROWS)]
            near = near_wide(beta_e, colour, at, ROWS)
            faces = [
                0.5 * (own + (other if mask is None else jnp.where(mask, other, 0.0)))
                for other, mask in zip(near, masks)
            ]
            total = faces[0] + faces[1] + faces[2] + faces[3] + faces[4] + faces[5]
            real = own > 0.0
            inv = jnp.where(real, 1.0 / total, 0.0)
            for n in range(6):
                keep = real if masks[n] is None else real & masks[n]
                coef_e[colour, n, pl.ds(k * ROWS, ROWS)] = jnp.where(keep, faces[n] * inv, 0.0)
            inv_e[colour, pl.ds(k * ROWS, ROWS)] = 16.0 * inv

    each(PAIRS, coarse_weights, 4)
    window_c[...] = window_choice(corner_c)
    wait_all(gather2, recv_sems.at[1], SAME_CORE)
    relay_out2[...] = gather2[chip_of(twin_guest)]
    relay(3, relay_out2, relay_in2)
    wait_one(relay_in2, relay_recv.at[3])

    piece = jnp.where(own_core(guest), gather2[chip_of(guest)], relay_in2[...])
    put = chosen_dot(placed_lhs(piece), place_c[...])
    for s in range(8):
        part = put[:, 128 * s : 128 * s + 128]
        for q in range(4):
            put_c[pl.ds(4 * s + q, 16, stride=32)] = part if q == 0 else pltpu.roll(part, 128 - 32 * q, 1)

    pad_c[16:32] = put_c[...].reshape(16, 32, 128)

    load_rhs_c.wait()

    def coarse_target(k):
        lane, line = iota((32, 128), 1), iota((32, 128), 0)
        odd = (line + lane) % 2 == 1
        y, z = line - corner_c[1], lane - corner_c[2]
        hit = (y >= 0) & (y < 16) & (z >= 0) & (z < 16)
        planes = []
        for d in (0, 1):
            x = 2 * k + d - corner_c[0]
            planes.append(jnp.where(hit & (x >= 0) & (x < 16), pad_c[16 + x], rhs_c[2 * k + d]))
        at = EDGE + (k + 2) * ROWS + 8
        g_e[0, pl.ds(at, 32)] = jnp.where(odd, planes[1], planes[0])
        g_e[1, pl.ds(at, 32)] = jnp.where(odd, planes[0], planes[1])

    each(16, coarse_target)
    fill_rim(1, g_e)
    send_rim(1)

    def coarse_first(first, count, line, rows):
        def body(i):
            at, here = EDGE + (first + i) * ROWS + line, (first + i) * ROWS + line
            field_e[0, pl.ds(at, rows)] = g_e[0, pl.ds(at, rows)] * inv_e[0, pl.ds(here, rows)]

        each(count, body)

    def coarse_sweep(colour, first, count, line=0, rows=ROWS):
        def body(i):
            k = first + i
            at, here = EDGE + k * ROWS + line, k * ROWS + line
            near = near_wide(field_e, colour, at, rows)
            out = g_e[colour, pl.ds(at, rows)] * inv_e[colour, pl.ds(here, rows)]
            for n in range(6):
                out = out + coef_e[colour, n, pl.ds(here, rows)] * near[n]
            field_e[colour, pl.ds(at, rows)] = out

        each(count, body)

    coarse_first(2, 16, 8, 32)
    wait_rim(1, 1)
    take_y(1, g_e, (None, None))
    coarse_first(2, 16, 0, 8)
    coarse_first(2, 16, 40, 8)
    coarse_sweep(1, 3, 14)
    coarse_sweep(0, 4, 12)
    coarse_sweep(1, 5, 10, 8, 32)
    wait_rim(1, 0)
    wait_rim(1, 2)
    take_x(1, g_e, (None, None), (None, None))
    for first in (0, 18):
        coarse_first(first, 2, 0, ROWS)
    for first in (1, 17):
        coarse_sweep(1, first, 2)
    for first in (1, 16):
        coarse_sweep(0, first, 3)
    for first in (2, 15):
        coarse_sweep(1, first, 3, 8, 32)

    def coarse_out(k):
        lane, line = iota((32, 128), 1), iota((32, 128), 0)
        odd = (line + lane) % 2 == 1
        at = EDGE + (k + 2) * ROWS + 8
        red, black = field_e[0, pl.ds(at, 32)], field_e[1, pl.ds(at, 32)]
        low, high = jnp.where(odd, black, red), jnp.where(odd, red, black)
        wide_c[1 + 2 * k] = low
        wide_c[2 + 2 * k] = high

    each(16, coarse_out)

    def post_window(buffer, stage, lhs, choice):
        got = chosen_dot(lhs, choice)
        for n in range(3):
            buffer[chip, pl.ds(16 * n, 16)] = got[1:17, 128 * n : 128 * n + 128]
        for n, (x, h) in enumerate(((0, 0), (0, 1), (17, 0), (17, 1))):
            buffer[chip, pl.ds(48 + n, 1)] = got[x : x + 1, 128 * h : 128 * h + 128]
        send_all(buffer, stage, chip, SAME_CORE)

    def cut_window_c(x):
        cut_c[pl.ds(32 * x, 32)] = wide_c[corner_c[0] + x]

    each(18, cut_window_c)
    lane24 = iota((24, 128), 1)
    blocks = []
    for s in range(8):
        block = None
        for q in range(4):
            part = cut_c[pl.ds(4 * s + q, 24, stride=32)]
            if q == 0:
                block = part
            else:
                block = jnp.where(lane24 // 32 == q, pltpu.roll(part, 32 * q, 1), block)
        blocks.append(block)
    post_window(gather3, 2, jnp.concatenate(blocks, axis=1), window_c[...])
    out_c[...] = wide_c[1:33]
    spread_ref[...] = spread_choice()
    window_m[...] = window_choice(corner_m)
    wait_all(gather3, recv_sems.at[2], SAME_CORE)
    relay_out3[...] = gather3[chip_of(parent_m[col, twin])]
    relay(1, relay_out3, relay_in3)
    wait_one(relay_in3, relay_recv.at[1])

    owner_m = parent_m[col, row]
    piece = jnp.where(own_core(owner_m), gather3[chip_of(owner_m)], relay_in3[...])
    mid.start_up([piece], spread_ref[...])
    mid.up()

    def mid_out(i):
        full = mid.finished(CH * i)
        mid.full[pl.ds(2 * CH * i, 2 * CH)] = full
        wide_m[pl.ds(1 + CH // 4 * i, CH // 4)] = full.reshape(CH // 4, 8, 128)

    each(mid.rows // CH, mid_out)

    def cut_window_m(x):
        cut_m[pl.ds(8 * x, 8)] = wide_m[corner_m[0] + x]

    each(18, cut_window_m)
    lhs = jnp.concatenate([cut_m[pl.ds(s, 24, stride=8)] for s in range(8)], axis=1)
    post_window(gather4, 3, lhs, window_m[...])
    for s in range(8):
        out_m[0, 0, :, 128 * s : 128 * s + 128] = mid.full[pl.ds(s, 32, stride=8)]
    wait_all(gather4, recv_sems.at[3], SAME_CORE)
    for slot in range(2):
        relay_out4[slot] = gather4[chip_of(jnp.maximum(parent_f[slot, twin], 0))]
    relay(2, relay_out4, relay_in4)
    wait_one(relay_in4, relay_recv.at[2])

    owners = [parent_f[slot, row] for slot in range(2)]
    pieces = []
    for slot, owner in enumerate(owners):
        owner = jnp.maximum(owner, 0)
        pieces.append(jnp.where(own_core(owner), gather4[chip_of(owner)], relay_in4[slot]))
    fine.start_up(pieces, spread_ref[...])
    fine.up()

    def fine_out(i):
        fine.full[pl.ds(2 * CH * i, 2 * CH)] = fine.finished(CH * i)

    each(fine.rows // CH, fine_out)
    for box in range(2):
        for s in range(8):
            part = fine.full[pl.ds(box * 256 + s, 32, stride=8)]
            out_f[0, 0, box, :, 128 * s : 128 * s + 128] = jnp.where(owners[box] >= 0, part, 0.0)

    wait_all(gather1, send_sems.at[0], SAME_CORE)
    wait_all(gather2, send_sems.at[1], SAME_CORE)
    wait_all(gather3, send_sems.at[2], SAME_CORE)
    wait_all(gather4, send_sems.at[3], SAME_CORE)
    for n, buffer in enumerate((relay_out1, relay_out3, relay_out4, relay_out2)):
        wait_one(buffer, relay_send.at[n])
    for turn in (0, 1):
        wait_one(rim_in.at[turn], rim_send.at[turn])


def level_scratch(count):
    rows = count * 128
    return [
        pltpu.VMEM((2 * rows, 128), F32),
        pltpu.VMEM((rows + 16, 128), F32),
        pltpu.VMEM((rows + 16, 128), F32),
        pltpu.VMEM((2, 6, rows, 128), F32),
        pltpu.VMEM((2, rows, 128), F32),
        pltpu.VMEM((2, rows, 128), F32),
        pltpu.VMEM((2, rows, 128), F32),
        pltpu.VMEM((rows, 128), F32),
        pltpu.VMEM((rows, 128), F32),
    ]


def write_out(*refs):
    sources, targets, sem = refs[:3], refs[3:6], refs[6]
    copies = [pltpu.make_async_copy(x, y, sem.at[n]) for n, (x, y) in enumerate(zip(sources, targets))]
    for copy in copies:
        copy.start()
    for copy in copies:
        copy.wait()


def on_device(*args):
    fields, (parent_m, offset_m, parent_f, offset_f) = args[:6], args[6:]
    tables = (
        jnp.transpose(parent_m),
        jnp.transpose(offset_m, (2, 1, 0)),
        jnp.transpose(parent_f, (1, 2, 0)),
        jnp.transpose(offset_f, (1, 3, 2, 0)),
    )
    shapes = [args[0].shape, args[2].shape, args[4].shape]
    out_shape = [jax.ShapeDtypeStruct(shape, F32) for shape in shapes]
    anywhere = pl.BlockSpec(memory_space=pl.ANY)
    call = pl.pallas_call(
        kernel,
        out_shape=out_shape,
        in_specs=[pl.BlockSpec(memory_space=pltpu.HBM)] * 10,
        out_specs=[pl.BlockSpec(memory_space=pltpu.VMEM)] * 3,
        scratch_shapes=[
            *[pltpu.VMEM(shape, F32) for shape in ((32, 32, 128),) * 2 + ((32, 1024),) * 2 + ((2, 32, 1024),) * 2],
            *[pltpu.SMEM(shape, jnp.int32) for shape in (tables[0].shape, tables[1].shape, (2, 16), (3, 2, 16))],
            pltpu.VMEM((8, 2, 32, 128), F32),
            pltpu.VMEM((8, 32, 128), F32),
            pltpu.VMEM((8, 56, 128), F32),
            pltpu.VMEM((8, 56, 128), F32),
            pltpu.VMEM((32, 128), F32),
            pltpu.VMEM((32, 128), F32),
            pltpu.VMEM((32, 128), F32),
            pltpu.VMEM((32, 128), F32),
            pltpu.VMEM((56, 128), F32),
            pltpu.VMEM((56, 128), F32),
            pltpu.VMEM((2, 56, 128), F32),
            pltpu.VMEM((2, 56, 128), F32),
            pltpu.VMEM((2, 512, 128), F32),
            pltpu.VMEM((2, 576, 128), F32),
            pltpu.VMEM((512, 128), BF16),
            pltpu.VMEM((256, 256), BF16),
            pltpu.VMEM((256, 1024), BF16),
            pltpu.VMEM((256, 1024), BF16),
            pltpu.VMEM((1024, 384), BF16),
            pltpu.VMEM((1024, 384), BF16),
            pltpu.VMEM((128, 128), F32),
            pltpu.VMEM((512, 128), F32),
            pltpu.VMEM((48, 8, 128), F32),
            pltpu.VMEM((48, 32, 128), F32),
            pltpu.VMEM((33, 8, 128), F32),
            pltpu.VMEM((33, 32, 128), F32),
            pltpu.VMEM((256, 128), F32),
            pltpu.VMEM((24 * 32, 128), F32),
            pltpu.VMEM((2, WIDE, 128), F32),
            pltpu.VMEM((2, WIDE, 128), F32),
            pltpu.VMEM((2, WIDE, 128), F32),
            pltpu.VMEM((2, 6, PAIRS * ROWS, 128), F32),
            pltpu.VMEM((2, PAIRS * ROWS, 128), F32),
            *level_scratch(2),
            *level_scratch(1),
            pltpu.SemaphoreType.DMA((4,)),
            pltpu.SemaphoreType.DMA((4,)),
            pltpu.SemaphoreType.DMA((4,)),
            pltpu.SemaphoreType.DMA((4,)),
            pltpu.SemaphoreType.DMA((2,)),
            pltpu.SemaphoreType.DMA((6,)),
            pltpu.SemaphoreType.DMA((10,)),
        ],
        compiler_params=pltpu.CompilerParams(
            collective_id=0, has_side_effects=True, vmem_limit_bytes=40 * 2**20
        ),
        name="v_cycle",
    )
    write = pl.pallas_call(
        write_out,
        out_shape=out_shape,
        in_specs=[pl.BlockSpec(memory_space=pltpu.VMEM)] * 3,
        out_specs=[anywhere] * 3,
        scratch_shapes=[pltpu.SemaphoreType.DMA((3,))],
        compiler_params=pltpu.CompilerParams(vmem_limit_bytes=8 * 2**20),
        name="write_out",
    )
    pinned = [pltpu.with_memory_space_constraint(arg, pltpu.HBM) for arg in fields + tables]
    return tuple(write(*call(*pinned)))


def solution(mesh):
    return jax.shard_map(
        on_device,
        mesh=mesh,
        in_specs=(
            P("xb", "yb", None),
            P("xb", "yb", None),
            P("xb", "yb", None, None),
            P("xb", "yb", None, None),
            P("xb", "yb", None, None, None),
            P("xb", "yb", None, None, None),
            P(),
            P(),
            P(),
            P(),
        ),
        out_specs=(P("xb", "yb", None), P("xb", "yb", None, None), P("xb", "yb", None, None, None)),
        check_vma=False,
    )
```
